32 devices in a mesh: row: 8 (over z, x), col: 4 (over y, core).
Axes of the slice: x: 2, y: 2, z: 4, core: 2. Of those that a mesh axis runs over, the one named last changes fastest.
Arguments:
- three_centre: bfloat16 [8, 4, 640, 4096], P('row', 'col'), may hold values from -0.3984375 to 0.3984375
- green_occ: bfloat16 [8, 2, 64, 64], P('row'), may hold values from -0.75 to 0.75
- green_vir: bfloat16 [4, 2, 64, 64], P('col'), may hold values from -0.75 to 0.75
- pair_live: int32 [8, 4], P('row', 'col'), may hold values 0 or 1
Outputs:
- chi_diag: float32 [8, 640, 640], P('row', 'col')
- chi_next: float32 [8, 640, 640], P('row', 'col')
The draws below stay inside these ranges and needn't reach their ends.
All inputs are finite; a program needn't handle non-finite values. No bound on the sum of `pair_live` on one device may be relied on, other than what follows from the above.
Results may differ from the reference program's by a relative error of at most 0.013.
Values may be sent and summed in bfloat16 or wider, within the bound.
No kernel may reach another device: no remote copies, remote signals or barrier semaphores. Data moves between devices by JAX's collectives and lax.ppermute only.
A program may use at most 128 MiB of HBM per device.

```python
import jax
import jax.numpy as jnp
from jax import lax

TILE = 64
AUX = 640
NOCC = 8
NVIR = 4


def place_ends(drawn, stream_key, smallest, largest):
    index_at = [jax.random.randint(jax.random.fold_in(stream_key, axis), (), 0, length) for axis, length in enumerate(drawn.shape)]
    main_axis = drawn.shape.index(max(drawn.shape))
    neighbour = index_at[:main_axis] + [(index_at[main_axis] + 1) % drawn.shape[main_axis]] + index_at[main_axis + 1:]
    return drawn.at[tuple(index_at)].set(smallest).at[tuple(neighbour)].set(largest)


def shard_levels(stream_key, shape, pieces, smallest, high):
    loudness = 1.0
    for axis_at, shards_of in pieces:
        steps = jax.random.uniform(jax.random.fold_in(jax.random.fold_in(stream_key, 6), axis_at), (shards_of,), jnp.float32, smallest / len(pieces), high / len(pieces))
        loudness = loudness * jnp.repeat(jnp.exp(steps), shape[axis_at] // shards_of).reshape((-1,) + (1,) * (len(shape) - 1 - axis_at))
    return loudness


def gaussian(rng, extent, deviation, bound, pieces=(), kind=jnp.bfloat16):
    entries = deviation * jax.random.normal(rng, extent, jnp.float32)
    if pieces:
        entries = entries * shard_levels(rng, extent, pieces, -0.22, 0.18)
    return jnp.clip(entries, -bound, bound).astype(kind)


def setup_inputs(seed: int = 0) -> dict:
    seeds = jax.random.split(jax.random.key(seed), 5)
    return {
        "three_centre": gaussian(seeds[0], (NOCC, NVIR, AUX, TILE * TILE), 0.05, 0.3984375, ((0, 8), (1, 4))),
        "green_occ": gaussian(seeds[1], (NOCC, 2, TILE, TILE), TILE ** -0.5, 0.75, ((0, 8),)),
        "green_vir": gaussian(seeds[2], (NVIR, 2, TILE, TILE), TILE ** -0.5, 0.75, ((0, 4),)),
        "pair_live": place_ends((jax.random.randint(seeds[3], (NOCC, NVIR), 0, 4) < 3).astype(jnp.int32), jax.random.fold_in(seeds[3], 1), 0, 1),
    }


def reference(three_centre, green_occ, green_vir, pair_live):
    live = pair_live.astype(jnp.bfloat16)[:, :, None, None]
    blocks = (three_centre * live).reshape(NOCC, NVIR, AUX, TILE, TILE)
    gv_self = green_vir[:, 0].astype(jnp.float32)
    gv_left = green_vir[:, 1].astype(jnp.float32)

    def one_row(n):
        upper = jnp.minimum(n + 1, NOCC - 1).astype(jnp.int32)
        flag = (n < NOCC - 1).astype(jnp.float32)
        own = lax.dynamic_index_in_dim(blocks, n, 0, keepdims=False).astype(jnp.float32)
        above = lax.dynamic_index_in_dim(blocks, upper, 0, keepdims=False).astype(jnp.float32)
        go_self = lax.dynamic_index_in_dim(green_occ, n, 0, keepdims=False)[0].astype(jnp.float32)
        go_down = lax.dynamic_index_in_dim(green_occ, upper, 0, keepdims=False)[1].astype(jnp.float32)
        xa = jnp.einsum('cpml,mn->cpnl', own, go_self).astype(jnp.bfloat16)
        xb = (jnp.einsum('cpml,mn->cpnl', above, go_down) * flag).astype(jnp.bfloat16)
        za = jnp.einsum('cpns,cls->cpnl', own, gv_self).astype(jnp.bfloat16)
        zl = jnp.einsum('cpns,cls->cpnl', own, gv_left).astype(jnp.bfloat16)
        zb = jnp.concatenate([zl[1:], jnp.zeros_like(zl[:1])], axis=0)
        xa = xa.reshape(NVIR, AUX, TILE * TILE).astype(jnp.float32)
        xb = xb.reshape(NVIR, AUX, TILE * TILE).astype(jnp.float32)
        za = za.reshape(NVIR, AUX, TILE * TILE).astype(jnp.float32)
        zb = zb.reshape(NVIR, AUX, TILE * TILE).astype(jnp.float32)
        diag = jnp.einsum('cpk,cqk->pq', xa, za) + jnp.einsum('cpk,cqk->pq', xa, zb)
        nxt = jnp.einsum('cpk,cqk->pq', xb, za) + jnp.einsum('cpk,cqk->pq', xb, zb)
        return diag, nxt

    chi_diag, chi_next = lax.map(one_row, jnp.arange(NOCC, dtype=jnp.int32))
    return chi_diag, chi_next
```

```python
import jax
import jax.numpy as jnp
from jax import lax
from jax.experimental import pallas as pl
from jax.experimental.pallas import tpu as pltpu
from jax.sharding import PartitionSpec as P

BF = jnp.bfloat16
F32 = jnp.float32
VMEM_BYTES = 56 * 1024 * 1024
LAM_GROUP = 16
SPAN = 256


def dot(a, b, dims=((1,), (0,))):
    return lax.dot_general(a, b, (dims, ((), ())), preferred_element_type=F32)


def iota(shape, axis):
    return lax.broadcasted_iota(jnp.int32, shape, axis)


def spread_rows(g, group):
    m, k = g.shape
    rows, cols = (m * group, m), (k, k * group)
    pick_row = (iota(rows, 0) // group == iota(rows, 1)).astype(BF)
    pick_col = (iota(cols, 1) // group == iota(cols, 0)).astype(BF)
    tall = dot(pick_row, g).astype(BF)
    full = dot(tall, pick_col)
    same = iota(full.shape, 0) % group == iota(full.shape, 1) % group
    return jnp.where(same, full, 0.0).astype(BF)


def repeated(g, count):
    t = g.shape[0]
    n = t * count
    pick = (iota((n, t), 0) % t == iota((n, t), 1)).astype(BF)
    tall = dot(pick, g).astype(BF)
    full = dot(tall, pick, ((1,), (1,)))
    same = iota(full.shape, 0) // t == iota(full.shape, 1) // t
    return jnp.where(same, full, 0.0).astype(BF)


def fill_forms(f_ref, kron_ref):
    for i in range(f_ref.shape[0]):
        kron_ref[i] = repeated(f_ref[i], SPAN // f_ref.shape[1])


def params():
    return pltpu.CompilerParams(vmem_limit_bytes=VMEM_BYTES)


def cost(flops, size):
    return pl.CostEstimate(flops=flops, bytes_accessed=size, transcendentals=0)


def occ_step(right, kron_ref, out_refs):
    width = right.shape[1]
    at = 0
    for out in out_refs:
        rows = out.shape[0]
        done = 0
        while done < rows:
            take = min(rows - done, 32)
            part = kron_ref[at * LAM_GROUP : (at + take) * LAM_GROUP]
            out[done : done + take] = dot(part, right).astype(BF).reshape(take, LAM_GROUP, width)
            done += take
            at += take


def turn_occ_kernel(live_ref, g_ref, y_ref, yt_out, *rest, units):
    *outs, yt_ref, kron_ref = rest
    tile, _, width = yt_ref.shape
    per = tile // units
    step = pl.program_id(0)

    @pl.when(step == 0)
    def _():
        kron_ref[...] = spread_rows(g_ref[...], LAM_GROUP)

    @pl.when(step < units)
    def _():
        scale = live_ref[0].astype(F32)
        eye = jnp.where(iota((SPAN, SPAN), 0) == iota((SPAN, SPAN), 1), scale, 0.0).astype(BF)
        turned = dot(eye, y_ref[...], ((1,), (1,))).astype(BF)
        yt_ref[pl.ds(step * per, per)] = turned.reshape(per, tile, width)

    for s in range(tile // LAM_GROUP):

        @pl.when(step == units + s)
        def _(s=s):
            part = yt_ref[:, s * LAM_GROUP : (s + 1) * LAM_GROUP, :]
            yt_out[...] = part
            occ_step(part.reshape(tile * LAM_GROUP, width), kron_ref, outs)


def turn_occ(live, mats, y, tile, parts):
    m = mats.shape[0]
    aux, size = y.shape
    units = size // SPAN
    groups = tile // LAM_GROUP
    late = lambda i: (0, jnp.maximum(i - units, 0), 0)
    return pl.pallas_call(
        lambda *refs: turn_occ_kernel(*refs, units=units),
        grid=(units + groups,),
        in_specs=[
            pl.BlockSpec(memory_space=pltpu.SMEM),
            pl.BlockSpec((m, tile), lambda i: (0, 0)),
            pl.BlockSpec((aux, SPAN), lambda i: (0, jnp.minimum(i, units - 1))),
        ],
        out_specs=[pl.BlockSpec((n, LAM_GROUP, aux), late) for n in (tile, *parts)],
        out_shape=[jax.ShapeDtypeStruct((n, tile, aux), BF) for n in (tile, *parts)],
        scratch_shapes=[pltpu.VMEM((tile, tile, aux), BF), pltpu.VMEM((m * LAM_GROUP, tile * LAM_GROUP), BF)],
        compiler_params=params(),
        cost_estimate=cost(2 * aux * size * (SPAN + m * LAM_GROUP), 2 * aux * (2 * size + m * tile)),
        name="turn_and_occ",
    )(live, mats, y)


def occ_kernel(g_ref, yt_ref, *rest):
    *outs, kron_ref = rest

    @pl.when(pl.program_id(0) == 0)
    def _():
        kron_ref[...] = spread_rows(g_ref[...], LAM_GROUP)

    tile, group, width = yt_ref.shape
    occ_step(yt_ref[...].reshape(tile * group, width), kron_ref, outs)


def occ(mats, yt, parts):
    m = mats.shape[0]
    tile, _, aux = yt.shape
    block = lambda n: pl.BlockSpec((n, LAM_GROUP, aux), lambda i: (0, i, 0))
    return pl.pallas_call(
        occ_kernel,
        grid=(tile // LAM_GROUP,),
        in_specs=[pl.BlockSpec((m, tile), lambda i: (0, 0)), block(tile)],
        out_specs=[block(n) for n in parts],
        out_shape=[jax.ShapeDtypeStruct((n, tile, aux), BF) for n in parts],
        scratch_shapes=[pltpu.VMEM((m * LAM_GROUP, tile * LAM_GROUP), BF)],
        compiler_params=params(),
        cost_estimate=cost(2 * aux * tile * tile * m * LAM_GROUP, 2 * aux * tile * (tile + m)),
        name="occ",
    )(mats, yt)


def vir_kernel(f_ref, s_ref, shifted_ref, out_ref, kron_ref):
    @pl.when(pl.program_id(0) == 0)
    def _():
        fill_forms(f_ref, kron_ref)

    out_ref[...] = (dot(kron_ref[0], s_ref[...]) + dot(kron_ref[1], shifted_ref[...])).astype(BF)


def vir(forms, s, shifted):
    rows, width = s.shape
    block = pl.BlockSpec((SPAN, width), lambda i: (i, 0))
    return pl.pallas_call(
        vir_kernel,
        grid=(rows // SPAN,),
        in_specs=[pl.BlockSpec(forms.shape, lambda i: (0, 0, 0)), block, block],
        out_specs=block,
        out_shape=jax.ShapeDtypeStruct((rows, width), BF),
        scratch_shapes=[pltpu.VMEM((2, SPAN, SPAN), BF)],
        compiler_params=params(),
        cost_estimate=cost(4 * rows * width * SPAN, 6 * rows * width),
        name="vir",
    )(forms, s, shifted)


def within(first, count):
    return lambda i: jnp.clip(i - first, 0, count - 1)


def diag_kernel(live_ref, f_ref, y_ref, t_ref, below2_ref, below1_ref, shifted_ref, out_ref, kron_ref, acc_ref, *, n2, n1):
    step = pl.program_id(0)

    @pl.when(step == 0)
    def _():
        fill_forms(f_ref, kron_ref)
        acc_ref[...] = jnp.zeros(acc_ref.shape, F32)

    live = live_ref[0].astype(F32)
    t = t_ref[...]
    own = dot(kron_ref[0], t) * live

    @pl.when(step < n2 + n1)
    def _():
        below = jnp.where(step < n2, below2_ref[...], below1_ref[...])
        acc_ref[...] += dot(y_ref[...], own.astype(BF)) + dot(below, dot(kron_ref[2], t).astype(BF))

    @pl.when(step >= n2 + n1)
    def _():
        total = own + dot(kron_ref[1], shifted_ref[...]) * live
        acc_ref[...] += dot(y_ref[...], total.astype(BF))

    @pl.when(step == pl.num_programs(0) - 1)
    def _():
        out_ref[...] = acc_ref[...]


def diag(live, forms, y, t, below2, below1, shifted):
    aux, size = y.shape
    units = size // SPAN
    n2, n1, nc = below2.shape[1] // SPAN, below1.shape[1] // SPAN, shifted.shape[0] // SPAN
    natural = lambda index: pl.BlockSpec((aux, SPAN), lambda i: (0, index(i)))
    turned = lambda index: pl.BlockSpec((SPAN, aux), lambda i: (index(i), 0))
    return pl.pallas_call(
        lambda *refs: diag_kernel(*refs, n2=n2, n1=n1),
        grid=(units,),
        in_specs=[
            pl.BlockSpec(memory_space=pltpu.SMEM),
            pl.BlockSpec(forms.shape, lambda i: (0, 0, 0)),
            natural(lambda i: i),
            turned(lambda i: i),
            natural(within(0, n2)),
            natural(within(n2, n1)),
            turned(within(n2 + n1, nc)),
        ],
        out_specs=pl.BlockSpec((aux, aux), lambda i: (0, 0)),
        out_shape=jax.ShapeDtypeStruct((aux, aux), F32),
        scratch_shapes=[pltpu.VMEM((3, SPAN, SPAN), BF), pltpu.VMEM((aux, aux), F32)],
        compiler_params=params(),
        cost_estimate=cost(2 * aux * size * (2 * SPAN + 2 * aux), 6 * aux * size),
        name="diag_product",
    )(live, forms, y, t, below2, below1, shifted)


def early_kernel(parity_ref, fw_ref, fv_ref, r2_ref, w_ref, ws_ref, raw_e_ref, v_ref, vs_ref, raw_o_ref, vc_ref, vcs_ref,
                 edge_ref, odd_ref, kw_ref, kv_ref, a1_ref, a2_ref):
    step = pl.program_id(0)
    even = parity_ref[0] == 0

    @pl.when(step == 0)
    def _():
        fill_forms(fw_ref, kw_ref)
        fill_forms(fv_ref, kv_ref)
        a1_ref[...] = jnp.zeros(a1_ref.shape, F32)
        a2_ref[...] = jnp.zeros(a2_ref.shape, F32)

    @pl.when(even)
    def _():
        w = (dot(kw_ref[0], w_ref[...]) + dot(kw_ref[1], ws_ref[...])).astype(BF)
        a1_ref[...] += dot(r2_ref[...], w)
        v = (dot(kv_ref[0], v_ref[...]) + dot(kv_ref[1], vs_ref[...])).astype(BF)
        a2_ref[...] += dot(raw_e_ref[...], v)

    @pl.when(jnp.logical_not(even))
    def _():
        v = (dot(kv_ref[0], vc_ref[...]) + dot(kv_ref[1], vcs_ref[...])).astype(BF)
        a2_ref[...] += dot(raw_o_ref[...], v)

    @pl.when(step == pl.num_programs(0) - 1)
    def _():
        edge_ref[...] = a1_ref[...]
        odd_ref[...] = a2_ref[...].T


def early(parity, form_z, form_x, r2, w, ws, raw_e, v, vs, raw_o, vc, vcs):
    aux = r2.shape[0]
    n2, nc = r2.shape[1] // SPAN, raw_o.shape[1] // SPAN
    natural = lambda n: pl.BlockSpec((aux, SPAN), lambda i: (0, jnp.minimum(i, n - 1)))
    turned = lambda n: pl.BlockSpec((SPAN, aux), lambda i: (jnp.minimum(i, n - 1), 0))
    assert n2 == nc
    whole = pl.BlockSpec((aux, aux), lambda i: (0, 0))
    forms = pl.BlockSpec(form_z.shape, lambda i: (0, 0, 0))
    return pl.pallas_call(
        early_kernel,
        grid=(n2,),
        in_specs=[
            pl.BlockSpec(memory_space=pltpu.SMEM), forms, forms,
            natural(n2), turned(n2), turned(n2),
            natural(n2), turned(n2), turned(n2),
            natural(nc), turned(nc), turned(nc),
        ],
        out_specs=[whole, whole],
        out_shape=[jax.ShapeDtypeStruct((aux, aux), F32)] * 2,
        scratch_shapes=[pltpu.VMEM((2, SPAN, SPAN), BF)] * 2 + [pltpu.VMEM((aux, aux), F32)] * 2,
        compiler_params=params(),
        cost_estimate=cost(4 * aux * n2 * SPAN * (2 * SPAN + aux), 12 * aux * n2 * SPAN),
        name="early_edges",
    )(parity, form_z, form_x, r2, w, ws, raw_e, v, vs, raw_o, vc, vcs)


def last_kernel(parity_ref, fw_ref, so_far_ref, r1_ref, w_ref, ws_ref, v_ref, yc_ref, wc_ref, out_ref, kw_ref, a1_ref, a2_ref, *, nc):
    step = pl.program_id(0)
    even = parity_ref[0] == 0

    @pl.when(step == 0)
    def _():
        fill_forms(fw_ref, kw_ref)
        a1_ref[...] = so_far_ref[...]
        a2_ref[...] = jnp.zeros(a2_ref.shape, F32)

    @pl.when(even)
    def _():
        w = (dot(kw_ref[0], w_ref[...]) + dot(kw_ref[1], ws_ref[...])).astype(BF)
        r1 = r1_ref[...]
        a1_ref[...] += dot(r1, w)
        a2_ref[...] += dot(r1, v_ref[...])

    @pl.when(jnp.logical_and(jnp.logical_not(even), step < nc))
    def _():
        a1_ref[...] += dot(yc_ref[...], wc_ref[...])

    @pl.when(step == pl.num_programs(0) - 1)
    def _():
        out_ref[0] = a1_ref[...]
        out_ref[1] = a2_ref[...].T


def last(parity, form_z, so_far, r1, w, ws, n2, v, yc, wc):
    aux = r1.shape[0]
    n1, nc = r1.shape[1] // SPAN, yc.shape[1] // SPAN
    natural = lambda n: pl.BlockSpec((aux, SPAN), lambda i: (0, jnp.minimum(i, n - 1)))
    turned = lambda n, at=0: pl.BlockSpec((SPAN, aux), lambda i: (at + jnp.minimum(i, n - 1), 0))
    return pl.pallas_call(
        lambda *refs: last_kernel(*refs, nc=nc),
        grid=(n1,),
        in_specs=[
            pl.BlockSpec(memory_space=pltpu.SMEM),
            pl.BlockSpec(form_z.shape, lambda i: (0, 0, 0)),
            pl.BlockSpec((aux, aux), lambda i: (0, 0)),
            natural(n1), turned(n1, n2), turned(n1, n2), turned(n1), natural(nc), turned(nc),
        ],
        out_specs=pl.BlockSpec((2, aux, aux), lambda i: (0, 0, 0)),
        out_shape=jax.ShapeDtypeStruct((2, aux, aux), F32),
        scratch_shapes=[pltpu.VMEM((2, SPAN, SPAN), BF)] + [pltpu.VMEM((aux, aux), F32)] * 2,
        compiler_params=params(),
        cost_estimate=cost(4 * aux * n1 * SPAN * (SPAN + aux), 10 * aux * n1 * SPAN),
        name="last_edges",
    )(parity, form_z, so_far, r1, w, ws, v, yc, wc)


def scattered(value, axis):
    size = lax.axis_size(axis)
    if size & (size - 1):
        return lax.psum_scatter(value.astype(BF), axis, scatter_dimension=1, tiled=True).astype(F32)
    me = lax.axis_index(axis)
    k, aux, width = value.shape
    blocks = value.reshape(k, size, aux // size, width)
    reach = 1
    while reach < size:
        bit = (me // reach) % 2
        pairs = blocks.reshape(k, blocks.shape[1] // 2, 2, *blocks.shape[2:])
        kept = lax.dynamic_index_in_dim(pairs, bit, 2, keepdims=False)
        given = lax.dynamic_index_in_dim(pairs, 1 - bit, 2, keepdims=False).astype(BF)
        got = lax.ppermute(given, axis, [(i, i ^ reach) for i in range(size)])
        blocks = kept + got.astype(F32)
        reach *= 2
    return blocks[:, 0]


def body(three_centre, green_occ, green_vir, pair_live):
    rows, cols = lax.axis_size("row"), lax.axis_size("col")
    tile = green_occ.shape[2]
    y = three_centre[0, 0]
    parity = (lax.axis_index("row") % 2).astype(jnp.int32)
    even = parity == 0
    parity = parity[None]
    live = pair_live[0]
    live_bf = live[0].astype(BF)

    units = tile * tile // SPAN
    per = SPAN // tile
    n2 = nc = max(1, units * 5 // 16)
    n1 = units - n2 - nc
    cut2, cut1 = n2 * SPAN, (n2 + n1) * SPAN
    mu2, mu1 = n2 * per, (n2 + n1) * per

    down = [(i, i - 1) for i in range(1, cols)]
    up = [(i, i + 1) for i in range(cols - 1)]

    def in_rows(start, pairs):
        return [(r * cols + a, r * cols + b) for r in range(start, rows, 2) for a, b in pairs]

    both = ("row", "col")
    to_even = [(i, i - 1) for i in range(1, rows, 2)]
    to_odd = [(i, i + 1) for i in range(0, rows, 2)]
    flat = lambda s: s.reshape(-1, s.shape[-1])

    y_a2 = y[:, :cut2] * live_bf
    r2 = lax.ppermute(y_a2, "row", to_even)
    y_c = y[:, cut1:] * live_bf
    raw_c = lax.ppermute(y_c, "row", [(i, i + 2) for i in range(1, rows - 2, 2)])
    y_a1 = y[:, cut2:cut1] * live_bf
    r1 = lax.ppermute(y_a1, "row", to_even)

    occ_above = lax.ppermute(green_occ[0, 1], "row", [(i, i - 1) for i in range(1, rows)])
    vir_above = lax.ppermute(green_vir[0, 1], "col", down)
    form_x = jnp.stack([green_vir[0, 0].T, green_vir[0, 1].T])
    form_z = jnp.stack([green_vir[0, 0], vir_above])
    occ_x = green_occ[0, 1].T

    yt, sv_1, sv_c = turn_occ(
        live, jnp.concatenate([occ_x[mu2:mu1], occ_x[mu1:]]), y, tile, (mu1 - mu2, tile - mu1)
    )
    sv_1, sv_c = flat(sv_1), flat(sv_c)
    sv_1s = lax.ppermute(sv_1, both, in_rows(0, up))
    sv_c = lax.ppermute(sv_c, "row", to_odd)
    sw_c, sw_a, sv_2 = occ(
        jnp.concatenate([occ_above[mu1:], occ_above[:mu1], occ_x[:mu2]]), yt, (tile - mu1, mu1, mu2)
    )
    sw_c, sw_a, sv_2 = flat(sw_c), flat(sw_a), flat(sv_2)
    sw_cs = lax.ppermute(sw_c, both, in_rows(0, down))
    sw_as = lax.ppermute(sw_a, both, in_rows(0, down))
    sv_2s = lax.ppermute(sv_2, both, in_rows(0, up))
    (t,) = occ(green_occ[0, 0], yt, (tile,))
    t = flat(t)
    t_shifted = lax.ppermute(t[cut1:], "col", down)
    below2 = lax.ppermute(y_a2, "col", up)
    below1 = lax.ppermute(y_a1, "col", up)

    v_1 = lax.ppermute(vir(form_x, sv_1, sv_1s), "row", [(i, i - 2) for i in range(2, rows, 2)])
    w_c = lax.ppermute(vir(form_z, sw_c, sw_cs), "row", to_odd)
    raw_2 = lax.ppermute(r2, "row", [(i, i + 2) for i in range(0, rows - 2, 2)])
    sv_cs = lax.ppermute(sv_c, both, in_rows(1, up))

    edge, side = early(parity, form_z, form_x, r2, sw_a, sw_as, raw_2, sv_2, sv_2s, raw_c, sv_c, sv_cs)
    chi_d = diag(live, jnp.concatenate([form_z, green_vir[:, 1]]), y, t, below2, below1, t_shifted)
    ahead = scattered(jnp.stack([chi_d, side]), "col")
    chi_d, side = ahead[0], ahead[1]
    side = lax.ppermute(side.astype(BF), "row", [(i, i - 2) for i in range(2, rows)]).astype(F32)
    ends = scattered(last(parity, form_z, edge, r1, sw_a, sw_as, n2, v_1, y_c, w_c), "col")
    sent = jnp.where(even, ends[1] + side, ends[0]).astype(BF)
    got = lax.ppermute(sent, "row", [(i, i ^ 1) for i in range(rows)]).astype(F32)
    chi_n = got + jnp.where(even, ends[0], side)
    return chi_d[None], chi_n[None]


def solution(mesh):
    return jax.shard_map(
        body,
        mesh=mesh,
        in_specs=(
            P("row", "col", None, None),
            P("row", None, None, None),
            P("col", None, None, None),
            P("row", "col"),
        ),
        out_specs=(P("row", "col", None), P("row", "col", None)),
        check_vma=False,
    )
```

```python
import jax
import jax.numpy as jnp
from jax import lax
from jax.experimental import pallas as pl
from jax.experimental.pallas import tpu as pltpu
from jax.sharding import PartitionSpec as P

BF = jnp.bfloat16
F32 = jnp.float32
VMEM_BYTES = 48 * 1024 * 1024
SPAN = 256
SUBLANES = 8


def dot(a, b, dims=((1,), (0,))):
    return lax.dot_general(a, b, (dims, ((), ())), preferred_element_type=F32)


def iota(shape, axis):
    return lax.broadcasted_iota(jnp.int32, shape, axis)


def spread(g, group):
    m, k = g.shape
    pick_row = (iota((m * group, 1), 0) // group == iota((1, m), 1)).astype(BF)
    pick_col = (iota((k, 1), 0) == iota((1, k * group), 1) // group).astype(BF)
    full = dot(dot(pick_row, g).astype(BF), pick_col)
    same = iota((m * group, 1), 0) % group == iota((1, k * group), 1) % group
    return jnp.where(same, full, 0.0).astype(BF)


def repeated(g, count):
    t = g.shape[0]
    n = t * count
    pick = (iota((n, 1), 0) % t == iota((1, t), 1)).astype(BF)
    full = dot(dot(pick, g).astype(BF), pick, ((1,), (1,)))
    same = iota((n, 1), 0) // t == iota((1, n), 1) // t
    return jnp.where(same, full, 0.0).astype(BF)


def params():
    return pltpu.CompilerParams(vmem_limit_bytes=VMEM_BYTES)


def cost(flops, size):
    return pl.CostEstimate(flops=flops, bytes_accessed=size, transcendentals=0)


def occ_kernel(live_ref, g_ref, y_ref, out_ref, rows_ref, yt_ref, sems, *, slices):
    width, size = rows_ref.shape
    m, tile = g_ref.shape
    per = SPAN // tile
    copies = []
    to = 0
    for i, (start, count) in enumerate(slices):
        copies.append(
            pltpu.make_async_copy(y_ref.at[pl.ds(start, count)], rows_ref.at[pl.ds(to, count)], sems.at[i])
        )
        to += count
    for copy in copies:
        copy.start()
    kron = spread(g_ref[...], SUBLANES)
    live = live_ref[0].astype(F32).astype(BF)
    for copy in copies:
        copy.wait()
    for j in range(size // SPAN):
        part = rows_ref[:, j * SPAN : (j + 1) * SPAN] * live
        yt_ref[j * per : (j + 1) * per] = part.T.reshape(per, tile, width)
    pair = 2 * SUBLANES
    for s in range(tile // pair):
        part = yt_ref[:, s * pair : (s + 1) * pair, :].astype(F32)
        low, high = (
            part[:, k : k + SUBLANES].reshape(tile * SUBLANES, width).astype(BF) for k in (0, SUBLANES)
        )
        low, high = (dot(kron, x).reshape(m, SUBLANES, width) for x in (low, high))
        out_ref[:, s * pair : (s + 1) * pair, :] = jnp.concatenate([low, high], axis=1).astype(BF)


def occ(live, mat, y, slices):
    m, tile = mat.shape
    size = y.shape[1]
    width = sum(count for _, count in slices)
    out = pl.pallas_call(
        lambda *refs: occ_kernel(*refs, slices=slices),
        in_specs=[
            pl.BlockSpec(memory_space=pltpu.SMEM),
            pl.BlockSpec(memory_space=pltpu.VMEM),
            pl.BlockSpec(memory_space=pl.ANY),
        ],
        out_specs=pl.BlockSpec(memory_space=pltpu.VMEM),
        out_shape=jax.ShapeDtypeStruct((m, tile, width), BF),
        scratch_shapes=[
            pltpu.VMEM((width, size), BF),
            pltpu.VMEM((tile, tile, width), BF),
            pltpu.SemaphoreType.DMA((len(slices),)),
        ],
        compiler_params=params(),
        cost_estimate=cost(2 * width * size * m * SUBLANES, 4 * width * size),
        name="occ",
    )(live, mat, y)
    return out.reshape(m * tile, width)


def vir_kernel(live_ref, g_ref, y_ref, *rest):
    *added, out_ref, kron_ref = rest

    @pl.when(pl.program_id(0) == 0)
    def _():
        scale = live_ref[0].astype(F32)
        kron_ref[...] = (repeated(g_ref[...], SPAN // g_ref.shape[0]).astype(F32) * scale).astype(BF)

    for j in range(y_ref.shape[1] // SPAN):
        at = slice(j * SPAN, (j + 1) * SPAN)
        got = dot(y_ref[:, at], kron_ref[...])
        for ref in added:
            got = got + ref[:, at].astype(F32)
        out_ref[:, at] = got.astype(BF)


def vir(live, mat, y, added=()):
    aux, size = y.shape
    span = 4 * SPAN if size % (4 * SPAN) == 0 else SPAN
    block = pl.BlockSpec((aux, span), lambda i: (0, i))
    return pl.pallas_call(
        vir_kernel,
        grid=(size // span,),
        in_specs=[
            pl.BlockSpec(memory_space=pltpu.SMEM),
            pl.BlockSpec(mat.shape, lambda i: (0, 0)),
            block,
            *(block for _ in added),
        ],
        out_specs=block,
        out_shape=jax.ShapeDtypeStruct((aux, size), BF),
        scratch_shapes=[pltpu.VMEM((SPAN, SPAN), BF)],
        compiler_params=params(),
        cost_estimate=cost(2 * aux * size * SPAN, 2 * (2 + len(added)) * aux * size),
        name="vir",
    )(live, mat, y, *added)


def product_kernel(z_ref, x_ref, out_ref, acc_ref):
    step = pl.program_id(0)

    @pl.when(step == 0)
    def _():
        acc_ref[...] = dot(z_ref[...], x_ref[...])

    @pl.when(step > 0)
    def _():
        acc_ref[...] += dot(z_ref[...], x_ref[...])

    @pl.when(step == pl.num_programs(0) - 1)
    def _():
        out_ref[...] = acc_ref[...].T


def product(z, x):
    aux, size = z.shape
    width = x.shape[1]
    span = 4 * SPAN if size % (4 * SPAN) == 0 else SPAN
    return pl.pallas_call(
        product_kernel,
        grid=(size // span,),
        in_specs=[pl.BlockSpec((aux, span), lambda i: (0, i)), pl.BlockSpec((span, width), lambda i: (i, 0))],
        out_specs=pl.BlockSpec((width, aux), lambda i: (0, 0)),
        out_shape=jax.ShapeDtypeStruct((width, aux), F32),
        scratch_shapes=[pltpu.VMEM((aux, width), F32)],
        compiler_params=params(),
        cost_estimate=cost(2 * aux * size * width, 2 * size * (aux + width)),
        name="product",
    )(z, x)


def scattered(value, axis):
    size = lax.axis_size(axis)
    if size & (size - 1):
        return lax.psum_scatter(value.astype(BF), axis, scatter_dimension=0, tiled=True).astype(F32)
    me = lax.axis_index(axis)
    blocks = value.reshape(size, value.shape[0] // size, value.shape[1])
    reach = 1
    while reach < size:
        bit = (me // reach) % 2
        pairs = blocks.reshape(blocks.shape[0] // 2, 2, *blocks.shape[1:])
        kept = lax.dynamic_index_in_dim(pairs, bit, 1, keepdims=False)
        given = lax.dynamic_index_in_dim(pairs, 1 - bit, 1, keepdims=False).astype(BF)
        got = lax.ppermute(given, axis, [(i, i ^ reach) for i in range(size)])
        blocks = kept + got.astype(F32)
        reach *= 2
    return blocks[0]


def chunks_of(aux, owners):
    each = aux // owners
    small = 128 // owners
    if owners * small == 128 and small % 16 == 0 and each % 16 == 0 and each > 2 * small:
        cuts = [0, small, each - small, each]
        return [[(j * each + a, b - a) for j in range(owners)] for a, b in zip(cuts, cuts[1:])]
    return [[(0, aux)]]


def body(three_centre, green_occ, green_vir, pair_live):
    rows, cols = lax.axis_size("row"), lax.axis_size("col")
    y = three_centre[0, 0]
    aux = y.shape[0]
    live = pair_live[0]
    up_row = [(i, i - 1) for i in range(1, rows)]
    up_col = [(i, i - 1) for i in range(1, cols)]
    to_own, to_lower = green_occ[0, 0].T, green_occ[0, 1].T

    halves = [occ(live, to_lower, y, part) for part in chunks_of(aux, cols)]
    above = [lax.ppermute(half, "row", up_row) for half in halves]
    shifted = lax.ppermute(vir(live, green_vir[0, 1].T, y), "col", up_col)
    own = occ(live, to_own, y, [(0, aux)])
    z = vir(live, green_vir[0, 0].T, y, (shifted,))
    chi_d = scattered(product(z, own), "col")
    chi_n = jnp.concatenate([scattered(product(z, half), "col") for half in above])
    return chi_d[None], chi_n[None]


def solution(mesh):
    return jax.shard_map(
        body,
        mesh=mesh,
        in_specs=(
            P("row", "col", None, None),
            P("row", None, None, None),
            P("col", None, None, None),
            P("row", "col"),
        ),
        out_specs=(P("row", "col", None), P("row", "col", None)),
        check_vma=False,
    )
```

```python
import jax
import jax.numpy as jnp
from jax import lax
from jax.experimental import pallas as pl
from jax.experimental.pallas import tpu as pltpu
from jax.sharding import PartitionSpec as P

BF = jnp.bfloat16
F32 = jnp.float32
VMEM_BYTES = 48 * 1024 * 1024
SPAN = 256
SUBLANES = 8
SMALL = 128
PIECES = 2


def dot(a, b, dims=((1,), (0,))):
    return lax.dot_general(a, b, (dims, ((), ())), preferred_element_type=F32)


def iota(shape, axis):
    return lax.broadcasted_iota(jnp.int32, shape, axis)


def spread(g, group):
    m, k = g.shape
    pick_row = (iota((m * group, 1), 0) // group == iota((1, m), 1)).astype(BF)
    pick_col = (iota((k, 1), 0) == iota((1, k * group), 1) // group).astype(BF)
    full = dot(dot(pick_row, g).astype(BF), pick_col)
    same = iota((m * group, 1), 0) % group == iota((1, k * group), 1) % group
    return jnp.where(same, full, 0.0).astype(BF)


def repeated(g, count):
    t = g.shape[0]
    n = t * count
    pick = (iota((n, 1), 0) % t == iota((1, t), 1)).astype(BF)
    full = dot(dot(pick, g).astype(BF), pick, ((1,), (1,)))
    same = iota((n, 1), 0) // t == iota((1, n), 1) // t
    return jnp.where(same, full, 0.0).astype(BF)


def params():
    return pltpu.CompilerParams(vmem_limit_bytes=VMEM_BYTES)


def cost(flops, size):
    return pl.CostEstimate(flops=1, bytes_accessed=1, transcendentals=0)


def unused(before):
    return [pl.BlockSpec(memory_space=pl.ANY)] * len(before)


def occ_kernel(live_ref, g_ref, y_ref, *rest, slices):
    out_ref, rows_ref, yt_ref, sems = rest[-4:]
    width, size = rows_ref.shape
    m, tile = g_ref.shape
    per = SPAN // tile
    copies = []
    to = 0
    for i, (start, count) in enumerate(slices):
        copies.append(
            pltpu.make_async_copy(y_ref.at[pl.ds(start, count)], rows_ref.at[pl.ds(to, count)], sems.at[i])
        )
        to += count
    for copy in copies:
        copy.start()
    kron = spread(g_ref[...], SUBLANES)
    live = live_ref[0].astype(F32).astype(BF)
    for copy in copies:
        copy.wait()
    for j in range(size // SPAN):
        part = rows_ref[:, j * SPAN : (j + 1) * SPAN] * live
        yt_ref[j * per : (j + 1) * per] = part.T.reshape(per, tile, width)
    pair = 2 * SUBLANES
    for s in range(tile // pair):
        part = yt_ref[:, s * pair : (s + 1) * pair, :].astype(F32)
        low, high = (
            part[:, k : k + SUBLANES].reshape(tile * SUBLANES, width).astype(BF) for k in (0, SUBLANES)
        )
        low, high = (dot(kron, x).reshape(m, SUBLANES, width) for x in (low, high))
        out_ref[:, s * pair : (s + 1) * pair, :] = jnp.concatenate([low, high], axis=1).astype(BF)


def occ(live, mat, y, slices, before=()):
    m, tile = mat.shape
    size = y.shape[1]
    width = sum(count for _, count in slices)
    out = pl.pallas_call(
        lambda *refs: occ_kernel(*refs, slices=slices),
        in_specs=[
            pl.BlockSpec(memory_space=pltpu.SMEM),
            pl.BlockSpec(memory_space=pltpu.VMEM),
            pl.BlockSpec(memory_space=pl.ANY),
            *unused(before),
        ],
        out_specs=pl.BlockSpec(memory_space=pltpu.VMEM),
        out_shape=jax.ShapeDtypeStruct((m, tile, width), BF),
        scratch_shapes=[
            pltpu.VMEM((width, size), BF),
            pltpu.VMEM((tile, tile, width), BF),
            pltpu.SemaphoreType.DMA((len(slices),)),
        ],
        compiler_params=params(),
        cost_estimate=cost(2 * width * size * m * SUBLANES, 4 * width * size),
        name="occ",
    )(live, mat, y, *before)
    return out.reshape(m * tile, width)


def vir_kernel(live_ref, g_ref, y_ref, *rest, n_added):
    added = rest[:n_added]
    out_ref, kron_ref = rest[-2:]

    @pl.when(pl.program_id(0) == 0)
    def _():
        scale = live_ref[0].astype(F32)
        kron_ref[...] = (repeated(g_ref[...], SPAN // g_ref.shape[0]).astype(F32) * scale).astype(BF)

    for j in range(y_ref.shape[1] // SPAN):
        at = slice(j * SPAN, (j + 1) * SPAN)
        got = dot(y_ref[:, at], kron_ref[...])
        for ref in added:
            got = got + ref[:, at].astype(F32)
        out_ref[:, at] = got.astype(BF)


def vir(live, mat, y, piece, added=(), before=()):
    aux = y.shape[0]
    size = y.shape[1] // PIECES
    span = 4 * SPAN if size % (4 * SPAN) == 0 else SPAN
    block = pl.BlockSpec((aux, span), lambda i: (0, i))
    return pl.pallas_call(
        lambda *refs: vir_kernel(*refs, n_added=len(added)),
        grid=(size // span,),
        in_specs=[
            pl.BlockSpec(memory_space=pltpu.SMEM),
            pl.BlockSpec(mat.shape, lambda i: (0, 0)),
            pl.BlockSpec((aux, span), lambda i: (0, piece * (size // span) + i)),
            *(block for _ in added),
            *unused(before),
        ],
        out_specs=block,
        out_shape=jax.ShapeDtypeStruct((aux, size), BF),
        scratch_shapes=[pltpu.VMEM((SPAN, SPAN), BF)],
        compiler_params=params(),
        cost_estimate=cost(2 * aux * size * SPAN, 2 * (2 + len(added)) * aux * size),
        name="vir",
    )(live, mat, y, *added, *before)


def product_kernel(x_ref, *rest, steps):
    z_refs = rest[:PIECES]
    out_ref, acc_ref = rest[-2:]
    step = pl.program_id(0)

    @pl.when(step == 0)
    def _():
        acc_ref[...] = dot(z_refs[0][...], x_ref[...])

    for i, z_ref in enumerate(z_refs):

        @pl.when(jnp.logical_and(step > 0, step // steps == i))
        def _(z_ref=z_ref):
            acc_ref[...] += dot(z_ref[...], x_ref[...])

    @pl.when(step == pl.num_programs(0) - 1)
    def _():
        out_ref[...] = acc_ref[...].T


def product(zs, x, before=()):
    aux, size = zs[0].shape
    width = x.shape[1]
    span = 4 * SPAN if size % (4 * SPAN) == 0 else SPAN
    steps = size // span
    piece = lambda k: pl.BlockSpec((aux, span), lambda i: (0, jnp.clip(i - k * steps, 0, steps - 1)))
    return pl.pallas_call(
        lambda *refs: product_kernel(*refs, steps=steps),
        grid=(len(zs) * steps,),
        in_specs=[pl.BlockSpec((span, width), lambda i: (i, 0)), *(piece(k) for k in range(len(zs))), *unused(before)],
        out_specs=pl.BlockSpec((width, aux), lambda i: (0, 0)),
        out_shape=jax.ShapeDtypeStruct((width, aux), F32),
        scratch_shapes=[pltpu.VMEM((aux, width), F32)],
        compiler_params=params(),
        cost_estimate=cost(2 * aux * size * width, 2 * size * (aux + width)),
        name="product",
    )(x, *zs, *before)


def scattered(parts, axis):
    size = lax.axis_size(axis)
    blocks = [part.reshape(size, part.shape[0] // size, part.shape[1]) for part in parts]
    blocks = jnp.concatenate(blocks, axis=1) if len(blocks) > 1 else blocks[0]
    if size & (size - 1):
        return lax.psum_scatter(blocks.astype(BF), axis, scatter_dimension=0).astype(F32)
    me = lax.axis_index(axis)
    reach = 1
    while reach < size:
        bit = (me // reach) % 2
        pairs = blocks.reshape(blocks.shape[0] // 2, 2, *blocks.shape[1:])
        kept = lax.dynamic_index_in_dim(pairs, bit, 1, keepdims=False)
        given = lax.dynamic_index_in_dim(pairs, 1 - bit, 1, keepdims=False).astype(BF)
        got = lax.ppermute(given, axis, [(i, i ^ reach) for i in range(size)])
        blocks = kept + got.astype(F32)
        reach *= 2
    return blocks[0]


def chunks_of(aux, owners):
    each = aux // owners
    small = SMALL // owners
    if owners * small == SMALL and small % 16 == 0 and each % 16 == 0 and each > small:
        cuts = [0, each - small, each]
        return [[(j * each + a, b - a) for j in range(owners)] for a, b in zip(cuts, cuts[1:])]
    return [[(0, aux)]]


def body(three_centre, green_occ, green_vir, pair_live):
    rows, cols = lax.axis_size("row"), lax.axis_size("col")
    y = three_centre[0, 0]
    aux = y.shape[0]
    live = pair_live[0]
    up_row = [(i, i - 1) for i in range(1, rows)]
    up_col = [(i, i - 1) for i in range(1, cols)]
    to_own, to_lower = green_occ[0, 0].T, green_occ[0, 1].T

    first, *others = chunks_of(aux, cols)
    send = lambda half: lax.ppermute(half, "row", up_row)
    last = occ(live, to_lower, y, first)
    above = [send(last)]
    shifted = []
    for i in range(PIECES):
        last = vir(live, green_vir[0, 1].T, y, i, before=(last,))
        shifted.append(lax.ppermute(last, "col", up_col))
    for part in others:
        last = occ(live, to_lower, y, part, before=(last,))
        above.append(send(last))
    own = occ(live, to_own, y, [(0, aux)], before=(last,))
    zs = []
    for i in range(PIECES):
        zs.append(vir(live, green_vir[0, 0].T, y, i, (shifted[i],), before=(own,)))
    chi_d = scattered([product(zs, own)], "col")
    blocks = []
    last = chi_d
    for half in above:
        last = product(zs, half, before=(last,))
        blocks.append(last)
    chi_n = scattered(blocks, "col")
    return chi_d[None], chi_n[None]


def solution(mesh):
    return jax.shard_map(
        body,
        mesh=mesh,
        in_specs=(
            P("row", "col", None, None),
            P("row", None, None, None),
            P("col", None, None, None),
            P("row", "col"),
        ),
        out_specs=(P("row", "col", None), P("row", "col", None)),
        check_vma=False,
    )
```

```python
import jax
import jax.numpy as jnp
from jax import lax
from jax.experimental import pallas as pl
from jax.experimental.pallas import tpu as pltpu
from jax.sharding import PartitionSpec as P

BF = jnp.bfloat16
F32 = jnp.float32
VMEM_BYTES = 48 * 1024 * 1024
SPAN = 256
SUBLANES = 8
SMALL = 128
PIECES = 2


def dot(a, b, dims=((1,), (0,))):
    return lax.dot_general(a, b, (dims, ((), ())), preferred_element_type=F32)


def iota(shape, axis):
    return lax.broadcasted_iota(jnp.int32, shape, axis)


def spread(g, group):
    m, k = g.shape
    pick_row = (iota((m * group, 1), 0) // group == iota((1, m), 1)).astype(BF)
    pick_col = (iota((k, 1), 0) == iota((1, k * group), 1) // group).astype(BF)
    full = dot(dot(pick_row, g).astype(BF), pick_col)
    same = iota((m * group, 1), 0) % group == iota((1, k * group), 1) % group
    return jnp.where(same, full, 0.0).astype(BF)


def repeated(g, count):
    t = g.shape[0]
    n = t * count
    pick = (iota((n, 1), 0) % t == iota((1, t), 1)).astype(BF)
    full = dot(dot(pick, g).astype(BF), pick, ((1,), (1,)))
    same = iota((n, 1), 0) // t == iota((1, n), 1) // t
    return jnp.where(same, full, 0.0).astype(BF)


def params():
    return pltpu.CompilerParams(vmem_limit_bytes=VMEM_BYTES)


def cost(flops, size):
    return pl.CostEstimate(flops=1, bytes_accessed=1, transcendentals=0)


def unused(before):
    return [pl.BlockSpec(memory_space=pl.ANY)] * len(before)


def occ_kernel(live_ref, g_ref, y_ref, *rest, groups):
    out_ref, rows_ref, yt_ref, held_ref, in_sems, out_sems = rest[-6:]
    tile, m = g_ref.shape
    size = y_ref.shape[1]
    per = SPAN // tile
    fetch = []
    to = 0
    for slices, _ in groups:
        for start, count in slices:
            fetch.append(
                pltpu.make_async_copy(
                    y_ref.at[pl.ds(start, count)], rows_ref.at[pl.ds(to, count)], in_sems.at[len(fetch)]
                )
            )
            to += count
    for copy in fetch:
        copy.start()
    kron = spread(g_ref[...].T, SUBLANES)
    live = live_ref[0].astype(F32).astype(BF)
    pair = 2 * SUBLANES
    store = []
    at, done = 0, 0
    for k, (slices, width) in enumerate(groups):
        for copy in fetch[done : done + len(slices)]:
            copy.wait()
        done += len(slices)
        lanes = slice(at, at + width)
        for j in range(size // SPAN):
            part = rows_ref[lanes, j * SPAN : (j + 1) * SPAN] * live
            yt_ref[k, j * per : (j + 1) * per, :, :width] = part.T.reshape(per, tile, width)
        for s in range(tile // pair):
            part = yt_ref[k, :, s * pair : (s + 1) * pair, :width].astype(F32)
            low, high = (
                part[:, i : i + SUBLANES].reshape(tile * SUBLANES, width).astype(BF) for i in (0, SUBLANES)
            )
            low, high = (dot(kron, x).reshape(m, SUBLANES, width) for x in (low, high))
            held_ref[:, s * pair : (s + 1) * pair, lanes] = jnp.concatenate([low, high], axis=1).astype(BF)
        store.append(
            pltpu.make_async_copy(
                held_ref.at[:, :, pl.ds(at, width)], out_ref.at[:, :, pl.ds(at, width)], out_sems.at[k]
            )
        )
        store[-1].start()
        at += width
    for copy in store:
        copy.wait()


def grouped(slices):
    groups, held = [], []
    for start, count in slices:
        held.append((start, count))
        width = sum(n for _, n in held)
        if width >= SPAN and width % 128 == 0:
            groups.append((held, width))
            held = []
    if held:
        groups.append((held, sum(n for _, n in held)))
    return groups


def occ(live, mat, y, slices, before=()):
    tile, m = mat.shape
    size = y.shape[1]
    groups = grouped(slices)
    width = sum(n for _, n in groups)
    widest = max(n for _, n in groups)
    out = pl.pallas_call(
        lambda *refs: occ_kernel(*refs, groups=groups),
        in_specs=[
            pl.BlockSpec(memory_space=pltpu.SMEM),
            pl.BlockSpec(memory_space=pltpu.VMEM),
            pl.BlockSpec(memory_space=pl.ANY),
            *unused(before),
        ],
        out_specs=pl.BlockSpec(memory_space=pl.ANY),
        out_shape=jax.ShapeDtypeStruct((m, tile, width), BF),
        scratch_shapes=[
            pltpu.VMEM((width, size), BF),
            pltpu.VMEM((len(groups), tile, tile, widest), BF),
            pltpu.VMEM((m, tile, width), BF),
            pltpu.SemaphoreType.DMA((len(slices),)),
            pltpu.SemaphoreType.DMA((len(groups),)),
        ],
        compiler_params=params(),
        cost_estimate=cost(2 * width * size * m * SUBLANES, 4 * width * size),
        name="occ",
    )(live, mat, y, *before)
    return out.reshape(m * tile, width)


def vir_kernel(live_ref, g_ref, y_ref, *rest, n_added):
    added = rest[:n_added]
    out_ref, kron_ref = rest[-2:]

    @pl.when(pl.program_id(0) == 0)
    def _():
        scale = live_ref[0].astype(F32)
        kron_ref[...] = (repeated(g_ref[...], SPAN // g_ref.shape[0]).astype(F32) * scale).astype(BF)

    for j in range(y_ref.shape[1] // SPAN):
        at = slice(j * SPAN, (j + 1) * SPAN)
        got = dot(y_ref[:, at], kron_ref[...])
        for ref in added:
            got = got + ref[:, at].astype(F32)
        out_ref[:, at] = got.astype(BF)


def vir(live, mat, y, piece, added=(), before=()):
    aux = y.shape[0]
    size = y.shape[1] // PIECES
    span = 4 * SPAN if size % (4 * SPAN) == 0 else SPAN
    block = pl.BlockSpec((aux, span), lambda i: (0, i))
    return pl.pallas_call(
        lambda *refs: vir_kernel(*refs, n_added=len(added)),
        grid=(size // span,),
        in_specs=[
            pl.BlockSpec(memory_space=pltpu.SMEM),
            pl.BlockSpec(mat.shape, lambda i: (0, 0)),
            pl.BlockSpec((aux, span), lambda i: (0, piece * (size // span) + i)),
            *(block for _ in added),
            *unused(before),
        ],
        out_specs=block,
        out_shape=jax.ShapeDtypeStruct((aux, size), BF),
        scratch_shapes=[pltpu.VMEM((SPAN, SPAN), BF)],
        compiler_params=params(),
        cost_estimate=cost(2 * aux * size * SPAN, 2 * (2 + len(added)) * aux * size),
        name="vir",
    )(live, mat, y, *added, *before)


def product_kernel(x_ref, *rest, steps):
    z_refs = rest[:PIECES]
    out_ref, acc_ref = rest[-2:]
    step = pl.program_id(0)

    @pl.when(step == 0)
    def _():
        acc_ref[...] = dot(z_refs[0][...], x_ref[...])

    for i, z_ref in enumerate(z_refs):

        @pl.when(jnp.logical_and(step > 0, step // steps == i))
        def _(z_ref=z_ref):
            acc_ref[...] += dot(z_ref[...], x_ref[...])

    @pl.when(step == pl.num_programs(0) - 1)
    def _():
        out_ref[...] = acc_ref[...].T


def product(zs, x, before=()):
    aux, size = zs[0].shape
    width = x.shape[1]
    span = 4 * SPAN if size % (4 * SPAN) == 0 else SPAN
    steps = size // span
    piece = lambda k: pl.BlockSpec((aux, span), lambda i: (0, jnp.clip(i - k * steps, 0, steps - 1)))
    return pl.pallas_call(
        lambda *refs: product_kernel(*refs, steps=steps),
        grid=(len(zs) * steps,),
        in_specs=[pl.BlockSpec((span, width), lambda i: (i, 0)), *(piece(k) for k in range(len(zs))), *unused(before)],
        out_specs=pl.BlockSpec((width, aux), lambda i: (0, 0)),
        out_shape=jax.ShapeDtypeStruct((width, aux), F32),
        scratch_shapes=[pltpu.VMEM((aux, width), F32)],
        compiler_params=params(),
        cost_estimate=cost(2 * aux * size * width, 2 * size * (aux + width)),
        name="product",
    )(x, *zs, *before)


def scattered(parts, axis, direct):
    size = lax.axis_size(axis)
    blocks = [part.reshape(size, part.shape[0] // size, part.shape[1]) for part in parts]
    blocks = jnp.concatenate(blocks, axis=1) if len(blocks) > 1 else blocks[0]
    if size & (size - 1):
        return lax.psum_scatter(blocks.astype(BF), axis, scatter_dimension=0).astype(F32)
    me = lax.axis_index(axis)
    reaches = [1 << i for i in range(size.bit_length() - 1)]
    if direct and size <= 4:
        total = lax.dynamic_index_in_dim(blocks, me, 0, keepdims=False)
        for reach in range(1, size):
            given = lax.dynamic_index_in_dim(blocks, me ^ reach, 0, keepdims=False).astype(BF)
            total = total + lax.ppermute(given, axis, [(i, i ^ reach) for i in range(size)]).astype(F32)
        return total
    for reach in reaches:
        bit = (me // reach) % 2
        pairs = blocks.reshape(blocks.shape[0] // 2, 2, *blocks.shape[1:])
        kept = lax.dynamic_index_in_dim(pairs, bit, 1, keepdims=False)
        given = lax.dynamic_index_in_dim(pairs, 1 - bit, 1, keepdims=False).astype(BF)
        got = lax.ppermute(given, axis, [(i, i ^ reach) for i in range(size)])
        blocks = kept + got.astype(F32)
    return blocks[0]


def chunks_of(aux, owners):
    each = aux // owners
    small = SMALL // owners
    if owners * small == SMALL and small % 16 == 0 and each % 16 == 0 and each > small:
        cuts = [0, each - small, each]
        return [[(j * each + a, b - a) for j in range(owners)] for a, b in zip(cuts, cuts[1:])]
    return [[(0, aux)]]


def body(three_centre, green_occ, green_vir, pair_live):
    rows, cols = lax.axis_size("row"), lax.axis_size("col")
    y = three_centre[0, 0]
    aux = y.shape[0]
    live = pair_live[0]
    up_row = [(i, i - 1) for i in range(1, rows)]
    up_col = [(i, i - 1) for i in range(1, cols)]
    to_own, to_lower = green_occ[0, 0], green_occ[0, 1]

    first, *others = chunks_of(aux, cols)
    send = lambda half: lax.ppermute(half, "row", up_row)
    last = occ(live, to_lower, y, first)
    above = [send(last)]
    shifted = []
    for i in range(PIECES):
        last = vir(live, green_vir[0, 1].T, y, i, before=(last,))
        shifted.append(lax.ppermute(last, "col", up_col))
    for part in others:
        last = occ(live, to_lower, y, part, before=(last,))
        above.append(send(last))
    own = occ(live, to_own, y, [(i, min(SPAN, aux - i)) for i in range(0, aux, SPAN)], before=(last,))
    zs = []
    for i in range(PIECES):
        zs.append(vir(live, green_vir[0, 0].T, y, i, (shifted[i],), before=(own,)))
    chi_d = scattered([product(zs, own)], "col", True)
    blocks = []
    last = chi_d
    for half in above:
        last = scattered([product(zs, half, before=(last,))], "col", half is not above[-1])
        blocks.append(last)
    return chi_d[None], jnp.concatenate(blocks)[None]


def solution(mesh):
    return jax.shard_map(
        body,
        mesh=mesh,
        in_specs=(
            P("row", "col", None, None),
            P("row", None, None, None),
            P("col", None, None, None),
            P("row", "col"),
        ),
        out_specs=(P("row", "col", None), P("row", "col", None)),
        check_vma=False,
    )
```

```python
import jax
import jax.numpy as jnp
from jax import lax
from jax.experimental import pallas as pl
from jax.experimental.pallas import tpu as pltpu
from jax.sharding import PartitionSpec as P

BF = jnp.bfloat16
F32 = jnp.float32
VMEM_BYTES = 48 * 1024 * 1024
SPAN = 256
SUBLANES = 8
CHUNKS = (512, 128)
PIECES = 2


def dot(a, b, dims=((1,), (0,))):
    return lax.dot_general(a, b, (dims, ((), ())), preferred_element_type=F32)


def iota(shape, axis):
    return lax.broadcasted_iota(jnp.int32, shape, axis)


def spread(g, group):
    m, k = g.shape
    pick_row = (iota((m * group, 1), 0) // group == iota((1, m), 1)).astype(BF)
    pick_col = (iota((k, 1), 0) == iota((1, k * group), 1) // group).astype(BF)
    full = dot(dot(pick_row, g).astype(BF), pick_col)
    same = iota((m * group, 1), 0) % group == iota((1, k * group), 1) % group
    return jnp.where(same, full, 0.0).astype(BF)


def repeated(g, count):
    t = g.shape[0]
    n = t * count
    pick = (iota((n, 1), 0) % t == iota((1, t), 1)).astype(BF)
    full = dot(dot(pick, g).astype(BF), pick, ((1,), (1,)))
    same = iota((n, 1), 0) // t == iota((1, n), 1) // t
    return jnp.where(same, full, 0.0).astype(BF)


def params():
    return pltpu.CompilerParams(vmem_limit_bytes=VMEM_BYTES)


def cost(flops, size):
    return pl.CostEstimate(flops=1, bytes_accessed=1, transcendentals=0)


def unused(before):
    return [pl.BlockSpec(memory_space=pl.ANY)] * len(before)


def occ_kernel(live_ref, g_ref, y_ref, *rest, groups, which, cuts):
    rows_ref, yt_ref, held_ref, in_sems, out_sems = rest[-5:]
    out_refs = rest[-5 - cuts : -5]
    tile, m = g_ref.shape[1:]
    size = y_ref.shape[1]
    per = SPAN // tile
    fetch = []
    to = 0
    for slices, _ in groups:
        for start, count in slices:
            fetch.append(
                pltpu.make_async_copy(
                    y_ref.at[pl.ds(start, count)], rows_ref.at[pl.ds(to, count)], in_sems.at[len(fetch)]
                )
            )
            to += count
    for copy in fetch:
        copy.start()
    kron = spread(g_ref[which].T, SUBLANES)
    live = live_ref[0].astype(F32).astype(BF)
    pair = 2 * SUBLANES
    store = []
    at, done = 0, 0
    for k, (slices, width) in enumerate(groups):
        for copy in fetch[done : done + len(slices)]:
            copy.wait()
        done += len(slices)
        lanes = slice(at, at + width)
        for j in range(size // SPAN):
            part = rows_ref[lanes, j * SPAN : (j + 1) * SPAN] * live
            yt_ref[k, j * per : (j + 1) * per, :, :width] = part.T.reshape(per, tile, width)
        for s in range(tile // pair):
            part = yt_ref[k, :, s * pair : (s + 1) * pair, :width].astype(F32)
            low, high = (
                part[:, i : i + SUBLANES].reshape(tile * SUBLANES, width).astype(BF) for i in (0, SUBLANES)
            )
            low, high = (dot(kron, x).reshape(m, SUBLANES, width) for x in (low, high))
            held_ref[:, s * pair : (s + 1) * pair, lanes] = jnp.concatenate([low, high], axis=1).astype(BF)
        for c, out_ref in enumerate(out_refs):
            some = pl.ds(c * (m // cuts), m // cuts)
            store.append(
                pltpu.make_async_copy(
                    held_ref.at[some, :, pl.ds(at, width)], out_ref.at[:, :, pl.ds(at, width)], out_sems.at[k, c]
                )
            )
            store[-1].start()
        at += width
    for copy in store:
        copy.wait()


def grouped(slices):
    groups, held = [], []
    for start, count in slices:
        held.append((start, count))
        width = sum(n for _, n in held)
        if width >= SPAN and width % 128 == 0:
            groups.append((held, width))
            held = []
    if held:
        groups.append((held, sum(n for _, n in held)))
    return groups


def occ(live, mats, which, y, slices, before=(), cuts=1):
    tile, m = mats.shape[1:]
    size = y.shape[1]
    groups = grouped(slices)
    width = sum(n for _, n in groups)
    widest = max(n for _, n in groups)
    outs = pl.pallas_call(
        lambda *refs: occ_kernel(*refs, groups=groups, which=which, cuts=cuts),
        in_specs=[
            pl.BlockSpec(memory_space=pltpu.SMEM),
            pl.BlockSpec(memory_space=pltpu.VMEM),
            pl.BlockSpec(memory_space=pl.ANY),
            *unused(before),
        ],
        out_specs=[pl.BlockSpec(memory_space=pl.ANY)] * cuts,
        out_shape=[jax.ShapeDtypeStruct((m // cuts, tile, width), BF)] * cuts,
        scratch_shapes=[
            pltpu.VMEM((width, size), BF),
            pltpu.VMEM((len(groups), tile, tile, widest), BF),
            pltpu.VMEM((m, tile, width), BF),
            pltpu.SemaphoreType.DMA((len(slices),)),
            pltpu.SemaphoreType.DMA((len(groups), cuts)),
        ],
        compiler_params=params(),
        cost_estimate=cost(2 * width * size * m * SUBLANES, 4 * width * size),
        name="occ",
    )(live, mats, y, *before)
    return [out.reshape(-1, width) for out in outs]


def vir_kernel(live_ref, g_ref, y_ref, *rest, n_added):
    added = rest[:n_added]
    out_ref, kron_ref = rest[-2:]

    @pl.when(pl.program_id(0) == 0)
    def _():
        scale = live_ref[0].astype(F32)
        kron_ref[...] = (repeated(g_ref[...], SPAN // g_ref.shape[0]).astype(F32) * scale).astype(BF)

    for j in range(y_ref.shape[1] // SPAN):
        at = slice(j * SPAN, (j + 1) * SPAN)
        got = dot(y_ref[:, at], kron_ref[...])
        for ref in added:
            got = got + ref[:, at].astype(F32)
        out_ref[:, at] = got.astype(BF)


def vir(live, mat, y, piece, added=(), before=()):
    aux = y.shape[0]
    size = y.shape[1] // PIECES
    span = 4 * SPAN if size % (4 * SPAN) == 0 else SPAN
    block = pl.BlockSpec((aux, span), lambda i: (0, i))
    return pl.pallas_call(
        lambda *refs: vir_kernel(*refs, n_added=len(added)),
        grid=(size // span,),
        in_specs=[
            pl.BlockSpec(memory_space=pltpu.SMEM),
            pl.BlockSpec(mat.shape, lambda i: (0, 0)),
            pl.BlockSpec((aux, span), lambda i: (0, piece * (size // span) + i)),
            *(block for _ in added),
            *unused(before),
        ],
        out_specs=block,
        out_shape=jax.ShapeDtypeStruct((aux, size), BF),
        scratch_shapes=[pltpu.VMEM((SPAN, SPAN), BF)],
        compiler_params=params(),
        cost_estimate=cost(2 * aux * size * SPAN, 2 * (2 + len(added)) * aux * size),
        name="vir",
    )(live, mat, y, *added, *before)


def product_kernel(x_ref, *rest, pieces, steps, started, turn):
    z_refs = rest[:pieces]
    out_ref, acc_ref = rest[-2:]
    step = pl.program_id(0)
    for i, z_ref in enumerate(z_refs):
        for first in (True, False) if i == 0 else (False,):

            @pl.when(step == 0 if first else jnp.logical_and(step > 0, step // steps == i))
            def _(z_ref=z_ref, first=first):
                got = dot(z_ref[...], x_ref[...])
                if not first:
                    got = acc_ref[...] + got
                elif started:
                    got = rest[pieces][...] + got
                acc_ref[...] = got

    @pl.when(step == pl.num_programs(0) - 1)
    def _():
        out_ref[...] = acc_ref[...].T if turn else acc_ref[...]


def product(zs, x, at=0, so_far=None, turn=True, before=()):
    aux, size = zs[0].shape
    width = x.shape[1]
    span = next(n * SPAN for n in (8, 4, 1) if size % (n * SPAN) == 0)
    steps = size // span
    piece = lambda k: pl.BlockSpec((aux, span), lambda i: (0, jnp.clip(i - k * steps, 0, steps - 1)))
    added = [] if so_far is None else [so_far]
    shape = (width, aux) if turn else (aux, width)
    return pl.pallas_call(
        lambda *refs: product_kernel(*refs, pieces=len(zs), steps=steps, started=bool(added), turn=turn),
        grid=(len(zs) * steps,),
        in_specs=[
            pl.BlockSpec((span, width), lambda i: (at // span + i, 0)),
            *(piece(k) for k in range(len(zs))),
            *[pl.BlockSpec((aux, width), lambda i: (0, 0))] * len(added),
            *unused(before),
        ],
        out_specs=pl.BlockSpec(shape, lambda i: (0, 0)),
        out_shape=jax.ShapeDtypeStruct(shape, F32),
        scratch_shapes=[pltpu.VMEM((aux, width), F32)],
        compiler_params=params(),
        cost_estimate=cost(2 * aux * size * width, 2 * size * (aux + width)),
        name="product",
    )(x, *zs, *added, *before)


def scattered(parts, axis, direct):
    size = lax.axis_size(axis)
    blocks = [part.reshape(size, part.shape[0] // size, part.shape[1]) for part in parts]
    blocks = jnp.concatenate(blocks, axis=1) if len(blocks) > 1 else blocks[0]
    if size & (size - 1):
        return lax.psum_scatter(blocks.astype(BF), axis, scatter_dimension=0).astype(F32)
    me = lax.axis_index(axis)
    reaches = [1 << i for i in range(size.bit_length() - 1)]
    if direct and size <= 4:
        total = lax.dynamic_index_in_dim(blocks, me, 0, keepdims=False)
        for reach in range(1, size):
            given = lax.dynamic_index_in_dim(blocks, me ^ reach, 0, keepdims=False).astype(BF)
            total = total + lax.ppermute(given, axis, [(i, i ^ reach) for i in range(size)]).astype(F32)
        return total
    for reach in reaches:
        bit = (me // reach) % 2
        pairs = blocks.reshape(blocks.shape[0] // 2, 2, *blocks.shape[1:])
        kept = lax.dynamic_index_in_dim(pairs, bit, 1, keepdims=False)
        given = lax.dynamic_index_in_dim(pairs, 1 - bit, 1, keepdims=False).astype(BF)
        got = lax.ppermute(given, axis, [(i, i ^ reach) for i in range(size)])
        blocks = kept + got.astype(F32)
    return blocks[0]


def chunks_of(aux, owners):
    each = aux // owners
    parts = [n // owners for n in CHUNKS]
    if aux == sum(CHUNKS) and all(n % (16 * owners) == 0 for n in CHUNKS):
        cuts = [sum(parts[:i]) for i in range(len(parts) + 1)]
        return [[(j * each + a, b - a) for j in range(owners)] for a, b in zip(cuts, cuts[1:])]
    return [[(0, aux)]]


def body(three_centre, green_occ, green_vir, pair_live):
    rows, cols = lax.axis_size("row"), lax.axis_size("col")
    y = three_centre[0, 0]
    aux, size = y.shape
    live = pair_live[0]
    up_row = [(i, i - 1) for i in range(1, rows)]
    up_col = [(i, i - 1) for i in range(1, cols)]

    *wide, final = chunks_of(aux, cols)
    send = lambda half: lax.ppermute(half, "row", up_row)
    above = []
    last = ()
    for part in wide[:1]:
        last = occ(live, green_occ[0], 1, y, part)
        above.append(send(last[0]))
    shifted = []
    for i in range(PIECES):
        last = [vir(live, green_vir[0, 1].T, y, i, before=last)]
        shifted.append(lax.ppermute(last[0], "col", up_col))
    for part in wide[1:]:
        last = occ(live, green_occ[0], 1, y, part, before=last)
        above.append(send(last[0]))
    last = occ(live, green_occ[0], 1, y, final, before=last, cuts=PIECES)
    ending = [send(half) for half in last]
    spans = [(i, min(SPAN, aux - i)) for i in range(0, aux, SPAN)]
    (own,) = last = occ(live, green_occ[0], 0, y, spans, before=last[:1])
    zs = []
    diag = None
    for i in range(PIECES):
        zs.append(vir(live, green_vir[0, 0].T, y, i, (shifted[i],), before=last))
        diag = product(zs[-1:], own, i * (size // PIECES), diag, i == PIECES - 1)
        last = [diag]
    last = chi_d = scattered([diag], "col", True)
    blocks = []
    for half in above:
        last = scattered([product(zs, half, before=[last])], "col", True)
        blocks.append(last)
    ended = None
    for i, half in enumerate(ending):
        ended = product(zs[i : i + 1], half, 0, ended, i == PIECES - 1, before=[last])
    blocks.append(scattered([ended], "col", False))
    return chi_d[None], jnp.concatenate(blocks)[None]


def solution(mesh):
    return jax.shard_map(
        body,
        mesh=mesh,
        in_specs=(
            P("row", "col", None, None),
            P("row", None, None, None),
            P("col", None, None, None),
            P("row", "col"),
        ),
        out_specs=(P("row", "col", None), P("row", "col", None)),
        check_vma=False,
    )
```

```python
import jax
import jax.numpy as jnp
from jax import lax
from jax.experimental import pallas as pl
from jax.experimental.pallas import tpu as pltpu
from jax.sharding import PartitionSpec as P

BF = jnp.bfloat16
F32 = jnp.float32
VMEM_BYTES = 48 * 1024 * 1024
SPAN = 256
SUBLANES = 8
CHUNKS = (384, 256)
PIECES = 2
IN_STEPS = 4


def dot(a, b, dims=((1,), (0,))):
    return lax.dot_general(a, b, (dims, ((), ())), preferred_element_type=F32)


def iota(shape, axis):
    return lax.broadcasted_iota(jnp.int32, shape, axis)


def spread(g, group):
    m, k = g.shape
    pick_row = (iota((m * group, 1), 0) // group == iota((1, m), 1)).astype(BF)
    pick_col = (iota((k, 1), 0) == iota((1, k * group), 1) // group).astype(BF)
    full = dot(dot(pick_row, g).astype(BF), pick_col)
    same = iota((m * group, 1), 0) % group == iota((1, k * group), 1) % group
    return jnp.where(same, full, 0.0).astype(BF)


def repeated(g, count):
    t = g.shape[0]
    n = t * count
    pick = (iota((n, 1), 0) % t == iota((1, t), 1)).astype(BF)
    full = dot(dot(pick, g).astype(BF), pick, ((1,), (1,)))
    same = iota((n, 1), 0) // t == iota((1, n), 1) // t
    return jnp.where(same, full, 0.0).astype(BF)


def params():
    return pltpu.CompilerParams(vmem_limit_bytes=VMEM_BYTES)


def cost(flops, size):
    return pl.CostEstimate(flops=1, bytes_accessed=1, transcendentals=0)


def unused(before):
    return [pl.BlockSpec(memory_space=pl.ANY)] * len(before)


def occ_group(kron, yt_ref, held_ref, part_of, lanes, size):
    m, tile, _ = held_ref.shape
    width = lanes.stop - lanes.start
    per = SPAN // tile
    for j in range(size // SPAN):
        turned = part_of(slice(j * SPAN, (j + 1) * SPAN)).T
        yt_ref[j * per : (j + 1) * per, :, :width] = turned.reshape(per, tile, width)
    pair = 2 * SUBLANES
    for s in range(tile // pair):
        part = yt_ref[:, s * pair : (s + 1) * pair, :width].astype(F32)
        low, high = (
            part[:, i : i + SUBLANES].reshape(tile * SUBLANES, width).astype(BF) for i in (0, SUBLANES)
        )
        low, high = (dot(kron, x).reshape(m, SUBLANES, width) for x in (low, high))
        held_ref[:, s * pair : (s + 1) * pair, lanes] = jnp.concatenate([low, high], axis=1).astype(BF)


def occ_kernel(live_ref, g_ref, y_ref, *rest, groups, which, cuts):
    rows_ref, yt_ref, held_ref, in_sems, out_sems = rest[-5:]
    out_refs = rest[-5 - cuts : -5]
    m = g_ref.shape[2]
    size = y_ref.shape[1]
    fetch = []
    to = 0
    for slices, _ in groups:
        for start, count in slices:
            fetch.append(
                pltpu.make_async_copy(
                    y_ref.at[pl.ds(start, count)], rows_ref.at[pl.ds(to, count)], in_sems.at[len(fetch)]
                )
            )
            to += count
    for copy in fetch:
        copy.start()
    kron = spread(g_ref[which].T, SUBLANES)
    live = live_ref[0].astype(F32).astype(BF)
    store = []
    at, done = 0, 0
    for k, (slices, width) in enumerate(groups):
        for copy in fetch[done : done + len(slices)]:
            copy.wait()
        done += len(slices)
        lanes = slice(at, at + width)
        occ_group(kron, yt_ref.at[k], held_ref, lambda span: rows_ref[lanes, span] * live, lanes, size)
        for c, out_ref in enumerate(out_refs):
            some = pl.ds(c * (m // cuts), m // cuts)
            store.append(
                pltpu.make_async_copy(
                    held_ref.at[some, :, pl.ds(at, width)], out_ref.at[:, :, pl.ds(at, width)], out_sems.at[k, c]
                )
            )
            store[-1].start()
        at += width
    for copy in store:
        copy.wait()


def raw_kernel(live_ref, g_ref, y_ref, out_ref, rows_ref, tile_ref, tail_ref, in_sems, out_sems, *, slices):
    count, size = rows_ref.shape
    tile = tile_ref.shape[0]
    tail, wide = tail_ref.shape
    blocks = size // wide
    fetch = []
    to = 0
    for i, (start, n) in enumerate(slices):
        fetch.append(pltpu.make_async_copy(y_ref.at[pl.ds(start, n)], rows_ref.at[pl.ds(to, n)], in_sems.at[i]))
        to += n
    for copy in fetch:
        copy.start()
    fetch_tile = pltpu.make_async_copy(g_ref.at[1], tile_ref, in_sems.at[len(slices)])
    fetch_tile.start()
    live = live_ref[0].astype(F32).astype(BF)
    store = []
    to = 0
    for k, (_, n) in enumerate(slices):
        fetch[k].wait()
        rows_ref[to : to + n] = rows_ref[to : to + n] * live
        for i in range(blocks):
            store.append(
                pltpu.make_async_copy(
                    rows_ref.at[pl.ds(to, n), pl.ds(i * wide, wide)],
                    out_ref.at[pl.ds(i * count + to, n)],
                    out_sems.at[k * blocks + i],
                )
            )
            store[-1].start()
        to += n
    fetch_tile.wait()
    tail_ref[...] = jnp.zeros((tail, wide), BF)
    for i in range(tile // tail):
        tail_ref[:, i * 128 : i * 128 + tile] = tile_ref[i * tail : (i + 1) * tail]
    store.append(
        pltpu.make_async_copy(tail_ref, out_ref.at[pl.ds(count * blocks, tail)], out_sems.at[len(slices) * blocks])
    )
    store[-1].start()
    for copy in store:
        copy.wait()


RAW_TAIL = 16


def raw_shape(count, size, tile):
    wide = 128 * (tile // RAW_TAIL)
    return count * (size // wide) + RAW_TAIL, wide


def raw(live, mats, y, slices):
    count = sum(n for _, n in slices)
    size = y.shape[1]
    tile = mats.shape[1]
    shape = raw_shape(count, size, tile)
    some = pl.BlockSpec(memory_space=pl.ANY)
    return pl.pallas_call(
        lambda *refs: raw_kernel(*refs, slices=slices),
        in_specs=[pl.BlockSpec(memory_space=pltpu.SMEM), some, some],
        out_specs=some,
        out_shape=jax.ShapeDtypeStruct(shape, BF),
        scratch_shapes=[
            pltpu.VMEM((count, size), BF),
            pltpu.VMEM((tile, tile), BF),
            pltpu.VMEM((RAW_TAIL, shape[1]), BF),
            pltpu.SemaphoreType.DMA((len(slices) + 1,)),
            pltpu.SemaphoreType.DMA((len(slices) * (size // shape[1]) + 1,)),
        ],
        compiler_params=params(),
        cost_estimate=cost(count * size, 4 * count * size),
        name="raw",
    )(live, mats, y)


def raw_product_kernel(r_ref, *rest):
    z_refs = rest[:PIECES]
    out_ref, g_ref, yt_ref, held_ref, z_held, rows_ref, tail_ref, sems = rest[-8:]
    tile, _, count = yt_ref.shape
    size = tile * tile
    wide = r_ref.shape[1]
    blocks = size // wide
    part = size // PIECES
    fetch_tail = pltpu.make_async_copy(r_ref.at[pl.ds(blocks * count, RAW_TAIL)], tail_ref, sems.at[PIECES])
    fetch_tail.start()
    fetch_rows = [
        pltpu.make_async_copy(r_ref.at[pl.ds(i * count, count)], rows_ref.at[i], sems.at[PIECES + 1 + i])
        for i in range(blocks)
    ]
    fetch = [pltpu.make_async_copy(z_refs[i], z_held.at[i], sems.at[i]) for i in range(PIECES)]
    for copy in fetch_rows + fetch:
        copy.start()
    fetch_tail.wait()
    for i in range(tile // RAW_TAIL):
        g_ref[i * RAW_TAIL : (i + 1) * RAW_TAIL] = tail_ref[:, i * 128 : i * 128 + tile]
    kron = spread(g_ref[...].T, SUBLANES)

    def part_of(span):
        block, at = divmod(span.start, wide)
        if at == 0:
            fetch_rows[block].wait()
        return rows_ref[block, :, at : at + SPAN]

    occ_group(kron, yt_ref, held_ref, part_of, slice(0, count), size)
    total = None
    for i in range(PIECES):
        fetch[i].wait()
        rows = slice(i * (tile // PIECES), (i + 1) * (tile // PIECES))
        got = dot(z_held[i], held_ref[rows].reshape(part, count))
        total = got if total is None else total + got
    out_ref[...] = total.T


def raw_product(received, zs, tile, before=()):
    size = tile * tile
    count = (received.shape[0] - RAW_TAIL) * received.shape[1] // size
    aux = zs[0].shape[0]
    return pl.pallas_call(
        raw_product_kernel,
        in_specs=[
            *[pl.BlockSpec(memory_space=pl.ANY)] * (1 + len(zs)),
            *unused(before),
        ],
        out_specs=pl.BlockSpec(memory_space=pltpu.VMEM),
        out_shape=jax.ShapeDtypeStruct((count, aux), F32),
        scratch_shapes=[
            pltpu.VMEM((tile, tile), BF),
            pltpu.VMEM((tile, tile, count), BF),
            pltpu.VMEM((tile, tile, count), BF),
            pltpu.VMEM((PIECES, aux, size // PIECES), BF),
            pltpu.VMEM((size // received.shape[1], count, received.shape[1]), BF),
            pltpu.VMEM((RAW_TAIL, received.shape[1]), BF),
            pltpu.SemaphoreType.DMA((PIECES + 1 + size // received.shape[1],)),
        ],
        compiler_params=params(),
        cost_estimate=cost(2 * count * size * (tile * SUBLANES + aux), 2 * size * (aux + count)),
        name="raw_product",
    )(received, *zs, *before)


def grouped(slices):
    groups, held = [], []
    for start, count in slices:
        held.append((start, count))
        width = sum(n for _, n in held)
        if width >= SPAN and width % 128 == 0:
            groups.append((held, width))
            held = []
    if held:
        groups.append((held, sum(n for _, n in held)))
    return groups


def occ(live, mats, which, y, slices, before=(), cuts=1):
    tile, m = mats.shape[1:]
    size = y.shape[1]
    groups = grouped(slices)
    width = sum(n for _, n in groups)
    widest = max(n for _, n in groups)
    outs = pl.pallas_call(
        lambda *refs: occ_kernel(*refs, groups=groups, which=which, cuts=cuts),
        in_specs=[
            pl.BlockSpec(memory_space=pltpu.SMEM),
            pl.BlockSpec(memory_space=pltpu.VMEM),
            pl.BlockSpec(memory_space=pl.ANY),
            *unused(before),
        ],
        out_specs=[pl.BlockSpec(memory_space=pl.ANY)] * cuts,
        out_shape=[jax.ShapeDtypeStruct((m // cuts, tile, width), BF)] * cuts,
        scratch_shapes=[
            pltpu.VMEM((width, size), BF),
            pltpu.VMEM((len(groups), tile, tile, widest), BF),
            pltpu.VMEM((m, tile, width), BF),
            pltpu.SemaphoreType.DMA((len(slices),)),
            pltpu.SemaphoreType.DMA((len(groups), cuts)),
        ],
        compiler_params=params(),
        cost_estimate=cost(2 * width * size * m * SUBLANES, 4 * width * size),
        name="occ",
    )(live, mats, y, *before)
    return outs[0].reshape(-1, width)


def both_kernel(live_ref, go_ref, gv_ref, y_ref, *rest, slices):
    rows_ref, yt_ref, half_ref, over_ref, in_sems, out_sems = rest[-6:]
    outs = rest[-6 - 2 * PIECES : -6]
    half_outs, over_outs = outs[:PIECES], outs[PIECES:]
    aux, size = y_ref.shape
    step = aux // IN_STEPS
    fetch = []
    for i in range(IN_STEPS):
        at = pl.ds(i * step, step)
        fetch.append(pltpu.make_async_copy(y_ref.at[at], rows_ref.at[at], in_sems.at[i]))
    for copy in fetch:
        copy.start()
    scale = live_ref[0].astype(F32)
    live = scale.astype(BF)
    occ_kron = spread(go_ref[1].T, SUBLANES)
    vir_kron = (repeated(gv_ref[1].T, SPAN // gv_ref.shape[1]).astype(F32) * scale).astype(BF)
    for copy in fetch:
        copy.wait()
    store = []
    for c, out in enumerate(over_outs):
        wide = size // PIECES
        for j in range(wide // SPAN):
            at = c * wide + j * SPAN
            over_ref[c, :, j * SPAN : (j + 1) * SPAN] = dot(rows_ref[:, at : at + SPAN], vir_kron).astype(BF)
        store.append(pltpu.make_async_copy(over_ref.at[c], out, out_sems.at[PIECES + c]))
        store[-1].start()

    def part_of(span):
        parts = [rows_ref[start : start + count, span] for start, count in slices]
        return (jnp.concatenate(parts, axis=0) if len(parts) > 1 else parts[0]) * live

    occ_group(occ_kron, yt_ref, half_ref, part_of, slice(0, yt_ref.shape[2]), size)
    some = half_ref.shape[0] // PIECES
    for c, out in enumerate(half_outs):
        store.append(pltpu.make_async_copy(half_ref.at[pl.ds(c * some, some)], out, out_sems.at[c]))
        store[-1].start()
    for copy in store:
        copy.wait()


def both(live, green_occ, green_vir, y, slices, before=()):
    aux, size = y.shape
    tile = green_occ.shape[1]
    width = sum(count for _, count in slices)
    whole = pl.BlockSpec(memory_space=pltpu.VMEM)
    some = pl.BlockSpec(memory_space=pl.ANY)
    outs = pl.pallas_call(
        lambda *refs: both_kernel(*refs, slices=slices),
        in_specs=[pl.BlockSpec(memory_space=pltpu.SMEM), whole, whole, some, *unused(before)],
        out_specs=[some] * (2 * PIECES),
        out_shape=[jax.ShapeDtypeStruct((tile // PIECES, tile, width), BF)] * PIECES
        + [jax.ShapeDtypeStruct((aux, size // PIECES), BF)] * PIECES,
        scratch_shapes=[
            pltpu.VMEM((aux, size), BF),
            pltpu.VMEM((tile, tile, width), BF),
            pltpu.VMEM((tile, tile, width), BF),
            pltpu.VMEM((PIECES, aux, size // PIECES), BF),
            pltpu.SemaphoreType.DMA((IN_STEPS,)),
            pltpu.SemaphoreType.DMA((2 * PIECES,)),
        ],
        compiler_params=params(),
        cost_estimate=cost(2 * width * size * tile * SUBLANES, 8 * aux * size),
        name="both_halves",
    )(live, green_occ, green_vir, y, *before)
    return [half.reshape(-1, width) for half in outs[:PIECES]], outs[PIECES:]


def fold_kernel(live_ref, g_ref, y_ref, shifted_ref, own_ref, *rest, started, turn):
    z_ref, out_ref, kron_ref, acc_ref = rest[-4:]
    step = pl.program_id(0)

    @pl.when(step == 0)
    def _():
        scale = live_ref[0].astype(F32)
        kron_ref[...] = (repeated(g_ref[0].T, SPAN // g_ref.shape[1]).astype(F32) * scale).astype(BF)
        acc_ref[...] = rest[0][...] if started else jnp.zeros(acc_ref.shape, F32)

    for j in range(y_ref.shape[1] // SPAN):
        at = slice(j * SPAN, (j + 1) * SPAN)
        z_ref[:, at] = (dot(y_ref[:, at], kron_ref[...]) + shifted_ref[:, at].astype(F32)).astype(BF)
    acc_ref[...] += dot(z_ref[...], own_ref[...])

    @pl.when(step == pl.num_programs(0) - 1)
    def _():
        out_ref[...] = acc_ref[...].T if turn else acc_ref[...]


def fold(live, mats, y, piece, shifted, own, so_far, turn, before=()):
    aux = y.shape[0]
    size = y.shape[1] // PIECES
    span = 4 * SPAN if size % (4 * SPAN) == 0 else SPAN
    steps = size // span
    block = pl.BlockSpec((aux, span), lambda i: (0, i))
    whole = pl.BlockSpec((aux, aux), lambda i: (0, 0))
    added = [] if so_far is None else [so_far]
    return pl.pallas_call(
        lambda *refs: fold_kernel(*refs, started=bool(added), turn=turn),
        grid=(steps,),
        in_specs=[
            pl.BlockSpec(memory_space=pltpu.SMEM),
            pl.BlockSpec(mats.shape, lambda i: (0, 0, 0)),
            pl.BlockSpec((aux, span), lambda i: (0, piece * steps + i)),
            block,
            pl.BlockSpec((span, aux), lambda i: (piece * steps + i, 0)),
            *[whole] * len(added),
            *unused(before),
        ],
        out_specs=[block, whole],
        out_shape=[jax.ShapeDtypeStruct((aux, size), BF), jax.ShapeDtypeStruct((aux, aux), F32)],
        scratch_shapes=[pltpu.VMEM((SPAN, SPAN), BF), pltpu.VMEM((aux, aux), F32)],
        compiler_params=params(),
        cost_estimate=cost(2 * aux * size * (SPAN + aux), 2 * 4 * aux * size),
        name="fold",
    )(live, mats, y, shifted, own, *added, *before)


def both_kernel(live_ref, go_ref, gv_ref, y_ref, *rest, slices):
    rows_ref, yt_ref, half_ref, over_ref, in_sems, out_sems = rest[-6:]
    outs = rest[-6 - 2 * PIECES : -6]
    half_outs, over_outs = outs[:PIECES], outs[PIECES:]
    aux, size = y_ref.shape
    step = aux // IN_STEPS
    fetch = []
    for i in range(IN_STEPS):
        at = pl.ds(i * step, step)
        fetch.append(pltpu.make_async_copy(y_ref.at[at], rows_ref.at[at], in_sems.at[i]))
    for copy in fetch:
        copy.start()
    scale = live_ref[0].astype(F32)
    live = scale.astype(BF)
    occ_kron = spread(go_ref[1].T, SUBLANES)
    vir_kron = (repeated(gv_ref[1].T, SPAN // gv_ref.shape[1]).astype(F32) * scale).astype(BF)
    for copy in fetch:
        copy.wait()
    store = []
    for c, out in enumerate(over_outs):
        wide = size // PIECES
        for j in range(wide // SPAN):
            at = c * wide + j * SPAN
            over_ref[c, :, j * SPAN : (j + 1) * SPAN] = dot(rows_ref[:, at : at + SPAN], vir_kron).astype(BF)
        store.append(pltpu.make_async_copy(over_ref.at[c], out, out_sems.at[PIECES + c]))
        store[-1].start()

    def part_of(span):
        parts = [rows_ref[start : start + count, span] for start, count in slices]
        return (jnp.concatenate(parts, axis=0) if len(parts) > 1 else parts[0]) * live

    occ_group(occ_kron, yt_ref, half_ref, part_of, slice(0, yt_ref.shape[2]), size)
    some = half_ref.shape[0] // PIECES
    for c, out in enumerate(half_outs):
        store.append(pltpu.make_async_copy(half_ref.at[pl.ds(c * some, some)], out, out_sems.at[c]))
        store[-1].start()
    for copy in store:
        copy.wait()


def both(live, green_occ, green_vir, y, slices, before=()):
    aux, size = y.shape
    tile = green_occ.shape[1]
    width = sum(count for _, count in slices)
    whole = pl.BlockSpec(memory_space=pltpu.VMEM)
    some = pl.BlockSpec(memory_space=pl.ANY)
    outs = pl.pallas_call(
        lambda *refs: both_kernel(*refs, slices=slices),
        in_specs=[pl.BlockSpec(memory_space=pltpu.SMEM), whole, whole, some, *unused(before)],
        out_specs=[some] * (2 * PIECES),
        out_shape=[jax.ShapeDtypeStruct((tile // PIECES, tile, width), BF)] * PIECES
        + [jax.ShapeDtypeStruct((aux, size // PIECES), BF)] * PIECES,
        scratch_shapes=[
            pltpu.VMEM((aux, size), BF),
            pltpu.VMEM((tile, tile, width), BF),
            pltpu.VMEM((tile, tile, width), BF),
            pltpu.VMEM((PIECES, aux, size // PIECES), BF),
            pltpu.SemaphoreType.DMA((IN_STEPS,)),
            pltpu.SemaphoreType.DMA((2 * PIECES,)),
        ],
        compiler_params=params(),
        cost_estimate=cost(2 * width * size * tile * SUBLANES, 8 * aux * size),
        name="both_halves",
    )(live, green_occ, green_vir, y, *before)
    return [half.reshape(-1, width) for half in outs[:PIECES]], outs[PIECES:]


def vir_kernel(live_ref, g_ref, y_ref, *rest, n_added):
    added = rest[:n_added]
    out_ref, kron_ref = rest[-2:]

    @pl.when(pl.program_id(0) == 0)
    def _():
        scale = live_ref[0].astype(F32)
        kron_ref[...] = (repeated(g_ref[...], SPAN // g_ref.shape[0]).astype(F32) * scale).astype(BF)

    for j in range(y_ref.shape[1] // SPAN):
        at = slice(j * SPAN, (j + 1) * SPAN)
        got = dot(y_ref[:, at], kron_ref[...])
        for ref in added:
            got = got + ref[:, at].astype(F32)
        out_ref[:, at] = got.astype(BF)


def vir(live, mat, y, piece, added=(), before=()):
    aux = y.shape[0]
    size = y.shape[1] // PIECES
    span = 4 * SPAN if size % (4 * SPAN) == 0 else SPAN
    block = pl.BlockSpec((aux, span), lambda i: (0, i))
    return pl.pallas_call(
        lambda *refs: vir_kernel(*refs, n_added=len(added)),
        grid=(size // span,),
        in_specs=[
            pl.BlockSpec(memory_space=pltpu.SMEM),
            pl.BlockSpec(mat.shape, lambda i: (0, 0)),
            pl.BlockSpec((aux, span), lambda i: (0, piece * (size // span) + i)),
            *(block for _ in added),
            *unused(before),
        ],
        out_specs=block,
        out_shape=jax.ShapeDtypeStruct((aux, size), BF),
        scratch_shapes=[pltpu.VMEM((SPAN, SPAN), BF)],
        compiler_params=params(),
        cost_estimate=cost(2 * aux * size * SPAN, 2 * (2 + len(added)) * aux * size),
        name="vir",
    )(live, mat, y, *added, *before)


def product_kernel(x_ref, *rest, pieces, steps, started, turn):
    z_refs = rest[:pieces]
    out_ref, acc_ref = rest[-2:]
    step = pl.program_id(0)
    for i, z_ref in enumerate(z_refs):
        for first in (True, False) if i == 0 else (False,):

            @pl.when(step == 0 if first else jnp.logical_and(step > 0, step // steps == i))
            def _(z_ref=z_ref, first=first):
                got = dot(z_ref[...], x_ref[...])
                if not first:
                    got = acc_ref[...] + got
                elif started:
                    got = rest[pieces][...] + got
                acc_ref[...] = got

    @pl.when(step == pl.num_programs(0) - 1)
    def _():
        out_ref[...] = acc_ref[...].T if turn else acc_ref[...]


def product(zs, x, at=0, so_far=None, turn=True, before=()):
    aux, size = zs[0].shape
    width = x.shape[1]
    span = next(n * SPAN for n in (8, 4, 1) if size % (n * SPAN) == 0)
    steps = size // span
    piece = lambda k: pl.BlockSpec((aux, span), lambda i: (0, jnp.clip(i - k * steps, 0, steps - 1)))
    added = [] if so_far is None else [so_far]
    shape = (width, aux) if turn else (aux, width)
    return pl.pallas_call(
        lambda *refs: product_kernel(*refs, pieces=len(zs), steps=steps, started=bool(added), turn=turn),
        grid=(len(zs) * steps,),
        in_specs=[
            pl.BlockSpec((span, width), lambda i: (at // span + i, 0)),
            *(piece(k) for k in range(len(zs))),
            *[pl.BlockSpec((aux, width), lambda i: (0, 0))] * len(added),
            *unused(before),
        ],
        out_specs=pl.BlockSpec(shape, lambda i: (0, 0)),
        out_shape=jax.ShapeDtypeStruct(shape, F32),
        scratch_shapes=[pltpu.VMEM((aux, width), F32)],
        compiler_params=params(),
        cost_estimate=cost(2 * aux * size * width, 2 * size * (aux + width)),
        name="product",
    )(x, *zs, *added, *before)


def scattered(parts, axis, direct):
    size = lax.axis_size(axis)
    blocks = [part.reshape(size, part.shape[0] // size, part.shape[1]) for part in parts]
    blocks = jnp.concatenate(blocks, axis=1) if len(blocks) > 1 else blocks[0]
    if size & (size - 1):
        return lax.psum_scatter(blocks.astype(BF), axis, scatter_dimension=0).astype(F32)
    me = lax.axis_index(axis)
    reaches = [1 << i for i in range(size.bit_length() - 1)]
    if direct and size <= 4:
        total = lax.dynamic_index_in_dim(blocks, me, 0, keepdims=False)
        for reach in range(1, size):
            given = lax.dynamic_index_in_dim(blocks, me ^ reach, 0, keepdims=False).astype(BF)
            total = total + lax.ppermute(given, axis, [(i, i ^ reach) for i in range(size)]).astype(F32)
        return total
    for reach in reaches:
        bit = (me // reach) % 2
        pairs = blocks.reshape(blocks.shape[0] // 2, 2, *blocks.shape[1:])
        kept = lax.dynamic_index_in_dim(pairs, bit, 1, keepdims=False)
        given = lax.dynamic_index_in_dim(pairs, 1 - bit, 1, keepdims=False).astype(BF)
        got = lax.ppermute(given, axis, [(i, i ^ reach) for i in range(size)])
        blocks = kept + got.astype(F32)
    return blocks[0]


def chunks_of(aux, owners):
    each = aux // owners
    parts = [n // owners for n in CHUNKS]
    if aux == sum(CHUNKS) and all(n % (16 * owners) == 0 for n in CHUNKS):
        cuts = [sum(parts[:i]) for i in range(len(parts) + 1)]
        return [[(j * each + a, b - a) for j in range(owners)] for a, b in zip(cuts, cuts[1:])]
    return [[(0, aux)]]


def body(three_centre, green_occ, green_vir, pair_live):
    rows, cols = lax.axis_size("row"), lax.axis_size("col")
    y = three_centre[0, 0]
    aux, size = y.shape
    live = pair_live[0]
    up_row = [(i, i - 1) for i in range(1, rows)]
    up_col = [(i, i - 1) for i in range(1, cols)]

    send = lambda half: lax.ppermute(half, "row", up_row)
    chunks = chunks_of(aux, cols)
    chunked = len(chunks) > 1
    last = ()
    if chunked:
        last = [raw(live, green_occ[0], y, chunks[0])]
        unfolded = send(last[0])
    halves, over = both(live, green_occ[0], green_vir[0], y, chunks[-1], last)
    shifted = [lax.ppermute(piece, "col", up_col) for piece in over]
    ending = [send(half) for half in halves]
    spans = [(i, min(SPAN, aux - i)) for i in range(0, aux, SPAN)]
    own = occ(live, green_occ[0], 0, y, spans, before=halves[:1])
    zs = []
    diag = None
    for i in range(PIECES):
        z, diag = fold(live, green_vir[0], y, i, shifted[i], own, diag, i == PIECES - 1)
        zs.append(z)
    blocks, order = [], [[diag]] * PIECES
    if chunked:
        early = raw_product(unfolded, zs, green_occ.shape[2], before=[diag])
        both_done = scattered([diag, early], "col", True)
        chi_d, blocks = both_done[: aux // cols], [both_done[aux // cols :]]
        order = [[early]] * (PIECES - 1) + [[both_done]]
    else:
        chi_d = scattered([diag], "col", True)
    ended = None
    for i, half in enumerate(ending):
        ended = product(zs[i : i + 1], half, 0, ended, i == PIECES - 1, before=order[i])
    blocks.append(scattered([ended], "col", False))
    return chi_d[None], jnp.concatenate(blocks)[None]


def solution(mesh):
    return jax.shard_map(
        body,
        mesh=mesh,
        in_specs=(
            P("row", "col", None, None),
            P("row", None, None, None),
            P("col", None, None, None),
            P("row", "col"),
        ),
        out_specs=(P("row", "col", None), P("row", "col", None)),
        check_vma=False,
    )
```

```python
import jax
import jax.numpy as jnp
from jax import lax
from jax.experimental import pallas as pl
from jax.experimental.pallas import tpu as pltpu
from jax.sharding import PartitionSpec as P

BF = jnp.bfloat16
F32 = jnp.float32
VMEM_BYTES = 48 * 1024 * 1024
SPAN = 256
SUBLANES = 8
CHUNKS = (384, 256)
PIECES = 2
IN_STEPS = 4
CUTS = (3, 1)


def dot(a, b, dims=((1,), (0,))):
    return lax.dot_general(a, b, (dims, ((), ())), preferred_element_type=F32)


def iota(shape, axis):
    return lax.broadcasted_iota(jnp.int32, shape, axis)


def spread(g, group):
    m, k = g.shape
    pick_row = (iota((m * group, 1), 0) // group == iota((1, m), 1)).astype(BF)
    pick_col = (iota((k, 1), 0) == iota((1, k * group), 1) // group).astype(BF)
    full = dot(dot(pick_row, g).astype(BF), pick_col)
    same = iota((m * group, 1), 0) % group == iota((1, k * group), 1) % group
    return jnp.where(same, full, 0.0).astype(BF)


def repeated(g, count):
    t = g.shape[0]
    n = t * count
    pick = (iota((n, 1), 0) % t == iota((1, t), 1)).astype(BF)
    full = dot(dot(pick, g).astype(BF), pick, ((1,), (1,)))
    same = iota((n, 1), 0) // t == iota((1, n), 1) // t
    return jnp.where(same, full, 0.0).astype(BF)


def params():
    return pltpu.CompilerParams(vmem_limit_bytes=VMEM_BYTES)


def cost(flops, size):
    return pl.CostEstimate(flops=1, bytes_accessed=1, transcendentals=0)


def unused(before):
    return [pl.BlockSpec(memory_space=pl.ANY)] * len(before)


def occ_group(kron, yt_ref, held_ref, part_of, lanes, size):
    m, tile, _ = held_ref.shape
    width = lanes.stop - lanes.start
    per = SPAN // tile
    for j in range(size // SPAN):
        turned = part_of(slice(j * SPAN, (j + 1) * SPAN)).T
        yt_ref[j * per : (j + 1) * per, :, :width] = turned.reshape(per, tile, width)
    pair = 2 * SUBLANES
    for s in range(tile // pair):
        part = yt_ref[:, s * pair : (s + 1) * pair, :width].astype(F32)
        low, high = (
            part[:, i : i + SUBLANES].reshape(tile * SUBLANES, width).astype(BF) for i in (0, SUBLANES)
        )
        low, high = (dot(kron, x).reshape(m, SUBLANES, width) for x in (low, high))
        held_ref[:, s * pair : (s + 1) * pair, lanes] = jnp.concatenate([low, high], axis=1).astype(BF)


def occ_kernel(live_ref, g_ref, y_ref, *rest, groups, which, cuts):
    rows_ref, yt_ref, held_ref, in_sems, out_sems = rest[-5:]
    out_refs = rest[-5 - cuts : -5]
    m = g_ref.shape[2]
    size = y_ref.shape[1]
    fetch = []
    to = 0
    for slices, _ in groups:
        for start, count in slices:
            fetch.append(
                pltpu.make_async_copy(
                    y_ref.at[pl.ds(start, count)], rows_ref.at[pl.ds(to, count)], in_sems.at[len(fetch)]
                )
            )
            to += count
    for copy in fetch:
        copy.start()
    kron = spread(g_ref[which].T, SUBLANES)
    live = live_ref[0].astype(F32).astype(BF)
    store = []
    at, done = 0, 0
    for k, (slices, width) in enumerate(groups):
        for copy in fetch[done : done + len(slices)]:
            copy.wait()
        done += len(slices)
        lanes = slice(at, at + width)
        occ_group(kron, yt_ref.at[k], held_ref, lambda span: rows_ref[lanes, span] * live, lanes, size)
        for c, out_ref in enumerate(out_refs):
            some = pl.ds(c * (m // cuts), m // cuts)
            store.append(
                pltpu.make_async_copy(
                    held_ref.at[some, :, pl.ds(at, width)], out_ref.at[:, :, pl.ds(at, width)], out_sems.at[k, c]
                )
            )
            store[-1].start()
        at += width
    for copy in store:
        copy.wait()


def raw_kernel(live_ref, g_ref, y_ref, out_ref, rows_ref, tile_ref, tail_ref, tile_sem, in_sems, out_sems, *, slices):
    count, size = rows_ref.shape
    tile = tile_ref.shape[0]
    tail, wide = tail_ref.shape
    blocks = size // wide
    fetch_tile = pltpu.make_async_copy(g_ref.at[1], tile_ref, tile_sem)
    fetch_tile.start()
    fetch = []
    to = 0
    for i, (start, n) in enumerate(slices):
        fetch.append(pltpu.make_async_copy(y_ref.at[pl.ds(start, n)], rows_ref.at[pl.ds(to, n)], in_sems.at[i]))
        fetch[-1].start()
        to += n
    fetch_tile.wait()
    live = live_ref[0].astype(F32).astype(BF)
    tail_ref[...] = jnp.zeros((tail, wide), BF)
    for i in range(tile // tail):
        tail_ref[:, i * 128 : i * 128 + tile] = tile_ref[i * tail : (i + 1) * tail] * live
    store = [pltpu.make_async_copy(tail_ref, out_ref.at[pl.ds(count * blocks, tail)], out_sems.at[0])]
    store[0].start()
    to = 0
    for k, (_, n) in enumerate(slices):
        fetch[k].wait()
        for i in range(blocks):
            store.append(
                pltpu.make_async_copy(
                    rows_ref.at[pl.ds(to, n), pl.ds(i * wide, wide)],
                    out_ref.at[pl.ds(i * count + to, n)],
                    out_sems.at[len(store)],
                )
            )
            store[-1].start()
        to += n
    for copy in store:
        copy.wait()


RAW_TAIL = 16


def raw_shape(count, size, tile):
    wide = 128 * (tile // RAW_TAIL)
    return count * (size // wide) + RAW_TAIL, wide


def raw(live, mats, y, slices):
    count = sum(n for _, n in slices)
    size = y.shape[1]
    tile = mats.shape[1]
    shape = raw_shape(count, size, tile)
    some = pl.BlockSpec(memory_space=pltpu.HBM)
    return pl.pallas_call(
        lambda *refs: raw_kernel(*refs, slices=slices),
        in_specs=[pl.BlockSpec(memory_space=pltpu.SMEM), some, some],
        out_specs=some,
        out_shape=jax.ShapeDtypeStruct(shape, BF),
        scratch_shapes=[
            pltpu.VMEM((count, size), BF),
            pltpu.VMEM((tile, tile), BF),
            pltpu.VMEM((RAW_TAIL, shape[1]), BF),
            pltpu.SemaphoreType.DMA(()),
            pltpu.SemaphoreType.DMA((len(slices),)),
            pltpu.SemaphoreType.DMA((len(slices) * (size // shape[1]) + 1,)),
        ],
        compiler_params=params(),
        cost_estimate=cost(count * size, 4 * count * size),
        name="raw",
    )(live, mats, y)


def raw_product_kernel(r_ref, *rest):
    z_refs = rest[:PIECES]
    out_ref, g_ref, yt_ref, held_ref, z_held, rows_ref, tail_ref, sems = rest[-8:]
    tile, _, count = yt_ref.shape
    size = tile * tile
    wide = r_ref.shape[1]
    blocks = size // wide
    part = size // PIECES
    fetch_tail = pltpu.make_async_copy(r_ref.at[pl.ds(blocks * count, RAW_TAIL)], tail_ref, sems.at[PIECES])
    fetch_tail.start()
    fetch_rows = [
        pltpu.make_async_copy(r_ref.at[pl.ds(i * count, count)], rows_ref.at[i], sems.at[PIECES + 1 + i])
        for i in range(blocks)
    ]
    fetch = [pltpu.make_async_copy(z_refs[i], z_held.at[i], sems.at[i]) for i in range(PIECES)]
    for copy in fetch_rows + fetch:
        copy.start()
    fetch_tail.wait()
    for i in range(tile // RAW_TAIL):
        g_ref[i * RAW_TAIL : (i + 1) * RAW_TAIL] = tail_ref[:, i * 128 : i * 128 + tile]
    kron = spread(g_ref[...].T, SUBLANES)

    def part_of(span):
        block, at = divmod(span.start, wide)
        if at == 0:
            fetch_rows[block].wait()
        return rows_ref[block, :, at : at + SPAN]

    occ_group(kron, yt_ref, held_ref, part_of, slice(0, count), size)
    total = None
    for i in range(PIECES):
        fetch[i].wait()
        rows = slice(i * (tile // PIECES), (i + 1) * (tile // PIECES))
        got = dot(z_held[i], held_ref[rows].reshape(part, count))
        total = got if total is None else total + got
    out_ref[...] = total.T


def raw_product(received, zs, tile, before=()):
    size = tile * tile
    count = (received.shape[0] - RAW_TAIL) * received.shape[1] // size
    aux = zs[0].shape[0]
    return pl.pallas_call(
        raw_product_kernel,
        in_specs=[
            *[pl.BlockSpec(memory_space=pl.ANY)] * (1 + len(zs)),
            *unused(before),
        ],
        out_specs=pl.BlockSpec(memory_space=pltpu.VMEM),
        out_shape=jax.ShapeDtypeStruct((count, aux), F32),
        scratch_shapes=[
            pltpu.VMEM((tile, tile), BF),
            pltpu.VMEM((tile, tile, count), BF),
            pltpu.VMEM((tile, tile, count), BF),
            pltpu.VMEM((PIECES, aux, size // PIECES), BF),
            pltpu.VMEM((size // received.shape[1], count, received.shape[1]), BF),
            pltpu.VMEM((RAW_TAIL, received.shape[1]), BF),
            pltpu.SemaphoreType.DMA((PIECES + 1 + size // received.shape[1],)),
        ],
        compiler_params=params(),
        cost_estimate=cost(2 * count * size * (tile * SUBLANES + aux), 2 * size * (aux + count)),
        name="raw_product",
    )(received, *zs, *before)


def grouped(slices):
    groups, held = [], []
    for start, count in slices:
        held.append((start, count))
        width = sum(n for _, n in held)
        if width >= SPAN and width % 128 == 0:
            groups.append((held, width))
            held = []
    if held:
        groups.append((held, sum(n for _, n in held)))
    return groups


def occ(live, mats, which, y, slices, before=(), cuts=1):
    tile, m = mats.shape[1:]
    size = y.shape[1]
    groups = grouped(slices)
    width = sum(n for _, n in groups)
    widest = max(n for _, n in groups)
    outs = pl.pallas_call(
        lambda *refs: occ_kernel(*refs, groups=groups, which=which, cuts=cuts),
        in_specs=[
            pl.BlockSpec(memory_space=pltpu.SMEM),
            pl.BlockSpec(memory_space=pltpu.VMEM),
            pl.BlockSpec(memory_space=pl.ANY),
            *unused(before),
        ],
        out_specs=[pl.BlockSpec(memory_space=pl.ANY)] * cuts,
        out_shape=[jax.ShapeDtypeStruct((m // cuts, tile, width), BF)] * cuts,
        scratch_shapes=[
            pltpu.VMEM((width, size), BF),
            pltpu.VMEM((len(groups), tile, tile, widest), BF),
            pltpu.VMEM((m, tile, width), BF),
            pltpu.SemaphoreType.DMA((len(slices),)),
            pltpu.SemaphoreType.DMA((len(groups), cuts)),
        ],
        compiler_params=params(),
        cost_estimate=cost(2 * width * size * m * SUBLANES, 4 * width * size),
        name="occ",
    )(live, mats, y, *before)
    return outs[0].reshape(-1, width)


def both_kernel(live_ref, go_ref, gv_ref, y_ref, *rest, slices):
    rows_ref, yt_ref, half_ref, over_ref, tiles_ref, in_sems, out_sems = rest[-7:]
    outs = rest[-7 - len(CUTS) - PIECES : -7]
    half_outs, over_outs = outs[: len(CUTS)], outs[len(CUTS) :]
    aux, size = y_ref.shape
    step = aux // IN_STEPS
    fetch = []
    for i in range(IN_STEPS):
        at = pl.ds(i * step, step)
        fetch.append(pltpu.make_async_copy(y_ref.at[at], rows_ref.at[at], in_sems.at[i]))
    for copy in fetch:
        copy.start()
    tiles = [pltpu.make_async_copy(g.at[1], tiles_ref.at[i], in_sems.at[IN_STEPS + i]) for i, g in enumerate((go_ref, gv_ref))]
    for copy in tiles:
        copy.start()
    scale = live_ref[0].astype(F32)
    live = scale.astype(BF)
    for copy in tiles:
        copy.wait()
    occ_kron = spread(tiles_ref[0].T, SUBLANES)
    vir_kron = (repeated(tiles_ref[1].T, SPAN // gv_ref.shape[1]).astype(F32) * scale).astype(BF)
    for copy in fetch:
        copy.wait()
    store = []
    for c, out in enumerate(over_outs):
        wide = size // PIECES
        for j in range(wide // SPAN):
            at = c * wide + j * SPAN
            over_ref[c, :, j * SPAN : (j + 1) * SPAN] = dot(rows_ref[:, at : at + SPAN], vir_kron).astype(BF)
        store.append(pltpu.make_async_copy(over_ref.at[c], out, out_sems.at[len(CUTS) + c]))
        store[-1].start()

    def part_of(span):
        parts = [rows_ref[start : start + count, span] for start, count in slices]
        return (jnp.concatenate(parts, axis=0) if len(parts) > 1 else parts[0]) * live

    occ_group(occ_kron, yt_ref, half_ref, part_of, slice(0, yt_ref.shape[2]), size)
    to = 0
    for c, out in enumerate(half_outs):
        store.append(pltpu.make_async_copy(half_ref.at[pl.ds(to, out.shape[0])], out, out_sems.at[c]))
        store[-1].start()
        to += out.shape[0]
    for copy in store:
        copy.wait()


def both(live, green_occ, green_vir, y, slices, before=()):
    aux, size = y.shape
    tile = green_occ.shape[1]
    width = sum(count for _, count in slices)
    some = pl.BlockSpec(memory_space=pl.ANY)
    fixed = pl.BlockSpec(memory_space=pltpu.HBM)
    parts = [tile * n // sum(CUTS) for n in CUTS]
    outs = pl.pallas_call(
        lambda *refs: both_kernel(*refs, slices=slices),
        in_specs=[pl.BlockSpec(memory_space=pltpu.SMEM), fixed, fixed, some, *unused(before)],
        out_specs=[some] * (len(CUTS) + PIECES),
        out_shape=[jax.ShapeDtypeStruct((n, tile, width), BF) for n in parts]
        + [jax.ShapeDtypeStruct((aux, size // PIECES), BF)] * PIECES,
        scratch_shapes=[
            pltpu.VMEM((aux, size), BF),
            pltpu.VMEM((tile, tile, width), BF),
            pltpu.VMEM((tile, tile, width), BF),
            pltpu.VMEM((PIECES, aux, size // PIECES), BF),
            pltpu.VMEM((2, tile, tile), BF),
            pltpu.SemaphoreType.DMA((IN_STEPS + 2,)),
            pltpu.SemaphoreType.DMA((len(CUTS) + PIECES,)),
        ],
        compiler_params=params(),
        cost_estimate=cost(2 * width * size * tile * SUBLANES, 8 * aux * size),
        name="both_halves",
    )(live, green_occ, green_vir, y, *before)
    return [half.reshape(-1, width) for half in outs[: len(CUTS)]], outs[len(CUTS) :]


def fold_kernel(live_ref, g_ref, y_ref, shifted_ref, own_ref, *rest, started, turn):
    z_ref, out_ref, kron_ref, acc_ref = rest[-4:]
    step = pl.program_id(0)

    @pl.when(step == 0)
    def _():
        scale = live_ref[0].astype(F32)
        kron_ref[...] = (repeated(g_ref[0].T, SPAN // g_ref.shape[1]).astype(F32) * scale).astype(BF)
        acc_ref[...] = rest[0][...] if started else jnp.zeros(acc_ref.shape, F32)

    for j in range(y_ref.shape[1] // SPAN):
        at = slice(j * SPAN, (j + 1) * SPAN)
        z_ref[:, at] = (dot(y_ref[:, at], kron_ref[...]) + shifted_ref[:, at].astype(F32)).astype(BF)
    acc_ref[...] += dot(z_ref[...], own_ref[...])

    @pl.when(step == pl.num_programs(0) - 1)
    def _():
        out_ref[...] = acc_ref[...].T if turn else acc_ref[...]


def fold(live, mats, y, piece, shifted, own, so_far, turn, before=()):
    aux = y.shape[0]
    size = y.shape[1] // PIECES
    span = 4 * SPAN if size % (4 * SPAN) == 0 else SPAN
    steps = size // span
    block = pl.BlockSpec((aux, span), lambda i: (0, i))
    whole = pl.BlockSpec((aux, aux), lambda i: (0, 0))
    added = [] if so_far is None else [so_far]
    return pl.pallas_call(
        lambda *refs: fold_kernel(*refs, started=bool(added), turn=turn),
        grid=(steps,),
        in_specs=[
            pl.BlockSpec(memory_space=pltpu.SMEM),
            pl.BlockSpec(mats.shape, lambda i: (0, 0, 0)),
            pl.BlockSpec((aux, span), lambda i: (0, piece * steps + i)),
            block,
            pl.BlockSpec((span, aux), lambda i: (piece * steps + i, 0)),
            *[whole] * len(added),
            *unused(before),
        ],
        out_specs=[block, whole],
        out_shape=[jax.ShapeDtypeStruct((aux, size), BF), jax.ShapeDtypeStruct((aux, aux), F32)],
        scratch_shapes=[pltpu.VMEM((SPAN, SPAN), BF), pltpu.VMEM((aux, aux), F32)],
        compiler_params=params(),
        cost_estimate=cost(2 * aux * size * (SPAN + aux), 2 * 4 * aux * size),
        name="fold",
    )(live, mats, y, shifted, own, *added, *before)


def both_kernel(live_ref, go_ref, gv_ref, y_ref, *rest, slices):
    rows_ref, yt_ref, half_ref, over_ref, tiles_ref, in_sems, out_sems = rest[-7:]
    outs = rest[-7 - len(CUTS) - PIECES : -7]
    half_outs, over_outs = outs[: len(CUTS)], outs[len(CUTS) :]
    aux, size = y_ref.shape
    step = aux // IN_STEPS
    fetch = []
    for i in range(IN_STEPS):
        at = pl.ds(i * step, step)
        fetch.append(pltpu.make_async_copy(y_ref.at[at], rows_ref.at[at], in_sems.at[i]))
    for copy in fetch:
        copy.start()
    tiles = [pltpu.make_async_copy(g.at[1], tiles_ref.at[i], in_sems.at[IN_STEPS + i]) for i, g in enumerate((go_ref, gv_ref))]
    for copy in tiles:
        copy.start()
    scale = live_ref[0].astype(F32)
    live = scale.astype(BF)
    for copy in tiles:
        copy.wait()
    occ_kron = spread(tiles_ref[0].T, SUBLANES)
    vir_kron = (repeated(tiles_ref[1].T, SPAN // gv_ref.shape[1]).astype(F32) * scale).astype(BF)
    for copy in fetch:
        copy.wait()
    store = []
    for c, out in enumerate(over_outs):
        wide = size // PIECES
        for j in range(wide // SPAN):
            at = c * wide + j * SPAN
            over_ref[c, :, j * SPAN : (j + 1) * SPAN] = dot(rows_ref[:, at : at + SPAN], vir_kron).astype(BF)
        store.append(pltpu.make_async_copy(over_ref.at[c], out, out_sems.at[len(CUTS) + c]))
        store[-1].start()

    def part_of(span):
        parts = [rows_ref[start : start + count, span] for start, count in slices]
        return (jnp.concatenate(parts, axis=0) if len(parts) > 1 else parts[0]) * live

    occ_group(occ_kron, yt_ref, half_ref, part_of, slice(0, yt_ref.shape[2]), size)
    to = 0
    for c, out in enumerate(half_outs):
        store.append(pltpu.make_async_copy(half_ref.at[pl.ds(to, out.shape[0])], out, out_sems.at[c]))
        store[-1].start()
        to += out.shape[0]
    for copy in store:
        copy.wait()


def both(live, green_occ, green_vir, y, slices, before=()):
    aux, size = y.shape
    tile = green_occ.shape[1]
    width = sum(count for _, count in slices)
    some = pl.BlockSpec(memory_space=pl.ANY)
    fixed = pl.BlockSpec(memory_space=pltpu.HBM)
    parts = [tile * n // sum(CUTS) for n in CUTS]
    outs = pl.pallas_call(
        lambda *refs: both_kernel(*refs, slices=slices),
        in_specs=[pl.BlockSpec(memory_space=pltpu.SMEM), fixed, fixed, some, *unused(before)],
        out_specs=[some] * (len(CUTS) + PIECES),
        out_shape=[jax.ShapeDtypeStruct((n, tile, width), BF) for n in parts]
        + [jax.ShapeDtypeStruct((aux, size // PIECES), BF)] * PIECES,
        scratch_shapes=[
            pltpu.VMEM((aux, size), BF),
            pltpu.VMEM((tile, tile, width), BF),
            pltpu.VMEM((tile, tile, width), BF),
            pltpu.VMEM((PIECES, aux, size // PIECES), BF),
            pltpu.VMEM((2, tile, tile), BF),
            pltpu.SemaphoreType.DMA((IN_STEPS + 2,)),
            pltpu.SemaphoreType.DMA((len(CUTS) + PIECES,)),
        ],
        compiler_params=params(),
        cost_estimate=cost(2 * width * size * tile * SUBLANES, 8 * aux * size),
        name="both_halves",
    )(live, green_occ, green_vir, y, *before)
    return [half.reshape(-1, width) for half in outs[: len(CUTS)]], outs[len(CUTS) :]


def vir_kernel(live_ref, g_ref, y_ref, *rest, n_added):
    added = rest[:n_added]
    out_ref, kron_ref = rest[-2:]

    @pl.when(pl.program_id(0) == 0)
    def _():
        scale = live_ref[0].astype(F32)
        kron_ref[...] = (repeated(g_ref[...], SPAN // g_ref.shape[0]).astype(F32) * scale).astype(BF)

    for j in range(y_ref.shape[1] // SPAN):
        at = slice(j * SPAN, (j + 1) * SPAN)
        got = dot(y_ref[:, at], kron_ref[...])
        for ref in added:
            got = got + ref[:, at].astype(F32)
        out_ref[:, at] = got.astype(BF)


def vir(live, mat, y, piece, added=(), before=()):
    aux = y.shape[0]
    size = y.shape[1] // PIECES
    span = 4 * SPAN if size % (4 * SPAN) == 0 else SPAN
    block = pl.BlockSpec((aux, span), lambda i: (0, i))
    return pl.pallas_call(
        lambda *refs: vir_kernel(*refs, n_added=len(added)),
        grid=(size // span,),
        in_specs=[
            pl.BlockSpec(memory_space=pltpu.SMEM),
            pl.BlockSpec(mat.shape, lambda i: (0, 0)),
            pl.BlockSpec((aux, span), lambda i: (0, piece * (size // span) + i)),
            *(block for _ in added),
            *unused(before),
        ],
        out_specs=block,
        out_shape=jax.ShapeDtypeStruct((aux, size), BF),
        scratch_shapes=[pltpu.VMEM((SPAN, SPAN), BF)],
        compiler_params=params(),
        cost_estimate=cost(2 * aux * size * SPAN, 2 * (2 + len(added)) * aux * size),
        name="vir",
    )(live, mat, y, *added, *before)


def product_kernel(x_ref, *rest, pieces, steps, at, started):
    z_refs = rest[:pieces]
    out_ref, acc_ref = rest[-2:]
    step = pl.program_id(0)

    @pl.when(step == 0)
    def _():
        acc_ref[...] = rest[pieces][...].T if started else jnp.zeros(acc_ref.shape, F32)

    for i, z_ref in enumerate(z_refs):

        @pl.when((step + at) // steps == i)
        def _(z_ref=z_ref):
            acc_ref[...] += dot(z_ref[...], x_ref[...])

    @pl.when(step == pl.num_programs(0) - 1)
    def _():
        out_ref[...] = acc_ref[...].T


def product(zs, x, start, so_far=None, before=()):
    aux, size = zs[0].shape
    width = x.shape[1]
    span = size // 2
    zs, at = zs[start // size :], start % size // span
    added = [] if so_far is None else [so_far]
    whole = pl.BlockSpec((width, aux), lambda i: (0, 0))
    piece = lambda k: pl.BlockSpec((aux, span), lambda i: (0, jnp.clip(i + at - 2 * k, 0, 1)))
    return pl.pallas_call(
        lambda *refs: product_kernel(*refs, pieces=len(zs), steps=2, at=at, started=bool(added)),
        grid=(x.shape[0] // span,),
        in_specs=[
            pl.BlockSpec((span, width), lambda i: (i, 0)),
            *(piece(k) for k in range(len(zs))),
            *[whole] * len(added),
            *unused(before),
        ],
        out_specs=whole,
        out_shape=jax.ShapeDtypeStruct((width, aux), F32),
        scratch_shapes=[pltpu.VMEM((aux, width), F32)],
        compiler_params=params(),
        cost_estimate=cost(2 * aux * x.shape[0] * width, 2 * x.shape[0] * (aux + width)),
        name="product",
    )(x, *zs, *added, *before)


def scattered(parts, axis, direct):
    size = lax.axis_size(axis)
    blocks = [part.reshape(size, part.shape[0] // size, part.shape[1]) for part in parts]
    blocks = jnp.concatenate(blocks, axis=1) if len(blocks) > 1 else blocks[0]
    if size & (size - 1):
        return lax.psum_scatter(blocks.astype(BF), axis, scatter_dimension=0).astype(F32)
    me = lax.axis_index(axis)
    reaches = [1 << i for i in range(size.bit_length() - 1)]
    if direct and size <= 4:
        total = lax.dynamic_index_in_dim(blocks, me, 0, keepdims=False)
        for reach in range(1, size):
            given = lax.dynamic_index_in_dim(blocks, me ^ reach, 0, keepdims=False).astype(BF)
            total = total + lax.ppermute(given, axis, [(i, i ^ reach) for i in range(size)]).astype(F32)
        return total
    for reach in reaches:
        bit = (me // reach) % 2
        pairs = blocks.reshape(blocks.shape[0] // 2, 2, *blocks.shape[1:])
        kept = lax.dynamic_index_in_dim(pairs, bit, 1, keepdims=False)
        given = lax.dynamic_index_in_dim(pairs, 1 - bit, 1, keepdims=False).astype(BF)
        got = lax.ppermute(given, axis, [(i, i ^ reach) for i in range(size)])
        blocks = kept + got.astype(F32)
    return blocks[0]


def chunks_of(aux, owners):
    each = aux // owners
    parts = [n // owners for n in CHUNKS]
    if aux == sum(CHUNKS) and all(n % (16 * owners) == 0 for n in CHUNKS):
        cuts = [sum(parts[:i]) for i in range(len(parts) + 1)]
        return [[(j * each + a, b - a) for j in range(owners)] for a, b in zip(cuts, cuts[1:])]
    return [[(0, aux)]]


def body(three_centre, green_occ, green_vir, pair_live):
    rows, cols = lax.axis_size("row"), lax.axis_size("col")
    y = three_centre[0, 0]
    aux, size = y.shape
    live = pair_live[0]
    up_row = [(i, i - 1) for i in range(1, rows)]
    up_col = [(i, i - 1) for i in range(1, cols)]

    send = lambda half: lax.ppermute(half, "row", up_row)
    chunks = chunks_of(aux, cols)
    chunked = len(chunks) > 1
    last = ()
    if chunked:
        last = [raw(live, green_occ[0], y, chunks[0])]
        unfolded = send(last[0])
    halves, over = both(live, green_occ[0], green_vir[0], y, chunks[-1], last)
    shifted = [lax.ppermute(piece, "col", up_col) for piece in over]
    ending = [send(half) for half in halves]
    spans = [(i, min(SPAN, aux - i)) for i in range(0, aux, SPAN)]
    own = occ(live, green_occ[0], 0, y, spans, before=halves[:1])
    zs = []
    diag = None
    for i in range(PIECES):
        z, diag = fold(live, green_vir[0], y, i, shifted[i], own, diag, i == PIECES - 1)
        zs.append(z)
    blocks, order = [], [[diag]] * len(ending)
    if chunked:
        early = raw_product(unfolded, zs, green_occ.shape[2], before=[diag])
        both_done = scattered([diag, early], "col", True)
        chi_d, blocks = both_done[: aux // cols], [both_done[aux // cols :]]
        order = [[early]] * (len(ending) - 1) + [[both_done]]
    else:
        chi_d = scattered([diag], "col", True)
    ended, start = None, 0
    for half, wait in zip(ending, order):
        ended = product(zs, half, start, ended, before=wait)
        start += half.shape[0]
    blocks.append(scattered([ended], "col", False))
    return chi_d[None], jnp.concatenate(blocks)[None]


def solution(mesh):
    return jax.shard_map(
        body,
        mesh=mesh,
        in_specs=(
            P("row", "col", None, None),
            P("row", None, None, None),
            P("col", None, None, None),
            P("row", "col"),
        ),
        out_specs=(P("row", "col", None), P("row", "col", None)),
        check_vma=False,
    )
```

```python
import jax
import jax.numpy as jnp
from jax import lax
from jax.experimental import pallas as pl
from jax.experimental.pallas import tpu as pltpu
from jax.sharding import PartitionSpec as P

BF = jnp.bfloat16
F32 = jnp.float32
VMEM_BYTES = 48 * 1024 * 1024
SPAN = 256
SUBLANES = 8
CHUNKS = (384, 256)
PIECES = 2
IN_STEPS = 4
CUTS = (3, 1)


def dot(a, b, dims=((1,), (0,))):
    return lax.dot_general(a, b, (dims, ((), ())), preferred_element_type=F32)


def iota(shape, axis):
    return lax.broadcasted_iota(jnp.int32, shape, axis)


def spread(g, group):
    m, k = g.shape
    pick_row = (iota((m * group, 1), 0) // group == iota((1, m), 1)).astype(BF)
    pick_col = (iota((k, 1), 0) == iota((1, k * group), 1) // group).astype(BF)
    full = dot(dot(pick_row, g).astype(BF), pick_col)
    same = iota((m * group, 1), 0) % group == iota((1, k * group), 1) % group
    return jnp.where(same, full, 0.0).astype(BF)


def repeated(g, count):
    t = g.shape[0]
    n = t * count
    pick = (iota((n, 1), 0) % t == iota((1, t), 1)).astype(BF)
    full = dot(dot(pick, g).astype(BF), pick, ((1,), (1,)))
    same = iota((n, 1), 0) // t == iota((1, n), 1) // t
    return jnp.where(same, full, 0.0).astype(BF)


def params():
    return pltpu.CompilerParams(vmem_limit_bytes=VMEM_BYTES)


def cost(flops, size):
    return pl.CostEstimate(flops=1, bytes_accessed=1, transcendentals=0)


def unused(before):
    return [pl.BlockSpec(memory_space=pl.ANY)] * len(before)


def occ_group(kron, yt_ref, held_ref, part_of, lanes, size):
    m, tile, _ = held_ref.shape
    width = lanes.stop - lanes.start
    per = SPAN // tile
    for j in range(size // SPAN):
        turned = part_of(slice(j * SPAN, (j + 1) * SPAN)).T
        yt_ref[j * per : (j + 1) * per, :, :width] = turned.reshape(per, tile, width)
    pair = 2 * SUBLANES
    for s in range(tile // pair):
        part = yt_ref[:, s * pair : (s + 1) * pair, :width].astype(F32)
        low, high = (
            part[:, i : i + SUBLANES].reshape(tile * SUBLANES, width).astype(BF) for i in (0, SUBLANES)
        )
        low, high = (dot(kron, x).reshape(m, SUBLANES, width) for x in (low, high))
        held_ref[:, s * pair : (s + 1) * pair, lanes] = jnp.concatenate([low, high], axis=1).astype(BF)


def occ_kernel(live_ref, g_ref, y_ref, *rest, groups, which, cuts):
    rows_ref, yt_ref, held_ref, in_sems, out_sems = rest[-5:]
    out_refs = rest[-5 - cuts : -5]
    m = g_ref.shape[2]
    size = y_ref.shape[1]
    fetch = []
    to = 0
    for slices, _ in groups:
        for start, count in slices:
            fetch.append(
                pltpu.make_async_copy(
                    y_ref.at[pl.ds(start, count)], rows_ref.at[pl.ds(to, count)], in_sems.at[len(fetch)]
                )
            )
            to += count
    for copy in fetch:
        copy.start()
    kron = spread(g_ref[which].T, SUBLANES)
    live = live_ref[0].astype(F32).astype(BF)
    store = []
    at, done = 0, 0
    for k, (slices, width) in enumerate(groups):
        for copy in fetch[done : done + len(slices)]:
            copy.wait()
        done += len(slices)
        lanes = slice(at, at + width)
        occ_group(kron, yt_ref.at[k], held_ref, lambda span: rows_ref[lanes, span] * live, lanes, size)
        for c, out_ref in enumerate(out_refs):
            some = pl.ds(c * (m // cuts), m // cuts)
            store.append(
                pltpu.make_async_copy(
                    held_ref.at[some, :, pl.ds(at, width)], out_ref.at[:, :, pl.ds(at, width)], out_sems.at[k, c]
                )
            )
            store[-1].start()
        at += width
    for copy in store:
        copy.wait()


def raw_kernel(live_ref, g_ref, y_ref, out_ref, rows_ref, tile_ref, tail_ref, tile_sem, in_sems, out_sems, *, slices):
    count, size = rows_ref.shape
    tile = tile_ref.shape[0]
    tail, wide = tail_ref.shape
    blocks = size // wide
    fetch_tile = pltpu.make_async_copy(g_ref.at[1], tile_ref, tile_sem)
    fetch_tile.start()
    fetch = []
    to = 0
    for i, (start, n) in enumerate(slices):
        fetch.append(pltpu.make_async_copy(y_ref.at[pl.ds(start, n)], rows_ref.at[pl.ds(to, n)], in_sems.at[i]))
        fetch[-1].start()
        to += n
    fetch_tile.wait()
    live = live_ref[0].astype(F32).astype(BF)
    tail_ref[...] = jnp.zeros((tail, wide), BF)
    for i in range(tile // tail):
        tail_ref[:, i * 128 : i * 128 + tile] = tile_ref[i * tail : (i + 1) * tail] * live
    store = [pltpu.make_async_copy(tail_ref, out_ref.at[pl.ds(count * blocks, tail)], out_sems.at[0])]
    store[0].start()
    to = 0
    for k, (_, n) in enumerate(slices):
        fetch[k].wait()
        for i in range(blocks):
            store.append(
                pltpu.make_async_copy(
                    rows_ref.at[pl.ds(to, n), pl.ds(i * wide, wide)],
                    out_ref.at[pl.ds(i * count + to, n)],
                    out_sems.at[len(store)],
                )
            )
            store[-1].start()
        to += n
    for copy in store:
        copy.wait()


RAW_TAIL = 16


def raw_shape(count, size, tile):
    wide = 128 * (tile // RAW_TAIL)
    return count * (size // wide) + RAW_TAIL, wide


def raw(live, mats, y, slices):
    count = sum(n for _, n in slices)
    size = y.shape[1]
    tile = mats.shape[1]
    shape = raw_shape(count, size, tile)
    some = pl.BlockSpec(memory_space=pltpu.HBM)
    return pl.pallas_call(
        lambda *refs: raw_kernel(*refs, slices=slices),
        in_specs=[pl.BlockSpec(memory_space=pltpu.SMEM), some, some],
        out_specs=some,
        out_shape=jax.ShapeDtypeStruct(shape, BF),
        scratch_shapes=[
            pltpu.VMEM((count, size), BF),
            pltpu.VMEM((tile, tile), BF),
            pltpu.VMEM((RAW_TAIL, shape[1]), BF),
            pltpu.SemaphoreType.DMA(()),
            pltpu.SemaphoreType.DMA((len(slices),)),
            pltpu.SemaphoreType.DMA((len(slices) * (size // shape[1]) + 1,)),
        ],
        compiler_params=params(),
        cost_estimate=cost(count * size, 4 * count * size),
        name="raw",
    )(live, mats, y)


def raw_product_kernel(r_ref, *rest):
    z_refs = rest[:PIECES]
    out_ref, g_ref, yt_ref, held_ref, z_held, rows_ref, tail_ref, sems = rest[-8:]
    tile, _, count = yt_ref.shape
    size = tile * tile
    wide = r_ref.shape[1]
    blocks = size // wide
    part = size // PIECES
    fetch_tail = pltpu.make_async_copy(r_ref.at[pl.ds(blocks * count, RAW_TAIL)], tail_ref, sems.at[PIECES])
    fetch_tail.start()
    fetch_rows = [
        pltpu.make_async_copy(r_ref.at[pl.ds(i * count, count)], rows_ref.at[i], sems.at[PIECES + 1 + i])
        for i in range(blocks)
    ]
    fetch = [pltpu.make_async_copy(z_refs[i], z_held.at[i], sems.at[i]) for i in range(PIECES)]
    for copy in fetch_rows + fetch:
        copy.start()
    fetch_tail.wait()
    for i in range(tile // RAW_TAIL):
        g_ref[i * RAW_TAIL : (i + 1) * RAW_TAIL] = tail_ref[:, i * 128 : i * 128 + tile]
    kron = spread(g_ref[...].T, SUBLANES)

    def part_of(span):
        block, at = divmod(span.start, wide)
        if at == 0:
            fetch_rows[block].wait()
        return rows_ref[block, :, at : at + SPAN]

    occ_group(kron, yt_ref, held_ref, part_of, slice(0, count), size)
    total = None
    for i in range(PIECES):
        fetch[i].wait()
        rows = slice(i * (tile // PIECES), (i + 1) * (tile // PIECES))
        got = dot(z_held[i], held_ref[rows].reshape(part, count))
        total = got if total is None else total + got
    out_ref[...] = total.T


def raw_product(received, zs, tile, before=()):
    size = tile * tile
    count = (received.shape[0] - RAW_TAIL) * received.shape[1] // size
    aux = zs[0].shape[0]
    return pl.pallas_call(
        raw_product_kernel,
        in_specs=[
            *[pl.BlockSpec(memory_space=pl.ANY)] * (1 + len(zs)),
            *unused(before),
        ],
        out_specs=pl.BlockSpec(memory_space=pltpu.VMEM),
        out_shape=jax.ShapeDtypeStruct((count, aux), F32),
        scratch_shapes=[
            pltpu.VMEM((tile, tile), BF),
            pltpu.VMEM((tile, tile, count), BF),
            pltpu.VMEM((tile, tile, count), BF),
            pltpu.VMEM((PIECES, aux, size // PIECES), BF),
            pltpu.VMEM((size // received.shape[1], count, received.shape[1]), BF),
            pltpu.VMEM((RAW_TAIL, received.shape[1]), BF),
            pltpu.SemaphoreType.DMA((PIECES + 1 + size // received.shape[1],)),
        ],
        compiler_params=params(),
        cost_estimate=cost(2 * count * size * (tile * SUBLANES + aux), 2 * size * (aux + count)),
        name="raw_product",
    )(received, *zs, *before)


def grouped(slices):
    groups, held = [], []
    for start, count in slices:
        held.append((start, count))
        width = sum(n for _, n in held)
        if width >= SPAN and width % 128 == 0:
            groups.append((held, width))
            held = []
    if held:
        groups.append((held, sum(n for _, n in held)))
    return groups


def occ(live, mats, which, y, slices, before=(), cuts=1):
    tile, m = mats.shape[1:]
    size = y.shape[1]
    groups = grouped(slices)
    width = sum(n for _, n in groups)
    widest = max(n for _, n in groups)
    outs = pl.pallas_call(
        lambda *refs: occ_kernel(*refs, groups=groups, which=which, cuts=cuts),
        in_specs=[
            pl.BlockSpec(memory_space=pltpu.SMEM),
            pl.BlockSpec(memory_space=pltpu.VMEM),
            pl.BlockSpec(memory_space=pl.ANY),
            *unused(before),
        ],
        out_specs=[pl.BlockSpec(memory_space=pl.ANY)] * cuts,
        out_shape=[jax.ShapeDtypeStruct((m // cuts, tile, width), BF)] * cuts,
        scratch_shapes=[
            pltpu.VMEM((width, size), BF),
            pltpu.VMEM((len(groups), tile, tile, widest), BF),
            pltpu.VMEM((m, tile, width), BF),
            pltpu.SemaphoreType.DMA((len(slices),)),
            pltpu.SemaphoreType.DMA((len(groups), cuts)),
        ],
        compiler_params=params(),
        cost_estimate=cost(2 * width * size * m * SUBLANES, 4 * width * size),
        name="occ",
    )(live, mats, y, *before)
    return outs[0].reshape(-1, width)


def both_kernel(live_ref, go_ref, gv_ref, y_ref, *rest, slices):
    rows_ref, yt_ref, half_ref, over_ref, tiles_ref, in_sems, out_sems = rest[-7:]
    outs = rest[-7 - len(CUTS) - PIECES : -7]
    half_outs, over_outs = outs[: len(CUTS)], outs[len(CUTS) :]
    aux, size = y_ref.shape
    step = aux // IN_STEPS
    fetch = []
    for i in range(IN_STEPS):
        at = pl.ds(i * step, step)
        fetch.append(pltpu.make_async_copy(y_ref.at[at], rows_ref.at[at], in_sems.at[i]))
    for copy in fetch:
        copy.start()
    tiles = [pltpu.make_async_copy(g.at[1], tiles_ref.at[i], in_sems.at[IN_STEPS + i]) for i, g in enumerate((go_ref, gv_ref))]
    for copy in tiles:
        copy.start()
    scale = live_ref[0].astype(F32)
    live = scale.astype(BF)
    for copy in tiles:
        copy.wait()
    occ_kron = spread(tiles_ref[0].T, SUBLANES)
    vir_kron = (repeated(tiles_ref[1].T, SPAN // gv_ref.shape[1]).astype(F32) * scale).astype(BF)
    for copy in fetch:
        copy.wait()
    store = []
    for c, out in enumerate(over_outs):
        wide = size // PIECES
        for j in range(wide // SPAN):
            at = c * wide + j * SPAN
            over_ref[c, :, j * SPAN : (j + 1) * SPAN] = dot(rows_ref[:, at : at + SPAN], vir_kron).astype(BF)
        store.append(pltpu.make_async_copy(over_ref.at[c], out, out_sems.at[len(CUTS) + c]))
        store[-1].start()

    def part_of(span):
        parts = [rows_ref[start : start + count, span] for start, count in slices]
        return (jnp.concatenate(parts, axis=0) if len(parts) > 1 else parts[0]) * live

    occ_group(occ_kron, yt_ref, half_ref, part_of, slice(0, yt_ref.shape[2]), size)
    to = 0
    for c, out in enumerate(half_outs):
        store.append(pltpu.make_async_copy(half_ref.at[pl.ds(to, out.shape[0])], out, out_sems.at[c]))
        store[-1].start()
        to += out.shape[0]
    for copy in store:
        copy.wait()


def both(live, green_occ, green_vir, y, slices, before=()):
    aux, size = y.shape
    tile = green_occ.shape[1]
    width = sum(count for _, count in slices)
    some = pl.BlockSpec(memory_space=pl.ANY)
    fixed = pl.BlockSpec(memory_space=pltpu.HBM)
    parts = [tile * n // sum(CUTS) for n in CUTS]
    outs = pl.pallas_call(
        lambda *refs: both_kernel(*refs, slices=slices),
        in_specs=[pl.BlockSpec(memory_space=pltpu.SMEM), fixed, fixed, some, *unused(before)],
        out_specs=[some] * (len(CUTS) + PIECES),
        out_shape=[jax.ShapeDtypeStruct((n, tile, width), BF) for n in parts]
        + [jax.ShapeDtypeStruct((aux, size // PIECES), BF)] * PIECES,
        scratch_shapes=[
            pltpu.VMEM((aux, size), BF),
            pltpu.VMEM((tile, tile, width), BF),
            pltpu.VMEM((tile, tile, width), BF),
            pltpu.VMEM((PIECES, aux, size // PIECES), BF),
            pltpu.VMEM((2, tile, tile), BF),
            pltpu.SemaphoreType.DMA((IN_STEPS + 2,)),
            pltpu.SemaphoreType.DMA((len(CUTS) + PIECES,)),
        ],
        compiler_params=params(),
        cost_estimate=cost(2 * width * size * tile * SUBLANES, 8 * aux * size),
        name="both_halves",
    )(live, green_occ, green_vir, y, *before)
    return [half.reshape(-1, width) for half in outs[: len(CUTS)]], outs[len(CUTS) :]


def fold_kernel(live_ref, g_ref, y_ref, shifted_ref, own_ref, *rest, started, turn):
    z_ref, out_ref, kron_ref, acc_ref = rest[-4:]
    step = pl.program_id(0)

    @pl.when(step == 0)
    def _():
        scale = live_ref[0].astype(F32)
        kron_ref[...] = (repeated(g_ref[0].T, SPAN // g_ref.shape[1]).astype(F32) * scale).astype(BF)
        acc_ref[...] = rest[0][...] if started else jnp.zeros(acc_ref.shape, F32)

    for j in range(y_ref.shape[1] // SPAN):
        at = slice(j * SPAN, (j + 1) * SPAN)
        z_ref[:, at] = (dot(y_ref[:, at], kron_ref[...]) + shifted_ref[:, at].astype(F32)).astype(BF)
    acc_ref[...] += dot(z_ref[...], own_ref[...])

    @pl.when(step == pl.num_programs(0) - 1)
    def _():
        out_ref[...] = acc_ref[...].T if turn else acc_ref[...]


def fold(live, mats, y, piece, shifted, own, so_far, turn, before=()):
    aux = y.shape[0]
    size = y.shape[1] // PIECES
    span = 4 * SPAN if size % (4 * SPAN) == 0 else SPAN
    steps = size // span
    block = pl.BlockSpec((aux, span), lambda i: (0, i))
    whole = pl.BlockSpec((aux, aux), lambda i: (0, 0))
    added = [] if so_far is None else [so_far]
    return pl.pallas_call(
        lambda *refs: fold_kernel(*refs, started=bool(added), turn=turn),
        grid=(steps,),
        in_specs=[
            pl.BlockSpec(memory_space=pltpu.SMEM),
            pl.BlockSpec(mats.shape, lambda i: (0, 0, 0)),
            pl.BlockSpec((aux, span), lambda i: (0, piece * steps + i)),
            block,
            pl.BlockSpec((span, aux), lambda i: (piece * steps + i, 0)),
            *[whole] * len(added),
            *unused(before),
        ],
        out_specs=[block, whole],
        out_shape=[jax.ShapeDtypeStruct((aux, size), BF), jax.ShapeDtypeStruct((aux, aux), F32)],
        scratch_shapes=[pltpu.VMEM((SPAN, SPAN), BF), pltpu.VMEM((aux, aux), F32)],
        compiler_params=params(),
        cost_estimate=cost(2 * aux * size * (SPAN + aux), 2 * 4 * aux * size),
        name="fold",
    )(live, mats, y, shifted, own, *added, *before)


def both_kernel(live_ref, go_ref, gv_ref, y_ref, *rest, slices):
    rows_ref, yt_ref, half_ref, over_ref, tiles_ref, in_sems, out_sems = rest[-7:]
    outs = rest[-7 - len(CUTS) - PIECES : -7]
    half_outs, over_outs = outs[: len(CUTS)], outs[len(CUTS) :]
    aux, size = y_ref.shape
    step = aux // IN_STEPS
    fetch = []
    for i in range(IN_STEPS):
        at = pl.ds(i * step, step)
        fetch.append(pltpu.make_async_copy(y_ref.at[at], rows_ref.at[at], in_sems.at[i]))
    for copy in fetch:
        copy.start()
    tiles = [pltpu.make_async_copy(g.at[1], tiles_ref.at[i], in_sems.at[IN_STEPS + i]) for i, g in enumerate((go_ref, gv_ref))]
    for copy in tiles:
        copy.start()
    scale = live_ref[0].astype(F32)
    live = scale.astype(BF)
    for copy in tiles:
        copy.wait()
    occ_kron = spread(tiles_ref[0].T, SUBLANES)
    vir_kron = (repeated(tiles_ref[1].T, SPAN // gv_ref.shape[1]).astype(F32) * scale).astype(BF)
    for copy in fetch:
        copy.wait()
    store = []
    for c, out in enumerate(over_outs):
        wide = size // PIECES
        for j in range(wide // SPAN):
            at = c * wide + j * SPAN
            over_ref[c, :, j * SPAN : (j + 1) * SPAN] = dot(rows_ref[:, at : at + SPAN], vir_kron).astype(BF)
        store.append(pltpu.make_async_copy(over_ref.at[c], out, out_sems.at[len(CUTS) + c]))
        store[-1].start()

    def part_of(span):
        parts = [rows_ref[start : start + count, span] for start, count in slices]
        return (jnp.concatenate(parts, axis=0) if len(parts) > 1 else parts[0]) * live

    occ_group(occ_kron, yt_ref, half_ref, part_of, slice(0, yt_ref.shape[2]), size)
    to = 0
    for c, out in enumerate(half_outs):
        store.append(pltpu.make_async_copy(half_ref.at[pl.ds(to, out.shape[0])], out, out_sems.at[c]))
        store[-1].start()
        to += out.shape[0]
    for copy in store:
        copy.wait()


def both(live, green_occ, green_vir, y, slices, before=()):
    aux, size = y.shape
    tile = green_occ.shape[1]
    width = sum(count for _, count in slices)
    some = pl.BlockSpec(memory_space=pl.ANY)
    fixed = pl.BlockSpec(memory_space=pltpu.HBM)
    parts = [tile * n // sum(CUTS) for n in CUTS]
    outs = pl.pallas_call(
        lambda *refs: both_kernel(*refs, slices=slices),
        in_specs=[pl.BlockSpec(memory_space=pltpu.SMEM), fixed, fixed, some, *unused(before)],
        out_specs=[some] * (len(CUTS) + PIECES),
        out_shape=[jax.ShapeDtypeStruct((n, tile, width), BF) for n in parts]
        + [jax.ShapeDtypeStruct((aux, size // PIECES), BF)] * PIECES,
        scratch_shapes=[
            pltpu.VMEM((aux, size), BF),
            pltpu.VMEM((tile, tile, width), BF),
            pltpu.VMEM((tile, tile, width), BF),
            pltpu.VMEM((PIECES, aux, size // PIECES), BF),
            pltpu.VMEM((2, tile, tile), BF),
            pltpu.SemaphoreType.DMA((IN_STEPS + 2,)),
            pltpu.SemaphoreType.DMA((len(CUTS) + PIECES,)),
        ],
        compiler_params=params(),
        cost_estimate=cost(2 * width * size * tile * SUBLANES, 8 * aux * size),
        name="both_halves",
    )(live, green_occ, green_vir, y, *before)
    return [half.reshape(-1, width) for half in outs[: len(CUTS)]], outs[len(CUTS) :]


def vir_kernel(live_ref, g_ref, y_ref, *rest, n_added):
    added = rest[:n_added]
    out_ref, kron_ref = rest[-2:]

    @pl.when(pl.program_id(0) == 0)
    def _():
        scale = live_ref[0].astype(F32)
        kron_ref[...] = (repeated(g_ref[...], SPAN // g_ref.shape[0]).astype(F32) * scale).astype(BF)

    for j in range(y_ref.shape[1] // SPAN):
        at = slice(j * SPAN, (j + 1) * SPAN)
        got = dot(y_ref[:, at], kron_ref[...])
        for ref in added:
            got = got + ref[:, at].astype(F32)
        out_ref[:, at] = got.astype(BF)


def vir(live, mat, y, piece, added=(), before=()):
    aux = y.shape[0]
    size = y.shape[1] // PIECES
    span = 4 * SPAN if size % (4 * SPAN) == 0 else SPAN
    block = pl.BlockSpec((aux, span), lambda i: (0, i))
    return pl.pallas_call(
        lambda *refs: vir_kernel(*refs, n_added=len(added)),
        grid=(size // span,),
        in_specs=[
            pl.BlockSpec(memory_space=pltpu.SMEM),
            pl.BlockSpec(mat.shape, lambda i: (0, 0)),
            pl.BlockSpec((aux, span), lambda i: (0, piece * (size // span) + i)),
            *(block for _ in added),
            *unused(before),
        ],
        out_specs=block,
        out_shape=jax.ShapeDtypeStruct((aux, size), BF),
        scratch_shapes=[pltpu.VMEM((SPAN, SPAN), BF)],
        compiler_params=params(),
        cost_estimate=cost(2 * aux * size * SPAN, 2 * (2 + len(added)) * aux * size),
        name="vir",
    )(live, mat, y, *added, *before)


def product_kernel(x_ref, *rest, pieces, steps, at, started):
    z_refs = rest[:pieces]
    out_ref, acc_ref = rest[-2:]
    step = pl.program_id(0)

    @pl.when(step == 0)
    def _():
        acc_ref[...] = rest[pieces][...].T if started else jnp.zeros(acc_ref.shape, F32)

    for i, z_ref in enumerate(z_refs):

        @pl.when((step + at) // steps == i)
        def _(z_ref=z_ref):
            acc_ref[...] += dot(z_ref[...], x_ref[...])

    @pl.when(step == pl.num_programs(0) - 1)
    def _():
        out_ref[...] = acc_ref[...].T


def product(zs, x, start, so_far=None, before=()):
    aux, size = zs[0].shape
    width = x.shape[1]
    span = size // 2
    zs, at = zs[start // size :], start % size // span
    added = [] if so_far is None else [so_far]
    whole = pl.BlockSpec((width, aux), lambda i: (0, 0))
    piece = lambda k: pl.BlockSpec((aux, span), lambda i: (0, jnp.clip(i + at - 2 * k, 0, 1)))
    return pl.pallas_call(
        lambda *refs: product_kernel(*refs, pieces=len(zs), steps=2, at=at, started=bool(added)),
        grid=(x.shape[0] // span,),
        in_specs=[
            pl.BlockSpec((span, width), lambda i: (i, 0)),
            *(piece(k) for k in range(len(zs))),
            *[whole] * len(added),
            *unused(before),
        ],
        out_specs=whole,
        out_shape=jax.ShapeDtypeStruct((width, aux), F32),
        scratch_shapes=[pltpu.VMEM((aux, width), F32)],
        compiler_params=params(),
        cost_estimate=cost(2 * aux * x.shape[0] * width, 2 * x.shape[0] * (aux + width)),
        name="product",
    )(x, *zs, *added, *before)


def scattered(parts, axis, direct):
    size = lax.axis_size(axis)
    blocks = [part.reshape(size, part.shape[0] // size, part.shape[1]) for part in parts]
    blocks = jnp.concatenate(blocks, axis=1) if len(blocks) > 1 else blocks[0]
    if size & (size - 1):
        return lax.psum_scatter(blocks.astype(BF), axis, scatter_dimension=0).astype(F32)
    me = lax.axis_index(axis)
    reaches = [1 << i for i in range(size.bit_length() - 1)]
    if direct and size <= 4:
        total = lax.dynamic_index_in_dim(blocks, me, 0, keepdims=False)
        for reach in range(1, size):
            given = lax.dynamic_index_in_dim(blocks, me ^ reach, 0, keepdims=False).astype(BF)
            total = total + lax.ppermute(given, axis, [(i, i ^ reach) for i in range(size)]).astype(F32)
        return total
    for reach in reaches:
        bit = (me // reach) % 2
        pairs = blocks.reshape(blocks.shape[0] // 2, 2, *blocks.shape[1:])
        kept = lax.dynamic_index_in_dim(pairs, bit, 1, keepdims=False)
        given = lax.dynamic_index_in_dim(pairs, 1 - bit, 1, keepdims=False).astype(BF)
        got = lax.ppermute(given, axis, [(i, i ^ reach) for i in range(size)])
        blocks = kept + got.astype(F32)
    return blocks[0]


def chunks_of(aux, owners):
    each = aux // owners
    parts = [n // owners for n in CHUNKS]
    if aux == sum(CHUNKS) and all(n % (16 * owners) == 0 for n in CHUNKS):
        cuts = [sum(parts[:i]) for i in range(len(parts) + 1)]
        return [[(j * each + a, b - a) for j in range(owners)] for a, b in zip(cuts, cuts[1:])]
    return [[(0, aux)]]


def body(three_centre, green_occ, green_vir, pair_live):
    rows, cols = lax.axis_size("row"), lax.axis_size("col")
    y = three_centre[0, 0]
    aux, size = y.shape
    live = pair_live[0]
    up_row = [(i, i - 1) for i in range(1, rows)]
    up_col = [(i, i - 1) for i in range(1, cols)]

    send = lambda half: lax.ppermute(half, "row", up_row)
    chunks = chunks_of(aux, cols)
    chunked = len(chunks) > 1
    last = ()
    if chunked:
        last = [raw(live, green_occ[0], y, chunks[0])]
        unfolded = send(last[0])
    halves, over = both(live, green_occ[0], green_vir[0], y, chunks[-1], last)
    shifted = [lax.ppermute(piece, "col", up_col) for piece in over]
    ending = [send(half) for half in halves]
    spans = [(i, min(SPAN, aux - i)) for i in range(0, aux, SPAN)]
    own = occ(live, green_occ[0], 0, y, spans, before=halves[:1])
    zs = []
    diag = None
    for i in range(PIECES):
        z, diag = fold(live, green_vir[0], y, i, shifted[i], own, diag, i == PIECES - 1)
        zs.append(z)
    blocks, order = [], [[diag]] * len(ending)
    if chunked:
        early = raw_product(unfolded, zs, green_occ.shape[2], before=[diag])
        both_done = scattered([diag, early], "col", True)
        chi_d, blocks = both_done[: aux // cols], [both_done[aux // cols :]]
        order = [[early]] * (len(ending) - 1) + [[both_done]]
    else:
        chi_d = scattered([diag], "col", True)
    ended, start = None, 0
    for half, wait in zip(ending, order):
        ended = product(zs, half, start, ended, before=wait)
        start += half.shape[0]
    blocks.append(scattered([ended], "col", True))
    return chi_d[None], jnp.concatenate(blocks)[None]


def solution(mesh):
    return jax.shard_map(
        body,
        mesh=mesh,
        in_specs=(
            P("row", "col", None, None),
            P("row", None, None, None),
            P("col", None, None, None),
            P("row", "col"),
        ),
        out_specs=(P("row", "col", None), P("row", "col", None)),
        check_vma=False,
    )
```

```python
import jax
import jax.numpy as jnp
from jax import lax
from jax.experimental import pallas as pl
from jax.experimental.pallas import tpu as pltpu
from jax.sharding import PartitionSpec as P

BF = jnp.bfloat16
F32 = jnp.float32
VMEM_BYTES = 48 * 1024 * 1024
SPAN = 256
SUBLANES = 8
LANES = 128
PIECES = 2
IN_STEPS = 4
CUTS = (3, 1)


def dot(a, b, dims=((1,), (0,))):
    return lax.dot_general(a, b, (dims, ((), ())), preferred_element_type=F32)


def iota(shape, axis):
    return lax.broadcasted_iota(jnp.int32, shape, axis)


def spread(g, group):
    m, k = g.shape
    pick_row = (iota((m * group, 1), 0) // group == iota((1, m), 1)).astype(BF)
    pick_col = (iota((k, 1), 0) == iota((1, k * group), 1) // group).astype(BF)
    full = dot(dot(pick_row, g).astype(BF), pick_col)
    same = iota((m * group, 1), 0) % group == iota((1, k * group), 1) % group
    return jnp.where(same, full, 0.0).astype(BF)


def repeated(g, count):
    t = g.shape[0]
    n = t * count
    pick = (iota((n, 1), 0) % t == iota((1, t), 1)).astype(BF)
    full = dot(dot(pick, g).astype(BF), pick, ((1,), (1,)))
    same = iota((n, 1), 0) // t == iota((1, n), 1) // t
    return jnp.where(same, full, 0.0).astype(BF)


def params():
    return pltpu.CompilerParams(vmem_limit_bytes=VMEM_BYTES)


def cost(flops, size):
    return pl.CostEstimate(flops=1, bytes_accessed=1, transcendentals=0)


def unused(before):
    return [pl.BlockSpec(memory_space=pl.ANY)] * len(before)


def occ_group(kron, yt_ref, held_ref, part_of, lanes, size):
    m, tile, _ = held_ref.shape
    width = lanes.stop - lanes.start
    per = SPAN // tile
    for j in range(size // SPAN):
        turned = part_of(slice(j * SPAN, (j + 1) * SPAN)).T
        yt_ref[j * per : (j + 1) * per, :, :width] = turned.reshape(per, tile, width)
    pair = 2 * SUBLANES
    for s in range(tile // pair):
        part = yt_ref[:, s * pair : (s + 1) * pair, :width].astype(F32)
        low, high = (
            part[:, i : i + SUBLANES].reshape(tile * SUBLANES, width).astype(BF) for i in (0, SUBLANES)
        )
        low, high = (dot(kron, x).reshape(m, SUBLANES, width) for x in (low, high))
        held_ref[:, s * pair : (s + 1) * pair, lanes] = jnp.concatenate([low, high], axis=1).astype(BF)


def occ_kernel(live_ref, g_ref, y_ref, *rest, groups, which, cuts):
    rows_ref, yt_ref, held_ref, in_sems, out_sems = rest[-5:]
    out_refs = rest[-5 - cuts : -5]
    m = g_ref.shape[2]
    size = y_ref.shape[1]
    fetch = []
    to = 0
    for slices, _ in groups:
        for start, count in slices:
            fetch.append(
                pltpu.make_async_copy(
                    y_ref.at[pl.ds(start, count)], rows_ref.at[pl.ds(to, count)], in_sems.at[len(fetch)]
                )
            )
            to += count
    for copy in fetch:
        copy.start()
    kron = spread(g_ref[which].T, SUBLANES)
    live = live_ref[0].astype(F32).astype(BF)
    store = []
    at, done = 0, 0
    for k, (slices, width) in enumerate(groups):
        for copy in fetch[done : done + len(slices)]:
            copy.wait()
        done += len(slices)
        lanes = slice(at, at + width)
        occ_group(kron, yt_ref.at[k], held_ref, lambda span: rows_ref[lanes, span] * live, lanes, size)
        for c, out_ref in enumerate(out_refs):
            some = pl.ds(c * (m // cuts), m // cuts)
            store.append(
                pltpu.make_async_copy(
                    held_ref.at[some, :, pl.ds(at, width)], out_ref.at[:, :, pl.ds(at, width)], out_sems.at[k, c]
                )
            )
            store[-1].start()
        at += width
    for copy in store:
        copy.wait()


def raw_kernel(live_ref, g_ref, y_ref, out_ref, rows_ref, tile_ref, tail_ref, tile_sem, in_sems, out_sems, *, slices):
    count, size = rows_ref.shape
    tile = tile_ref.shape[0]
    tail, wide = tail_ref.shape
    blocks = size // wide
    fetch_tile = pltpu.make_async_copy(g_ref.at[1], tile_ref, tile_sem)
    fetch_tile.start()
    fetch = []
    to = 0
    for i, (start, n) in enumerate(slices):
        fetch.append(pltpu.make_async_copy(y_ref.at[pl.ds(start, n)], rows_ref.at[pl.ds(to, n)], in_sems.at[i]))
        fetch[-1].start()
        to += n
    fetch_tile.wait()
    live = live_ref[0].astype(F32).astype(BF)
    tail_ref[...] = jnp.zeros((tail, wide), BF)
    for i in range(tile // tail):
        tail_ref[:, i * 128 : i * 128 + tile] = tile_ref[i * tail : (i + 1) * tail] * live
    store = [pltpu.make_async_copy(tail_ref, out_ref.at[pl.ds(count * blocks, tail)], out_sems.at[0])]
    store[0].start()
    to = 0
    for k, (_, n) in enumerate(slices):
        fetch[k].wait()
        for i in range(blocks):
            store.append(
                pltpu.make_async_copy(
                    rows_ref.at[pl.ds(to, n), pl.ds(i * wide, wide)],
                    out_ref.at[pl.ds(i * count + to, n)],
                    out_sems.at[len(store)],
                )
            )
            store[-1].start()
        to += n
    for copy in store:
        copy.wait()


RAW_TAIL = 16


def raw_shape(count, size, tile):
    wide = 128 * (tile // RAW_TAIL)
    return count * (size // wide) + RAW_TAIL, wide


def raw(live, mats, y, slices):
    count = sum(n for _, n in slices)
    size = y.shape[1]
    tile = mats.shape[1]
    shape = raw_shape(count, size, tile)
    some = pl.BlockSpec(memory_space=pltpu.HBM)
    return pl.pallas_call(
        lambda *refs: raw_kernel(*refs, slices=slices),
        in_specs=[pl.BlockSpec(memory_space=pltpu.SMEM), some, some],
        out_specs=some,
        out_shape=jax.ShapeDtypeStruct(shape, BF),
        scratch_shapes=[
            pltpu.VMEM((count, size), BF),
            pltpu.VMEM((tile, tile), BF),
            pltpu.VMEM((RAW_TAIL, shape[1]), BF),
            pltpu.SemaphoreType.DMA(()),
            pltpu.SemaphoreType.DMA((len(slices),)),
            pltpu.SemaphoreType.DMA((len(slices) * (size // shape[1]) + 1,)),
        ],
        compiler_params=params(),
        cost_estimate=cost(count * size, 4 * count * size),
        name="raw",
    )(live, mats, y)


def raw_product_kernel(r_ref, *rest):
    z_refs = rest[:PIECES]
    out_ref, g_ref, yt_ref, held_ref, z_held, rows_ref, tail_ref, sems = rest[-8:]
    tile, _, count = yt_ref.shape
    size = tile * tile
    wide = r_ref.shape[1]
    blocks = size // wide
    part = size // PIECES
    fetch_tail = pltpu.make_async_copy(r_ref.at[pl.ds(blocks * count, RAW_TAIL)], tail_ref, sems.at[PIECES])
    fetch_tail.start()
    fetch_rows = [
        pltpu.make_async_copy(r_ref.at[pl.ds(i * count, count)], rows_ref.at[i], sems.at[PIECES + 1 + i])
        for i in range(blocks)
    ]
    fetch = [pltpu.make_async_copy(z_refs[i], z_held.at[i], sems.at[i]) for i in range(PIECES)]
    for copy in fetch_rows + fetch:
        copy.start()
    fetch_tail.wait()
    for i in range(tile // RAW_TAIL):
        g_ref[i * RAW_TAIL : (i + 1) * RAW_TAIL] = tail_ref[:, i * 128 : i * 128 + tile]
    kron = spread(g_ref[...].T, SUBLANES)

    def part_of(span):
        block, at = divmod(span.start, wide)
        if at == 0:
            fetch_rows[block].wait()
        return rows_ref[block, :, at : at + SPAN]

    occ_group(kron, yt_ref, held_ref, part_of, slice(0, count), size)
    total = None
    for i in range(PIECES):
        fetch[i].wait()
        rows = slice(i * (tile // PIECES), (i + 1) * (tile // PIECES))
        got = dot(z_held[i], held_ref[rows].reshape(part, count))
        total = got if total is None else total + got
    out_ref[...] = total.T


def raw_product(received, zs, tile, before=()):
    size = tile * tile
    count = (received.shape[0] - RAW_TAIL) * received.shape[1] // size
    aux = zs[0].shape[0]
    return pl.pallas_call(
        raw_product_kernel,
        in_specs=[
            *[pl.BlockSpec(memory_space=pl.ANY)] * (1 + len(zs)),
            *unused(before),
        ],
        out_specs=pl.BlockSpec(memory_space=pltpu.VMEM),
        out_shape=jax.ShapeDtypeStruct((count, aux), F32),
        scratch_shapes=[
            pltpu.VMEM((tile, tile), BF),
            pltpu.VMEM((tile, tile, count), BF),
            pltpu.VMEM((tile, tile, count), BF),
            pltpu.VMEM((PIECES, aux, size // PIECES), BF),
            pltpu.VMEM((size // received.shape[1], count, received.shape[1]), BF),
            pltpu.VMEM((RAW_TAIL, received.shape[1]), BF),
            pltpu.SemaphoreType.DMA((PIECES + 1 + size // received.shape[1],)),
        ],
        compiler_params=params(),
        cost_estimate=cost(2 * count * size * (tile * SUBLANES + aux), 2 * size * (aux + count)),
        name="raw_product",
    )(received, *zs, *before)


def grouped(slices):
    groups, held = [], []
    for start, count in slices:
        held.append((start, count))
        width = sum(n for _, n in held)
        if width >= SPAN and width % 128 == 0:
            groups.append((held, width))
            held = []
    if held:
        groups.append((held, sum(n for _, n in held)))
    return groups


def occ(live, mats, which, y, slices, before=(), cuts=1):
    tile, m = mats.shape[1:]
    size = y.shape[1]
    groups = grouped(slices)
    width = sum(n for _, n in groups)
    widest = max(n for _, n in groups)
    outs = pl.pallas_call(
        lambda *refs: occ_kernel(*refs, groups=groups, which=which, cuts=cuts),
        in_specs=[
            pl.BlockSpec(memory_space=pltpu.SMEM),
            pl.BlockSpec(memory_space=pltpu.VMEM),
            pl.BlockSpec(memory_space=pl.ANY),
            *unused(before),
        ],
        out_specs=[pl.BlockSpec(memory_space=pl.ANY)] * cuts,
        out_shape=[jax.ShapeDtypeStruct((m // cuts, tile, width), BF)] * cuts,
        scratch_shapes=[
            pltpu.VMEM((width, size), BF),
            pltpu.VMEM((len(groups), tile, tile, widest), BF),
            pltpu.VMEM((m, tile, width), BF),
            pltpu.SemaphoreType.DMA((len(slices),)),
            pltpu.SemaphoreType.DMA((len(groups), cuts)),
        ],
        compiler_params=params(),
        cost_estimate=cost(2 * width * size * m * SUBLANES, 4 * width * size),
        name="occ",
    )(live, mats, y, *before)
    return outs[0].reshape(-1, width)


def both_kernel(live_ref, go_ref, gv_ref, y_ref, *rest, slices):
    rows_ref, yt_ref, half_ref, over_ref, tiles_ref, in_sems, out_sems = rest[-7:]
    outs = rest[-7 - len(CUTS) - PIECES : -7]
    half_outs, over_outs = outs[: len(CUTS)], outs[len(CUTS) :]
    aux, size = y_ref.shape
    step = aux // IN_STEPS
    fetch = []
    for i in range(IN_STEPS):
        at = pl.ds(i * step, step)
        fetch.append(pltpu.make_async_copy(y_ref.at[at], rows_ref.at[at], in_sems.at[i]))
    for copy in fetch:
        copy.start()
    tiles = [pltpu.make_async_copy(g.at[1], tiles_ref.at[i], in_sems.at[IN_STEPS + i]) for i, g in enumerate((go_ref, gv_ref))]
    for copy in tiles:
        copy.start()
    scale = live_ref[0].astype(F32)
    live = scale.astype(BF)
    for copy in tiles:
        copy.wait()
    occ_kron = spread(tiles_ref[0].T, SUBLANES)
    vir_kron = (repeated(tiles_ref[1].T, SPAN // gv_ref.shape[1]).astype(F32) * scale).astype(BF)
    for copy in fetch:
        copy.wait()
    store = []
    for c, out in enumerate(over_outs):
        wide = size // PIECES
        for j in range(wide // SPAN):
            at = c * wide + j * SPAN
            over_ref[c, :, j * SPAN : (j + 1) * SPAN] = dot(rows_ref[:, at : at + SPAN], vir_kron).astype(BF)
        store.append(pltpu.make_async_copy(over_ref.at[c], out, out_sems.at[len(CUTS) + c]))
        store[-1].start()

    def part_of(span):
        parts = [rows_ref[start : start + count, span] for start, count in slices]
        return (jnp.concatenate(parts, axis=0) if len(parts) > 1 else parts[0]) * live

    occ_group(occ_kron, yt_ref, half_ref, part_of, slice(0, yt_ref.shape[2]), size)
    to = 0
    for c, out in enumerate(half_outs):
        store.append(pltpu.make_async_copy(half_ref.at[pl.ds(to, out.shape[0])], out, out_sems.at[c]))
        store[-1].start()
        to += out.shape[0]
    for copy in store:
        copy.wait()


def both(live, green_occ, green_vir, y, slices, before=()):
    aux, size = y.shape
    tile = green_occ.shape[1]
    width = sum(count for _, count in slices)
    some = pl.BlockSpec(memory_space=pl.ANY)
    fixed = pl.BlockSpec(memory_space=pltpu.HBM)
    parts = [tile * n // sum(CUTS) for n in CUTS]
    outs = pl.pallas_call(
        lambda *refs: both_kernel(*refs, slices=slices),
        in_specs=[pl.BlockSpec(memory_space=pltpu.SMEM), fixed, fixed, some, *unused(before)],
        out_specs=[some] * (len(CUTS) + PIECES),
        out_shape=[jax.ShapeDtypeStruct((n, tile, width), BF) for n in parts]
        + [jax.ShapeDtypeStruct((aux, size // PIECES), BF)] * PIECES,
        scratch_shapes=[
            pltpu.VMEM((aux, size), BF),
            pltpu.VMEM((tile, tile, width), BF),
            pltpu.VMEM((tile, tile, width), BF),
            pltpu.VMEM((PIECES, aux, size // PIECES), BF),
            pltpu.VMEM((2, tile, tile), BF),
            pltpu.SemaphoreType.DMA((IN_STEPS + 2,)),
            pltpu.SemaphoreType.DMA((len(CUTS) + PIECES,)),
        ],
        compiler_params=params(),
        cost_estimate=cost(2 * width * size * tile * SUBLANES, 8 * aux * size),
        name="both_halves",
    )(live, green_occ, green_vir, y, *before)
    return [half.reshape(-1, width) for half in outs[: len(CUTS)]], outs[len(CUTS) :]


def fold_kernel(live_ref, g_ref, y_ref, shifted_ref, own_ref, *rest, started, turn):
    z_ref, out_ref, kron_ref, acc_ref = rest[-4:]
    step = pl.program_id(0)

    @pl.when(step == 0)
    def _():
        scale = live_ref[0].astype(F32)
        kron_ref[...] = (repeated(g_ref[0].T, SPAN // g_ref.shape[1]).astype(F32) * scale).astype(BF)
        acc_ref[...] = rest[0][...] if started else jnp.zeros(acc_ref.shape, F32)

    for j in range(y_ref.shape[1] // SPAN):
        at = slice(j * SPAN, (j + 1) * SPAN)
        z_ref[:, at] = (dot(y_ref[:, at], kron_ref[...]) + shifted_ref[:, at].astype(F32)).astype(BF)
    acc_ref[...] += dot(z_ref[...], own_ref[...])

    @pl.when(step == pl.num_programs(0) - 1)
    def _():
        out_ref[...] = acc_ref[...].T if turn else acc_ref[...]


def fold(live, mats, y, piece, shifted, own, so_far, turn, before=()):
    aux = y.shape[0]
    size = y.shape[1] // PIECES
    span = 4 * SPAN if size % (4 * SPAN) == 0 else SPAN
    steps = size // span
    block = pl.BlockSpec((aux, span), lambda i: (0, i))
    whole = pl.BlockSpec((aux, aux), lambda i: (0, 0))
    added = [] if so_far is None else [so_far]
    return pl.pallas_call(
        lambda *refs: fold_kernel(*refs, started=bool(added), turn=turn),
        grid=(steps,),
        in_specs=[
            pl.BlockSpec(memory_space=pltpu.SMEM),
            pl.BlockSpec(mats.shape, lambda i: (0, 0, 0)),
            pl.BlockSpec((aux, span), lambda i: (0, piece * steps + i)),
            block,
            pl.BlockSpec((span, aux), lambda i: (piece * steps + i, 0)),
            *[whole] * len(added),
            *unused(before),
        ],
        out_specs=[block, whole],
        out_shape=[jax.ShapeDtypeStruct((aux, size), BF), jax.ShapeDtypeStruct((aux, aux), F32)],
        scratch_shapes=[pltpu.VMEM((SPAN, SPAN), BF), pltpu.VMEM((aux, aux), F32)],
        compiler_params=params(),
        cost_estimate=cost(2 * aux * size * (SPAN + aux), 2 * 4 * aux * size),
        name="fold",
    )(live, mats, y, shifted, own, *added, *before)


def both_kernel(live_ref, go_ref, gv_ref, y_ref, *rest, slices):
    rows_ref, yt_ref, half_ref, over_ref, tiles_ref, in_sems, out_sems = rest[-7:]
    outs = rest[-7 - len(CUTS) - PIECES : -7]
    half_outs, over_outs = outs[: len(CUTS)], outs[len(CUTS) :]
    aux, size = y_ref.shape
    step = aux // IN_STEPS
    fetch = []
    for i in range(IN_STEPS):
        at = pl.ds(i * step, step)
        fetch.append(pltpu.make_async_copy(y_ref.at[at], rows_ref.at[at], in_sems.at[i]))
    for copy in fetch:
        copy.start()
    tiles = [pltpu.make_async_copy(g.at[1], tiles_ref.at[i], in_sems.at[IN_STEPS + i]) for i, g in enumerate((go_ref, gv_ref))]
    for copy in tiles:
        copy.start()
    scale = live_ref[0].astype(F32)
    live = scale.astype(BF)
    for copy in tiles:
        copy.wait()
    occ_kron = spread(tiles_ref[0].T, SUBLANES)
    vir_kron = (repeated(tiles_ref[1].T, SPAN // gv_ref.shape[1]).astype(F32) * scale).astype(BF)
    for copy in fetch:
        copy.wait()
    store = []
    for c, out in enumerate(over_outs):
        wide = size // PIECES
        for j in range(wide // SPAN):
            at = c * wide + j * SPAN
            over_ref[c, :, j * SPAN : (j + 1) * SPAN] = dot(rows_ref[:, at : at + SPAN], vir_kron).astype(BF)
        store.append(pltpu.make_async_copy(over_ref.at[c], out, out_sems.at[len(CUTS) + c]))
        store[-1].start()

    def part_of(span):
        parts = [rows_ref[start : start + count, span] for start, count in slices]
        return (jnp.concatenate(parts, axis=0) if len(parts) > 1 else parts[0]) * live

    occ_group(occ_kron, yt_ref, half_ref, part_of, slice(0, yt_ref.shape[2]), size)
    to = 0
    for c, out in enumerate(half_outs):
        store.append(pltpu.make_async_copy(half_ref.at[pl.ds(to, out.shape[0])], out, out_sems.at[c]))
        store[-1].start()
        to += out.shape[0]
    for copy in store:
        copy.wait()


def both(live, green_occ, green_vir, y, slices, before=()):
    aux, size = y.shape
    tile = green_occ.shape[1]
    width = sum(count for _, count in slices)
    some = pl.BlockSpec(memory_space=pl.ANY)
    fixed = pl.BlockSpec(memory_space=pltpu.HBM)
    parts = [tile * n // sum(CUTS) for n in CUTS]
    outs = pl.pallas_call(
        lambda *refs: both_kernel(*refs, slices=slices),
        in_specs=[pl.BlockSpec(memory_space=pltpu.SMEM), fixed, fixed, some, *unused(before)],
        out_specs=[some] * (len(CUTS) + PIECES),
        out_shape=[jax.ShapeDtypeStruct((n, tile, width), BF) for n in parts]
        + [jax.ShapeDtypeStruct((aux, size // PIECES), BF)] * PIECES,
        scratch_shapes=[
            pltpu.VMEM((aux, size), BF),
            pltpu.VMEM((tile, tile, width), BF),
            pltpu.VMEM((tile, tile, width), BF),
            pltpu.VMEM((PIECES, aux, size // PIECES), BF),
            pltpu.VMEM((2, tile, tile), BF),
            pltpu.SemaphoreType.DMA((IN_STEPS + 2,)),
            pltpu.SemaphoreType.DMA((len(CUTS) + PIECES,)),
        ],
        compiler_params=params(),
        cost_estimate=cost(2 * width * size * tile * SUBLANES, 8 * aux * size),
        name="both_halves",
    )(live, green_occ, green_vir, y, *before)
    return [half.reshape(-1, width) for half in outs[: len(CUTS)]], outs[len(CUTS) :]


def vir_kernel(live_ref, g_ref, y_ref, *rest, n_added):
    added = rest[:n_added]
    out_ref, kron_ref = rest[-2:]

    @pl.when(pl.program_id(0) == 0)
    def _():
        scale = live_ref[0].astype(F32)
        kron_ref[...] = (repeated(g_ref[...], SPAN // g_ref.shape[0]).astype(F32) * scale).astype(BF)

    for j in range(y_ref.shape[1] // SPAN):
        at = slice(j * SPAN, (j + 1) * SPAN)
        got = dot(y_ref[:, at], kron_ref[...])
        for ref in added:
            got = got + ref[:, at].astype(F32)
        out_ref[:, at] = got.astype(BF)


def vir(live, mat, y, piece, added=(), before=()):
    aux = y.shape[0]
    size = y.shape[1] // PIECES
    span = 4 * SPAN if size % (4 * SPAN) == 0 else SPAN
    block = pl.BlockSpec((aux, span), lambda i: (0, i))
    return pl.pallas_call(
        lambda *refs: vir_kernel(*refs, n_added=len(added)),
        grid=(size // span,),
        in_specs=[
            pl.BlockSpec(memory_space=pltpu.SMEM),
            pl.BlockSpec(mat.shape, lambda i: (0, 0)),
            pl.BlockSpec((aux, span), lambda i: (0, piece * (size // span) + i)),
            *(block for _ in added),
            *unused(before),
        ],
        out_specs=block,
        out_shape=jax.ShapeDtypeStruct((aux, size), BF),
        scratch_shapes=[pltpu.VMEM((SPAN, SPAN), BF)],
        compiler_params=params(),
        cost_estimate=cost(2 * aux * size * SPAN, 2 * (2 + len(added)) * aux * size),
        name="vir",
    )(live, mat, y, *added, *before)


def product_kernel(x_ref, *rest, pieces, steps, at, started):
    z_refs = rest[:pieces]
    out_ref, acc_ref = rest[-2:]
    step = pl.program_id(0)

    @pl.when(step == 0)
    def _():
        acc_ref[...] = rest[pieces][...].T if started else jnp.zeros(acc_ref.shape, F32)

    for i, z_ref in enumerate(z_refs):

        @pl.when((step + at) // steps == i)
        def _(z_ref=z_ref):
            acc_ref[...] += dot(z_ref[...], x_ref[...])

    @pl.when(step == pl.num_programs(0) - 1)
    def _():
        out_ref[...] = acc_ref[...].T


def product(zs, x, start, so_far=None, before=()):
    aux, size = zs[0].shape
    width = x.shape[1]
    span = size // 2
    zs, at = zs[start // size :], start % size // span
    added = [] if so_far is None else [so_far]
    whole = pl.BlockSpec((width, aux), lambda i: (0, 0))
    piece = lambda k: pl.BlockSpec((aux, span), lambda i: (0, jnp.clip(i + at - 2 * k, 0, 1)))
    return pl.pallas_call(
        lambda *refs: product_kernel(*refs, pieces=len(zs), steps=2, at=at, started=bool(added)),
        grid=(x.shape[0] // span,),
        in_specs=[
            pl.BlockSpec((span, width), lambda i: (i, 0)),
            *(piece(k) for k in range(len(zs))),
            *[whole] * len(added),
            *unused(before),
        ],
        out_specs=whole,
        out_shape=jax.ShapeDtypeStruct((width, aux), F32),
        scratch_shapes=[pltpu.VMEM((aux, width), F32)],
        compiler_params=params(),
        cost_estimate=cost(2 * aux * x.shape[0] * width, 2 * x.shape[0] * (aux + width)),
        name="product",
    )(x, *zs, *added, *before)


def scattered(parts, axis, direct):
    size = lax.axis_size(axis)
    blocks = [part.reshape(size, part.shape[0] // size, part.shape[1]) for part in parts]
    blocks = jnp.concatenate(blocks, axis=1) if len(blocks) > 1 else blocks[0]
    if size & (size - 1):
        return lax.psum_scatter(blocks.astype(BF), axis, scatter_dimension=0).astype(F32)
    me = lax.axis_index(axis)
    reaches = [1 << i for i in range(size.bit_length() - 1)]
    if direct and size <= 4:
        total = lax.dynamic_index_in_dim(blocks, me, 0, keepdims=False)
        for reach in range(1, size):
            given = lax.dynamic_index_in_dim(blocks, me ^ reach, 0, keepdims=False).astype(BF)
            total = total + lax.ppermute(given, axis, [(i, i ^ reach) for i in range(size)]).astype(F32)
        return total
    for reach in reaches:
        bit = (me // reach) % 2
        pairs = blocks.reshape(blocks.shape[0] // 2, 2, *blocks.shape[1:])
        kept = lax.dynamic_index_in_dim(pairs, bit, 1, keepdims=False)
        given = lax.dynamic_index_in_dim(pairs, 1 - bit, 1, keepdims=False).astype(BF)
        got = lax.ppermute(given, axis, [(i, i ^ reach) for i in range(size)])
        blocks = kept + got.astype(F32)
    return blocks[0]


def chunks_of(aux, owners):
    each = aux // owners
    final = aux * 2 // 5 // LANES * LANES
    parts = [(aux - final) // owners, final // owners]
    if final and (aux - final) % LANES == 0 and all(n % (16 * owners) == 0 for n in (aux - final, final)):
        cuts = [0, parts[0], each]
        return [[(j * each + a, b - a) for j in range(owners)] for a, b in zip(cuts, cuts[1:])]
    return [[(0, aux)]]


def body(three_centre, green_occ, green_vir, pair_live):
    rows, cols = lax.axis_size("row"), lax.axis_size("col")
    y = three_centre[0, 0]
    aux, size = y.shape
    live = pair_live[0]
    up_row = [(i, i - 1) for i in range(1, rows)]
    up_col = [(i, i - 1) for i in range(1, cols)]

    send = lambda half: lax.ppermute(half, "row", up_row)
    chunks = chunks_of(aux, cols)
    chunked = len(chunks) > 1
    last = ()
    if chunked:
        last = [raw(live, green_occ[0], y, chunks[0])]
        unfolded = send(last[0])
    halves, over = both(live, green_occ[0], green_vir[0], y, chunks[-1], last)
    shifted = [lax.ppermute(piece, "col", up_col) for piece in over]
    ending = [send(half) for half in halves]
    spans = [(i, min(SPAN, aux - i)) for i in range(0, aux, SPAN)]
    own = occ(live, green_occ[0], 0, y, spans, before=halves[:1])
    zs = []
    diag = None
    for i in range(PIECES):
        z, diag = fold(live, green_vir[0], y, i, shifted[i], own, diag, i == PIECES - 1)
        zs.append(z)
    blocks, order = [], [[diag]] * len(ending)
    if chunked:
        early = raw_product(unfolded, zs, green_occ.shape[2], before=[diag])
        both_done = scattered([diag, early], "col", True)
        chi_d, blocks = both_done[: aux // cols], [both_done[aux // cols :]]
        order = [[early]] * (len(ending) - 1) + [[both_done]]
    else:
        chi_d = scattered([diag], "col", True)
    ended, start = None, 0
    for half, wait in zip(ending, order):
        ended = product(zs, half, start, ended, before=wait)
        start += half.shape[0]
    blocks.append(scattered([ended], "col", True))
    return chi_d[None], jnp.concatenate(blocks)[None]


def solution(mesh):
    return jax.shard_map(
        body,
        mesh=mesh,
        in_specs=(
            P("row", "col", None, None),
            P("row", None, None, None),
            P("col", None, None, None),
            P("row", "col"),
        ),
        out_specs=(P("row", "col", None), P("row", "col", None)),
        check_vma=False,
    )
```

```python
import jax
import jax.numpy as jnp
from jax import lax
from jax.experimental import pallas as pl
from jax.experimental.pallas import tpu as pltpu
from jax.sharding import PartitionSpec as P

BF = jnp.bfloat16
F32 = jnp.float32
VMEM_BYTES = 48 * 1024 * 1024
SPAN = 256
SUBLANES = 8
LANES = 128
PIECES = 2
IN_STEPS = 4
CUTS = (3, 1)


def dot(a, b, dims=((1,), (0,))):
    return lax.dot_general(a, b, (dims, ((), ())), preferred_element_type=F32)


def iota(shape, axis):
    return lax.broadcasted_iota(jnp.int32, shape, axis)


def spread(g, group):
    m, k = g.shape
    pick_row = (iota((m * group, 1), 0) // group == iota((1, m), 1)).astype(BF)
    pick_col = (iota((k, 1), 0) == iota((1, k * group), 1) // group).astype(BF)
    full = dot(dot(pick_row, g).astype(BF), pick_col)
    same = iota((m * group, 1), 0) % group == iota((1, k * group), 1) % group
    return jnp.where(same, full, 0.0).astype(BF)


def repeated(g, count):
    t = g.shape[0]
    n = t * count
    pick = (iota((n, 1), 0) % t == iota((1, t), 1)).astype(BF)
    full = dot(dot(pick, g).astype(BF), pick, ((1,), (1,)))
    same = iota((n, 1), 0) // t == iota((1, n), 1) // t
    return jnp.where(same, full, 0.0).astype(BF)


def params():
    return pltpu.CompilerParams(vmem_limit_bytes=VMEM_BYTES)


def cost(flops, size):
    return pl.CostEstimate(flops=1, bytes_accessed=1, transcendentals=0)


def unused(before):
    return [pl.BlockSpec(memory_space=pl.ANY)] * len(before)


def occ_group(kron, yt_ref, held_ref, part_of, lanes, size):
    m, tile, _ = held_ref.shape
    width = lanes.stop - lanes.start
    per = SPAN // tile
    for j in range(size // SPAN):
        turned = part_of(slice(j * SPAN, (j + 1) * SPAN)).T
        yt_ref[j * per : (j + 1) * per, :, :width] = turned.reshape(per, tile, width)
    pair = 2 * SUBLANES
    for s in range(tile // pair):
        part = yt_ref[:, s * pair : (s + 1) * pair, :width].astype(F32)
        low, high = (
            part[:, i : i + SUBLANES].reshape(tile * SUBLANES, width).astype(BF) for i in (0, SUBLANES)
        )
        low, high = (dot(kron, x).reshape(m, SUBLANES, width) for x in (low, high))
        held_ref[:, s * pair : (s + 1) * pair, lanes] = jnp.concatenate([low, high], axis=1).astype(BF)


def occ_kernel(live_ref, g_ref, y_ref, *rest, groups, which, cuts):
    rows_ref, yt_ref, held_ref, in_sems, out_sems = rest[-5:]
    out_refs = rest[-5 - cuts : -5]
    m = g_ref.shape[2]
    size = y_ref.shape[1]
    fetch = []
    to = 0
    for slices, _ in groups:
        for start, count in slices:
            fetch.append(
                pltpu.make_async_copy(
                    y_ref.at[pl.ds(start, count)], rows_ref.at[pl.ds(to, count)], in_sems.at[len(fetch)]
                )
            )
            to += count
    for copy in fetch:
        copy.start()
    kron = spread(g_ref[which].T, SUBLANES)
    live = live_ref[0].astype(F32).astype(BF)
    store = []
    at, done = 0, 0
    for k, (slices, width) in enumerate(groups):
        for copy in fetch[done : done + len(slices)]:
            copy.wait()
        done += len(slices)
        lanes = slice(at, at + width)
        occ_group(kron, yt_ref.at[k], held_ref, lambda span: rows_ref[lanes, span] * live, lanes, size)
        for c, out_ref in enumerate(out_refs):
            some = pl.ds(c * (m // cuts), m // cuts)
            store.append(
                pltpu.make_async_copy(
                    held_ref.at[some, :, pl.ds(at, width)], out_ref.at[:, :, pl.ds(at, width)], out_sems.at[k, c]
                )
            )
            store[-1].start()
        at += width
    for copy in store:
        copy.wait()


def raw_kernel(live_ref, g_ref, y_ref, out_ref, rows_ref, tile_ref, tail_ref, tile_sem, in_sems, out_sems, *, slices):
    count, size = rows_ref.shape
    tile = tile_ref.shape[0]
    tail, wide = tail_ref.shape
    blocks = size // wide
    fetch_tile = pltpu.make_async_copy(g_ref.at[1], tile_ref, tile_sem)
    fetch_tile.start()
    fetch = []
    to = 0
    for i, (start, n) in enumerate(slices):
        fetch.append(pltpu.make_async_copy(y_ref.at[pl.ds(start, n)], rows_ref.at[pl.ds(to, n)], in_sems.at[i]))
        fetch[-1].start()
        to += n
    fetch_tile.wait()
    live = live_ref[0].astype(F32).astype(BF)
    tail_ref[...] = jnp.zeros((tail, wide), BF)
    for i in range(tile // tail):
        tail_ref[:, i * 128 : i * 128 + tile] = tile_ref[i * tail : (i + 1) * tail] * live
    store = [pltpu.make_async_copy(tail_ref, out_ref.at[pl.ds(count * blocks, tail)], out_sems.at[0])]
    store[0].start()
    to = 0
    for k, (_, n) in enumerate(slices):
        fetch[k].wait()
        for i in range(blocks):
            store.append(
                pltpu.make_async_copy(
                    rows_ref.at[pl.ds(to, n), pl.ds(i * wide, wide)],
                    out_ref.at[pl.ds(i * count + to, n)],
                    out_sems.at[len(store)],
                )
            )
            store[-1].start()
        to += n
    for copy in store:
        copy.wait()


RAW_TAIL = 16


def raw_shape(count, size, tile):
    wide = 128 * (tile // RAW_TAIL)
    return count * (size // wide) + RAW_TAIL, wide


def raw(live, mats, y, slices):
    count = sum(n for _, n in slices)
    size = y.shape[1]
    tile = mats.shape[1]
    shape = raw_shape(count, size, tile)
    some = pl.BlockSpec(memory_space=pltpu.HBM)
    return pl.pallas_call(
        lambda *refs: raw_kernel(*refs, slices=slices),
        in_specs=[pl.BlockSpec(memory_space=pltpu.SMEM), some, some],
        out_specs=some,
        out_shape=jax.ShapeDtypeStruct(shape, BF),
        scratch_shapes=[
            pltpu.VMEM((count, size), BF),
            pltpu.VMEM((tile, tile), BF),
            pltpu.VMEM((RAW_TAIL, shape[1]), BF),
            pltpu.SemaphoreType.DMA(()),
            pltpu.SemaphoreType.DMA((len(slices),)),
            pltpu.SemaphoreType.DMA((len(slices) * (size // shape[1]) + 1,)),
        ],
        compiler_params=params(),
        cost_estimate=cost(count * size, 4 * count * size),
        name="raw",
    )(live, mats, y)


def raw_product_kernel(r_ref, *rest):
    z_refs = rest[:PIECES]
    out_ref, g_ref, yt_ref, held_ref, z_held, rows_ref, tail_ref, sems = rest[-8:]
    tile, _, count = yt_ref.shape
    size = tile * tile
    wide = r_ref.shape[1]
    blocks = size // wide
    part = size // PIECES
    fetch_tail = pltpu.make_async_copy(r_ref.at[pl.ds(blocks * count, RAW_TAIL)], tail_ref, sems.at[PIECES])
    fetch_tail.start()
    fetch_rows = [
        pltpu.make_async_copy(r_ref.at[pl.ds(i * count, count)], rows_ref.at[i], sems.at[PIECES + 1 + i])
        for i in range(blocks)
    ]
    fetch = [pltpu.make_async_copy(z_refs[i], z_held.at[i], sems.at[i]) for i in range(PIECES)]
    for copy in fetch_rows + fetch:
        copy.start()
    fetch_tail.wait()
    for i in range(tile // RAW_TAIL):
        g_ref[i * RAW_TAIL : (i + 1) * RAW_TAIL] = tail_ref[:, i * 128 : i * 128 + tile]
    kron = spread(g_ref[...].T, SUBLANES)

    def part_of(span):
        block, at = divmod(span.start, wide)
        if at == 0:
            fetch_rows[block].wait()
        return rows_ref[block, :, at : at + SPAN]

    occ_group(kron, yt_ref, held_ref, part_of, slice(0, count), size)
    total = None
    for i in range(PIECES):
        fetch[i].wait()
        rows = slice(i * (tile // PIECES), (i + 1) * (tile // PIECES))
        got = dot(z_held[i], held_ref[rows].reshape(part, count))
        total = got if total is None else total + got
    out_ref[...] = total.T


def raw_product(received, zs, tile, before=()):
    size = tile * tile
    count = (received.shape[0] - RAW_TAIL) * received.shape[1] // size
    aux = zs[0].shape[0]
    return pl.pallas_call(
        raw_product_kernel,
        in_specs=[
            *[pl.BlockSpec(memory_space=pl.ANY)] * (1 + len(zs)),
            *unused(before),
        ],
        out_specs=pl.BlockSpec(memory_space=pltpu.VMEM),
        out_shape=jax.ShapeDtypeStruct((count, aux), F32),
        scratch_shapes=[
            pltpu.VMEM((tile, tile), BF),
            pltpu.VMEM((tile, tile, count), BF),
            pltpu.VMEM((tile, tile, count), BF),
            pltpu.VMEM((PIECES, aux, size // PIECES), BF),
            pltpu.VMEM((size // received.shape[1], count, received.shape[1]), BF),
            pltpu.VMEM((RAW_TAIL, received.shape[1]), BF),
            pltpu.SemaphoreType.DMA((PIECES + 1 + size // received.shape[1],)),
        ],
        compiler_params=params(),
        cost_estimate=cost(2 * count * size * (tile * SUBLANES + aux), 2 * size * (aux + count)),
        name="raw_product",
    )(received, *zs, *before)


def grouped(slices):
    groups, held = [], []
    for start, count in slices:
        held.append((start, count))
        width = sum(n for _, n in held)
        if width >= SPAN and width % 128 == 0:
            groups.append((held, width))
            held = []
    if held:
        groups.append((held, sum(n for _, n in held)))
    return groups


def occ(live, mats, which, y, slices, before=(), cuts=1):
    tile, m = mats.shape[1:]
    size = y.shape[1]
    groups = grouped(slices)
    width = sum(n for _, n in groups)
    widest = max(n for _, n in groups)
    outs = pl.pallas_call(
        lambda *refs: occ_kernel(*refs, groups=groups, which=which, cuts=cuts),
        in_specs=[
            pl.BlockSpec(memory_space=pltpu.SMEM),
            pl.BlockSpec(memory_space=pltpu.VMEM),
            pl.BlockSpec(memory_space=pl.ANY),
            *unused(before),
        ],
        out_specs=[pl.BlockSpec(memory_space=pl.ANY)] * cuts,
        out_shape=[jax.ShapeDtypeStruct((m // cuts, tile, width), BF)] * cuts,
        scratch_shapes=[
            pltpu.VMEM((width, size), BF),
            pltpu.VMEM((len(groups), tile, tile, widest), BF),
            pltpu.VMEM((m, tile, width), BF),
            pltpu.SemaphoreType.DMA((len(slices),)),
            pltpu.SemaphoreType.DMA((len(groups), cuts)),
        ],
        compiler_params=params(),
        cost_estimate=cost(2 * width * size * m * SUBLANES, 4 * width * size),
        name="occ",
    )(live, mats, y, *before)
    return outs[0].reshape(-1, width)


def both_kernel(live_ref, go_ref, gv_ref, y_ref, *rest, slices):
    rows_ref, yt_ref, half_ref, over_ref, tiles_ref, in_sems, out_sems = rest[-7:]
    outs = rest[-7 - len(CUTS) - PIECES : -7]
    half_outs, over_outs = outs[: len(CUTS)], outs[len(CUTS) :]
    aux, size = y_ref.shape
    step = aux // IN_STEPS
    fetch = []
    for i in range(IN_STEPS):
        at = pl.ds(i * step, step)
        fetch.append(pltpu.make_async_copy(y_ref.at[at], rows_ref.at[at], in_sems.at[i]))
    for copy in fetch:
        copy.start()
    tiles = [pltpu.make_async_copy(g.at[1], tiles_ref.at[i], in_sems.at[IN_STEPS + i]) for i, g in enumerate((go_ref, gv_ref))]
    for copy in tiles:
        copy.start()
    scale = live_ref[0].astype(F32)
    live = scale.astype(BF)
    for copy in tiles:
        copy.wait()
    occ_kron = spread(tiles_ref[0].T, SUBLANES)
    vir_kron = (repeated(tiles_ref[1].T, SPAN // gv_ref.shape[1]).astype(F32) * scale).astype(BF)
    for copy in fetch:
        copy.wait()
    store = []
    for c, out in enumerate(over_outs):
        wide = size // PIECES
        for j in range(wide // SPAN):
            at = c * wide + j * SPAN
            over_ref[c, :, j * SPAN : (j + 1) * SPAN] = dot(rows_ref[:, at : at + SPAN], vir_kron).astype(BF)
        store.append(pltpu.make_async_copy(over_ref.at[c], out, out_sems.at[len(CUTS) + c]))
        store[-1].start()

    def part_of(span):
        parts = [rows_ref[start : start + count, span] for start, count in slices]
        return (jnp.concatenate(parts, axis=0) if len(parts) > 1 else parts[0]) * live

    occ_group(occ_kron, yt_ref, half_ref, part_of, slice(0, yt_ref.shape[2]), size)
    to = 0
    for c, out in enumerate(half_outs):
        store.append(pltpu.make_async_copy(half_ref.at[pl.ds(to, out.shape[0])], out, out_sems.at[c]))
        store[-1].start()
        to += out.shape[0]
    for copy in store:
        copy.wait()


def both(live, green_occ, green_vir, y, slices, before=()):
    aux, size = y.shape
    tile = green_occ.shape[1]
    width = sum(count for _, count in slices)
    some = pl.BlockSpec(memory_space=pl.ANY)
    fixed = pl.BlockSpec(memory_space=pltpu.HBM)
    parts = [tile * n // sum(CUTS) for n in CUTS]
    outs = pl.pallas_call(
        lambda *refs: both_kernel(*refs, slices=slices),
        in_specs=[pl.BlockSpec(memory_space=pltpu.SMEM), fixed, fixed, some, *unused(before)],
        out_specs=[some] * (len(CUTS) + PIECES),
        out_shape=[jax.ShapeDtypeStruct((n, tile, width), BF) for n in parts]
        + [jax.ShapeDtypeStruct((aux, size // PIECES), BF)] * PIECES,
        scratch_shapes=[
            pltpu.VMEM((aux, size), BF),
            pltpu.VMEM((tile, tile, width), BF),
            pltpu.VMEM((tile, tile, width), BF),
            pltpu.VMEM((PIECES, aux, size // PIECES), BF),
            pltpu.VMEM((2, tile, tile), BF),
            pltpu.SemaphoreType.DMA((IN_STEPS + 2,)),
            pltpu.SemaphoreType.DMA((len(CUTS) + PIECES,)),
        ],
        compiler_params=params(),
        cost_estimate=cost(2 * width * size * tile * SUBLANES, 8 * aux * size),
        name="both_halves",
    )(live, green_occ, green_vir, y, *before)
    return [half.reshape(-1, width) for half in outs[: len(CUTS)]], outs[len(CUTS) :]


def fold_kernel(live_ref, g_ref, y_ref, shifted_ref, own_ref, *rest, started, turn):
    z_ref, out_ref, kron_ref, acc_ref = rest[-4:]
    step = pl.program_id(0)

    @pl.when(step == 0)
    def _():
        scale = live_ref[0].astype(F32)
        kron_ref[...] = (repeated(g_ref[0].T, SPAN // g_ref.shape[1]).astype(F32) * scale).astype(BF)
        acc_ref[...] = rest[0][...] if started else jnp.zeros(acc_ref.shape, F32)

    for j in range(y_ref.shape[1] // SPAN):
        at = slice(j * SPAN, (j + 1) * SPAN)
        z_ref[:, at] = (dot(y_ref[:, at], kron_ref[...]) + shifted_ref[:, at].astype(F32)).astype(BF)
    acc_ref[...] += dot(z_ref[...], own_ref[...])

    @pl.when(step == pl.num_programs(0) - 1)
    def _():
        out_ref[...] = acc_ref[...].T if turn else acc_ref[...]


def fold(live, mats, y, piece, shifted, own, so_far, turn, before=()):
    aux = y.shape[0]
    size = y.shape[1] // PIECES
    span = 4 * SPAN if size % (4 * SPAN) == 0 else SPAN
    steps = size // span
    block = pl.BlockSpec((aux, span), lambda i: (0, i))
    whole = pl.BlockSpec((aux, aux), lambda i: (0, 0))
    added = [] if so_far is None else [so_far]
    return pl.pallas_call(
        lambda *refs: fold_kernel(*refs, started=bool(added), turn=turn),
        grid=(steps,),
        in_specs=[
            pl.BlockSpec(memory_space=pltpu.SMEM),
            pl.BlockSpec(mats.shape, lambda i: (0, 0, 0)),
            pl.BlockSpec((aux, span), lambda i: (0, piece * steps + i)),
            block,
            pl.BlockSpec((span, aux), lambda i: (piece * steps + i, 0)),
            *[whole] * len(added),
            *unused(before),
        ],
        out_specs=[block, whole],
        out_shape=[jax.ShapeDtypeStruct((aux, size), BF), jax.ShapeDtypeStruct((aux, aux), F32)],
        scratch_shapes=[pltpu.VMEM((SPAN, SPAN), BF), pltpu.VMEM((aux, aux), F32)],
        compiler_params=params(),
        cost_estimate=cost(2 * aux * size * (SPAN + aux), 2 * 4 * aux * size),
        name="fold",
    )(live, mats, y, shifted, own, *added, *before)


def both_kernel(live_ref, go_ref, gv_ref, y_ref, *rest, slices):
    rows_ref, yt_ref, half_ref, over_ref, tiles_ref, in_sems, out_sems = rest[-7:]
    outs = rest[-7 - len(CUTS) - PIECES : -7]
    half_outs, over_outs = outs[: len(CUTS)], outs[len(CUTS) :]
    aux, size = y_ref.shape
    step = aux // IN_STEPS
    fetch = []
    for i in range(IN_STEPS):
        at = pl.ds(i * step, step)
        fetch.append(pltpu.make_async_copy(y_ref.at[at], rows_ref.at[at], in_sems.at[i]))
    for copy in fetch:
        copy.start()
    tiles = [pltpu.make_async_copy(g.at[1], tiles_ref.at[i], in_sems.at[IN_STEPS + i]) for i, g in enumerate((go_ref, gv_ref))]
    for copy in tiles:
        copy.start()
    scale = live_ref[0].astype(F32)
    live = scale.astype(BF)
    for copy in tiles:
        copy.wait()
    occ_kron = spread(tiles_ref[0].T, SUBLANES)
    vir_kron = (repeated(tiles_ref[1].T, SPAN // gv_ref.shape[1]).astype(F32) * scale).astype(BF)
    for copy in fetch:
        copy.wait()
    store = []
    for c, out in enumerate(over_outs):
        wide = size // PIECES
        for j in range(wide // SPAN):
            at = c * wide + j * SPAN
            over_ref[c, :, j * SPAN : (j + 1) * SPAN] = dot(rows_ref[:, at : at + SPAN], vir_kron).astype(BF)
        store.append(pltpu.make_async_copy(over_ref.at[c], out, out_sems.at[len(CUTS) + c]))
        store[-1].start()

    def part_of(span):
        parts = [rows_ref[start : start + count, span] for start, count in slices]
        return (jnp.concatenate(parts, axis=0) if len(parts) > 1 else parts[0]) * live

    occ_group(occ_kron, yt_ref, half_ref, part_of, slice(0, yt_ref.shape[2]), size)
    to = 0
    for c, out in enumerate(half_outs):
        store.append(pltpu.make_async_copy(half_ref.at[pl.ds(to, out.shape[0])], out, out_sems.at[c]))
        store[-1].start()
        to += out.shape[0]
    for copy in store:
        copy.wait()


def both(live, green_occ, green_vir, y, slices, before=()):
    aux, size = y.shape
    tile = green_occ.shape[1]
    width = sum(count for _, count in slices)
    some = pl.BlockSpec(memory_space=pl.ANY)
    fixed = pl.BlockSpec(memory_space=pltpu.HBM)
    parts = [tile * n // sum(CUTS) for n in CUTS]
    outs = pl.pallas_call(
        lambda *refs: both_kernel(*refs, slices=slices),
        in_specs=[pl.BlockSpec(memory_space=pltpu.SMEM), fixed, fixed, some, *unused(before)],
        out_specs=[some] * (len(CUTS) + PIECES),
        out_shape=[jax.ShapeDtypeStruct((n, tile, width), BF) for n in parts]
        + [jax.ShapeDtypeStruct((aux, size // PIECES), BF)] * PIECES,
        scratch_shapes=[
            pltpu.VMEM((aux, size), BF),
            pltpu.VMEM((tile, tile, width), BF),
            pltpu.VMEM((tile, tile, width), BF),
            pltpu.VMEM((PIECES, aux, size // PIECES), BF),
            pltpu.VMEM((2, tile, tile), BF),
            pltpu.SemaphoreType.DMA((IN_STEPS + 2,)),
            pltpu.SemaphoreType.DMA((len(CUTS) + PIECES,)),
        ],
        compiler_params=params(),
        cost_estimate=cost(2 * width * size * tile * SUBLANES, 8 * aux * size),
        name="both_halves",
    )(live, green_occ, green_vir, y, *before)
    return [half.reshape(-1, width) for half in outs[: len(CUTS)]], outs[len(CUTS) :]


def vir_kernel(live_ref, g_ref, y_ref, *rest, n_added):
    added = rest[:n_added]
    out_ref, kron_ref = rest[-2:]

    @pl.when(pl.program_id(0) == 0)
    def _():
        scale = live_ref[0].astype(F32)
        kron_ref[...] = (repeated(g_ref[...], SPAN // g_ref.shape[0]).astype(F32) * scale).astype(BF)

    for j in range(y_ref.shape[1] // SPAN):
        at = slice(j * SPAN, (j + 1) * SPAN)
        got = dot(y_ref[:, at], kron_ref[...])
        for ref in added:
            got = got + ref[:, at].astype(F32)
        out_ref[:, at] = got.astype(BF)


def vir(live, mat, y, piece, added=(), before=()):
    aux = y.shape[0]
    size = y.shape[1] // PIECES
    span = 4 * SPAN if size % (4 * SPAN) == 0 else SPAN
    block = pl.BlockSpec((aux, span), lambda i: (0, i))
    return pl.pallas_call(
        lambda *refs: vir_kernel(*refs, n_added=len(added)),
        grid=(size // span,),
        in_specs=[
            pl.BlockSpec(memory_space=pltpu.SMEM),
            pl.BlockSpec(mat.shape, lambda i: (0, 0)),
            pl.BlockSpec((aux, span), lambda i: (0, piece * (size // span) + i)),
            *(block for _ in added),
            *unused(before),
        ],
        out_specs=block,
        out_shape=jax.ShapeDtypeStruct((aux, size), BF),
        scratch_shapes=[pltpu.VMEM((SPAN, SPAN), BF)],
        compiler_params=params(),
        cost_estimate=cost(2 * aux * size * SPAN, 2 * (2 + len(added)) * aux * size),
        name="vir",
    )(live, mat, y, *added, *before)


def product_kernel(x_ref, *rest, pieces, steps, at, started):
    z_refs = rest[:pieces]
    out_ref, acc_ref = rest[-2:]
    step = pl.program_id(0)

    @pl.when(step == 0)
    def _():
        acc_ref[...] = rest[pieces][...].T if started else jnp.zeros(acc_ref.shape, F32)

    for i, z_ref in enumerate(z_refs):

        @pl.when((step + at) // steps == i)
        def _(z_ref=z_ref):
            acc_ref[...] += dot(z_ref[...], x_ref[...])

    @pl.when(step == pl.num_programs(0) - 1)
    def _():
        out_ref[...] = acc_ref[...].T


def product(zs, x, start, so_far=None, before=()):
    aux, size = zs[0].shape
    width = x.shape[1]
    span = size // 2
    zs, at = zs[start // size :], start % size // span
    added = [] if so_far is None else [so_far]
    whole = pl.BlockSpec((width, aux), lambda i: (0, 0))
    piece = lambda k: pl.BlockSpec((aux, span), lambda i: (0, jnp.clip(i + at - 2 * k, 0, 1)))
    return pl.pallas_call(
        lambda *refs: product_kernel(*refs, pieces=len(zs), steps=2, at=at, started=bool(added)),
        grid=(x.shape[0] // span,),
        in_specs=[
            pl.BlockSpec((span, width), lambda i: (i, 0)),
            *(piece(k) for k in range(len(zs))),
            *[whole] * len(added),
            *unused(before),
        ],
        out_specs=whole,
        out_shape=jax.ShapeDtypeStruct((width, aux), F32),
        scratch_shapes=[pltpu.VMEM((aux, width), F32)],
        compiler_params=params(),
        cost_estimate=cost(2 * aux * x.shape[0] * width, 2 * x.shape[0] * (aux + width)),
        name="product",
    )(x, *zs, *added, *before)


def scattered(parts, axis, direct):
    size = lax.axis_size(axis)
    blocks = [part.reshape(size, part.shape[0] // size, part.shape[1]) for part in parts]
    blocks = jnp.concatenate(blocks, axis=1) if len(blocks) > 1 else blocks[0]
    if size & (size - 1):
        return lax.psum_scatter(blocks.astype(BF), axis, scatter_dimension=0).astype(F32)
    me = lax.axis_index(axis)
    reaches = [1 << i for i in range(size.bit_length() - 1)]
    if direct and size <= 4:
        total = lax.dynamic_index_in_dim(blocks, me, 0, keepdims=False)
        for reach in range(1, size):
            given = lax.dynamic_index_in_dim(blocks, me ^ reach, 0, keepdims=False).astype(BF)
            total = total + lax.ppermute(given, axis, [(i, i ^ reach) for i in range(size)]).astype(F32)
        return total
    for reach in reaches:
        bit = (me // reach) % 2
        pairs = blocks.reshape(blocks.shape[0] // 2, 2, *blocks.shape[1:])
        kept = lax.dynamic_index_in_dim(pairs, bit, 1, keepdims=False)
        given = lax.dynamic_index_in_dim(pairs, 1 - bit, 1, keepdims=False).astype(BF)
        got = lax.ppermute(given, axis, [(i, i ^ reach) for i in range(size)])
        blocks = kept + got.astype(F32)
    return blocks[0]


def chunks_of(aux, owners):
    each = aux // owners
    final = aux * 2 // 5 // LANES * LANES
    parts = [(aux - final) // owners, final // owners]
    if final and (aux - final) % LANES == 0 and all(n % (16 * owners) == 0 for n in (aux - final, final)):
        cuts = [0, parts[0], each]
        return [[(j * each + a, b - a) for j in range(owners)] for a, b in zip(cuts, cuts[1:])]
    return [[(0, aux)]]


def body(three_centre, green_occ, green_vir, pair_live):
    rows, cols = lax.axis_size("row"), lax.axis_size("col")
    y = three_centre[0, 0]
    aux, size = y.shape
    live = pair_live[0]
    up_row = [(i, i - 1) for i in range(1, rows)]
    up_col = [(i, i - 1) for i in range(1, cols)]

    send = lambda half: lax.ppermute(half, "row", up_row)
    chunks = chunks_of(aux, cols)
    chunked = len(chunks) > 1
    last = ()
    if chunked:
        halved = [(a + i, n // 2) for a, n in chunks[0] for i in (0, n // 2)] if chunks[0][0][1] % 32 == 0 else chunks[0]
        last = [raw(live, green_occ[0], y, halved)]
        unfolded = send(last[0])
    halves, over = both(live, green_occ[0], green_vir[0], y, chunks[-1], last)
    shifted = [lax.ppermute(piece, "col", up_col) for piece in over]
    ending = [send(half) for half in halves]
    spans = [(i, min(SPAN, aux - i)) for i in range(0, aux, SPAN)]
    own = occ(live, green_occ[0], 0, y, spans, before=halves[:1])
    zs = []
    diag = None
    for i in range(PIECES):
        z, diag = fold(live, green_vir[0], y, i, shifted[i], own, diag, i == PIECES - 1)
        zs.append(z)
    blocks, order = [], [[diag]] * len(ending)
    if chunked:
        early = raw_product(unfolded, zs, green_occ.shape[2], before=[diag])
        both_done = scattered([diag, early], "col", True)
        chi_d, blocks = both_done[: aux // cols], [both_done[aux // cols :]]
        order = [[early]] * (len(ending) - 1) + [[both_done]]
    else:
        chi_d = scattered([diag], "col", True)
    ended, start = None, 0
    for half, wait in zip(ending, order):
        ended = product(zs, half, start, ended, before=wait)
        start += half.shape[0]
    blocks.append(scattered([ended], "col", True))
    return chi_d[None], jnp.concatenate(blocks)[None]


def solution(mesh):
    return jax.shard_map(
        body,
        mesh=mesh,
        in_specs=(
            P("row", "col", None, None),
            P("row", None, None, None),
            P("col", None, None, None),
            P("row", "col"),
        ),
        out_specs=(P("row", "col", None), P("row", "col", None)),
        check_vma=False,
    )
```
